32 devices in a mesh: dp: 8 (over z, x), fsdp: 4 (over y, core).
Axes of the slice: x: 2, y: 2, z: 4, core: 2. Of those that a mesh axis runs over, the one named last changes fastest.
Arguments:
- tokens: bfloat16 [32768, 512], P(('dp', 'fsdp')), may hold values from -6 to 6
- cotangent: bfloat16 [32768, 512], P(('dp', 'fsdp')), may hold values from -6 to 6
- attention_params: bfloat16 [1048576], P(('dp', 'fsdp')), may hold values from -0.25 to 0.25
- feedforward_params: bfloat16 [2097152], P(('dp', 'fsdp')), may hold values from -0.25 to 0.25
- bias_params: bfloat16 [4096], P(('dp', 'fsdp')), may hold values from -3 to 3
- branch_gates: float32 [2], replicated, may hold values from 0.5 to 2
- bucket_counts: int32 [32, 3], P(('dp', 'fsdp')), may hold values from 0 to 8, as said below
- valid_lengths: int32 [32, 8], P(('dp', 'fsdp')), may hold values from 0 to 1024, as said below
Outputs:
- layer_output: bfloat16 [32768, 512], P(('dp', 'fsdp'))
- input_grad: float32 [32768, 512], P(('dp', 'fsdp'))
- attention_grad: float32 [1048576], P(('dp', 'fsdp'))
- feedforward_grad: float32 [2097152], P(('dp', 'fsdp'))
- bias_grad: float32 [4096], P(('dp', 'fsdp'))
- gate_grad: float32 [2], replicated
The draws below stay inside these ranges and needn't reach their ends.
Inputs may be any that keep to these rules, and one draw needn't show every extreme that they name: `bucket_counts`: row r counts slots of 128, 512 and 1024 rows in that order; the slots fill exactly 1024 rows. `valid_lengths`: entry (r, s) lies between half the size of slot s of buffer r (rounded up) and that size, and is 0 for slots beyond the buffer's count.
All inputs are finite; a program needn't handle non-finite values.
Results may differ from the reference program's by a relative error of at most 0.012.
The reference program's roundings to bfloat16 on the way count: a program that leaves them out, or rounds other values in their place, can miss the bound.
Values may be sent and summed in bfloat16 or wider, within the bound.
No kernel may reach another device: no remote copies, remote signals or barrier semaphores. Data moves between devices by JAX's collectives and lax.ppermute only.
A program may use at most 128 MiB of HBM per device.

```python
import math
import jax
import jax.numpy as jnp
from jax import lax

D = 512
H = 8
HD = 64
FF = 2048
TOK_DEV = 1024
SLOTS = 8
SHORT = 128
MID = 512
LONG = 1024
BUFFERS = 32
TOKENS = 32768


def bucket_layout(key):
    compositions = jnp.array([[0, 0, 1], [0, 2, 0], [4, 1, 0], [8, 0, 0]], dtype=jnp.int32)
    first_key, second_key, third_key = jax.random.split(key, 3)
    chosen = jax.random.randint(first_key, (BUFFERS,), 0, 4).astype(jnp.int32)
    shuffled = jax.random.permutation(second_key, BUFFERS)
    chosen = chosen.at[shuffled[0:4]].set(jnp.arange(4, dtype=jnp.int32))
    slot_counts = compositions[chosen]
    slot_ids = jnp.arange(SLOTS, dtype=jnp.int32)[None, :]
    first_end = slot_counts[:, 2:3]
    second_end = first_end + slot_counts[:, 1:2]
    third_end = second_end + slot_counts[:, 0:1]
    slot_sizes = jnp.where(slot_ids < first_end, LONG, jnp.where(slot_ids < second_end, MID, jnp.where(slot_ids < third_end, SHORT, 0))).astype(jnp.int32)
    spread = jax.random.randint(third_key, (BUFFERS, SLOTS), 0, 1 << 20).astype(jnp.int32) % (slot_sizes // 2 + 1)
    lengths = slot_sizes - slot_sizes // 2 + spread
    lengths = lengths.at[shuffled[0], 0].set(LONG)
    return (slot_counts, lengths.astype(jnp.int32))


def draw_bucket_counts(key, part):
    return bucket_layout(key)[0]


def draw_valid_lengths(key, part):
    return bucket_layout(key)[1]


def steps_of(own_key, extent, cuts, smallest, largest):
    def one(dim, blocks):
        heights = jax.random.uniform(jax.random.fold_in(jax.random.fold_in(own_key, 6), dim), (blocks,), jnp.float32, smallest / len(cuts), largest / len(cuts))
        return jnp.repeat(jnp.exp(heights), extent[dim] // blocks).reshape((-1,) + (1,) * (len(extent) - dim - 1))

    level = one(*cuts[0])
    for cut in cuts[1:]:
        level = level * one(*cut)
    return level


def scatter_about(own_key, shape, width, limit, cuts=(), kind=jnp.bfloat16):
    values = width * jax.random.normal(own_key, shape, jnp.float32)
    if cuts:
        values = values * steps_of(own_key, shape, cuts, -0.22, 0.18)
    return jnp.clip(values, -limit, limit).astype(kind)


def setup_inputs(seed: int = 0) -> dict:
    key_of = jax.random.split(jax.random.key(seed), 9)
    return {
        "tokens": scatter_about(key_of[0], (TOKENS, D), 1.0, 6.0, ((0, 32),)),
        "cotangent": scatter_about(key_of[1], (TOKENS, D), 1.0, 6.0, ((0, 32),)),
        "attention_params": scatter_about(key_of[2], (4 * D * D,), D ** -0.5, 0.25, ((0, 32),)),
        "feedforward_params": scatter_about(key_of[3], (2 * D * FF,), D ** -0.5, 0.25, ((0, 32),)),
        "bias_params": scatter_about(key_of[4], (4 * D + FF,), 0.5, 3.0, ((0, 32),)),
        "branch_gates": jnp.clip(jax.random.uniform(key_of[5], (2,), jnp.float32, 0.5, 2.0), 0.5, 2.0),
        "bucket_counts": draw_bucket_counts(jax.random.fold_in(key_of[8], 71), 0),
        "valid_lengths": draw_valid_lengths(jax.random.fold_in(key_of[8], 71), 0),
    }


@jax.custom_vjp
def low(v):
    return lax.optimization_barrier(v.astype(jnp.bfloat16)).astype(jnp.float32)

@jax.custom_vjp
def low_back(v):
    return v

def low_keep(v):
    return (low(v), None)

def low_pass(kept, grad):
    return (grad,)

def back_keep(v):
    return (v, None)

def back_low(kept, grad):
    return (low(grad),)
low.defvjp(low_keep, low_pass)
low_back.defvjp(back_keep, back_low)

def both_round(value):
    return low(low_back(value))

def product(former, latter):
    return jnp.dot(former, latter, precision=lax.Precision.HIGHEST, preferred_element_type=jnp.float32)

def layout(slot_counts, lengths):
    slot_ids = jnp.arange(SLOTS).astype(jnp.int32)
    first_end = slot_counts[2]
    second_end = first_end + slot_counts[1]
    third_end = second_end + slot_counts[0]
    slot_sizes = jnp.where(slot_ids < first_end, LONG, jnp.where(slot_ids < second_end, MID, jnp.where(slot_ids < third_end, SHORT, 0))).astype(jnp.int32)
    slot_ends = jnp.cumsum(slot_sizes).astype(jnp.int32)
    slot_starts = slot_ends - slot_sizes
    finish = jnp.where(slot_sizes > 0, slot_ends, TOK_DEV).astype(jnp.int32)
    position = jnp.arange(TOK_DEV).astype(jnp.int32)
    member = (position[:, None] >= finish[None, :]).astype(jnp.int32)
    slot_of = lax.optimization_barrier(jnp.sum(member, axis=1)).astype(jnp.int32)
    chosen = (slot_of[:, None] == slot_ids[None, :]).astype(jnp.int32)
    offset = position - lax.optimization_barrier(jnp.sum(chosen * slot_starts[None, :], axis=1))
    usable = offset < lax.optimization_barrier(jnp.sum(chosen * lengths[None, :], axis=1))
    return (slot_of, usable)

def attend(pieces):
    queries, key_rows, value_rows, slot_of, usable = pieces
    scaling = 1.0 / math.sqrt(HD)
    raw_scores = jnp.einsum('qhd,khd->hqk', queries, key_rows, precision=lax.Precision.HIGHEST)
    scores = low_back(raw_scores * scaling)
    allowed = (slot_of[:, None] == slot_of[None, :]) & usable[None, :]
    scores = jnp.where(allowed[None], scores, -1e+30)
    probs = jax.nn.softmax(scores, axis=-1)
    return jnp.einsum('hqk,khd->qhd', low(probs), value_rows, precision=lax.Precision.HIGHEST)

def forward(inputs, attention_flat, bias_flat, feedforward_flat, gate_values, slot_of, usable):
    block_size = D * D
    w_query = attention_flat[0:block_size].reshape(D, D)
    w_key = attention_flat[block_size:2 * block_size].reshape(D, D)
    w_value = attention_flat[2 * block_size:3 * block_size].reshape(D, D)
    w_out = attention_flat[3 * block_size:4 * block_size].reshape(D, D)
    b_query = bias_flat[0:D]
    b_value = bias_flat[D:2 * D]
    b_out = bias_flat[2 * D:3 * D]
    b_down = bias_flat[3 * D:4 * D]
    b_up = bias_flat[4 * D:]
    w_up = feedforward_flat[0:D * FF].reshape(D, FF)
    w_down = feedforward_flat[D * FF:].reshape(FF, D)
    queries = both_round(product(inputs, w_query) + b_query)
    key_rows = both_round(product(inputs, w_key))
    value_rows = both_round(product(inputs, w_value) + b_value)
    shape_four = (BUFFERS, TOK_DEV, H, HD)
    attended = lax.map(jax.checkpoint(attend), (queries.reshape(shape_four), key_rows.reshape(shape_four), value_rows.reshape(shape_four), slot_of, usable))
    context = both_round(attended.reshape(TOKENS, D))
    branch = low_back(product(context, w_out) + b_out)
    middle = inputs + gate_values[0] * branch
    hidden = low_back(product(low(middle), w_up) + b_up)
    active = low(jax.nn.gelu(hidden))
    second = low_back(product(active, w_down) + b_down)
    return middle + gate_values[1] * second

def reference(tokens, cotangent, attention_params, feedforward_params, bias_params, branch_gates, bucket_counts, valid_lengths):
    slot_of, usable = jax.vmap(layout)(bucket_counts, valid_lengths)

    def forward_run(inputs, attention_flat, bias_flat, feedforward_flat, gate_values):
        return forward(inputs, attention_flat, bias_flat, feedforward_flat, gate_values, slot_of, usable)
    output, pullback = jax.vjp(forward_run, tokens.astype(jnp.float32), attention_params.astype(jnp.float32), bias_params.astype(jnp.float32), feedforward_params.astype(jnp.float32), branch_gates.astype(jnp.float32))
    gradients = pullback(cotangent.astype(jnp.float32))
    return (output.astype(jnp.bfloat16), gradients[0], gradients[1], gradients[3], gradients[2], gradients[4])
```

```python
from functools import partial

import jax
import jax.numpy as jnp
from jax import lax
from jax.experimental import pallas as pl
from jax.experimental.pallas import tpu as pltpu
from jax.sharding import PartitionSpec as P

D = 512
H = 8
HD = 64
FF = 2048
ROWS = 1024
SLOTS = 8
SHORT = 128
MID = 512
LONG = 1024
AXES = ("dp", "fsdp")
PARTS = 32
BF = jnp.bfloat16
F32 = jnp.float32
VMEM = pl.BlockSpec(memory_space=pltpu.VMEM)
SMEM = pl.BlockSpec(memory_space=pltpu.SMEM)


def nn(a, b):
    return lax.dot_general(a, b, (((1,), (0,)), ((), ())), preferred_element_type=F32)


def nt(a, b):
    return lax.dot_general(a, b, (((1,), (1,)), ((), ())), preferred_element_type=F32)


def tn(a, b):
    return lax.dot_general(a, b, (((0,), (0,)), ((), ())), preferred_element_type=F32)


def call(body, outs, ins, scratch, flops, moved, limit):
    return pl.pallas_call(
        body,
        out_shape=[jax.ShapeDtypeStruct(s, d) for s, d in outs],
        in_specs=ins,
        out_specs=[VMEM] * len(outs),
        scratch_shapes=[pltpu.VMEM(s, d) for s, d in scratch],
        compiler_params=pltpu.CompilerParams(vmem_limit_bytes=limit << 20),
        cost_estimate=pl.CostEstimate(flops=flops, bytes_accessed=moved, transcendentals=0),
    )


def slot_masks(counts, lengths, keys_out, rows_out):
    lane = lax.broadcasted_iota(jnp.int32, (1, 128), 1)
    slot = lane & 63
    longs, mids, shorts = counts[0, 2], counts[0, 1], counts[0, 0]
    in_long = jnp.minimum(slot, longs)
    in_mid = jnp.clip(slot - longs, 0, mids)
    in_short = jnp.clip(slot - longs - mids, 0, shorts)
    start = in_long * LONG + in_mid * MID + in_short * SHORT
    size = jnp.where(
        slot < longs,
        LONG,
        jnp.where(slot < longs + mids, MID, jnp.where(slot < longs + mids + shorts, SHORT, 0)),
    )
    valid = jnp.zeros((1, 128), jnp.int32)
    for s in range(SLOTS):
        valid = jnp.where(slot == s, lengths[0, s], valid)
    row = lax.broadcasted_iota(jnp.int32, (ROWS, 128), 0)
    member = (row >= start) & (row < start + size)
    usable = (row >= start) & (row < start + valid)
    for parity in range(2):
        here = (slot < SLOTS) & ((lane >= 64) if parity == 0 else (lane < 64))
        rows_out[parity] = jnp.where(here & member, 1.0, 0.0).astype(BF)
        keys_out[parity] = jnp.where(here & jnp.logical_not(usable), -1e30, 0.0).astype(BF)


def half_of(parity, shape):
    lane = lax.broadcasted_iota(jnp.int32, shape, len(shape) - 1)
    return (lane < 64) if parity == 0 else (lane >= 64)


def attend_body(
    n, counts, lengths, place, tok, gathered, q_out, k_out, v_out, ctx_out, lse_out, branch_out,
    w_out, bias_out, keys_mask, rows_mask, lse_cols,
):
    rows_each = D * 4 // n
    tiles = rows_each // 16

    def assemble(o, _):
        piece = o ^ place[0]
        square, row = o // (n // 4), (o % (n // 4)) * rows_each
        for i in range(tiles):
            for j in range(4):
                w_out[square, pl.ds(pl.multiple_of(row + 16 * i, 16), 16), 128 * j : 128 * j + 128] = (
                    gathered[piece, 4 * i + j]
                )
        tail = gathered[piece, 4 * tiles].astype(F32)
        bias_out[0:1, pl.ds(pl.multiple_of(o * 128, 128), 128)] = tail[0:1]
        return 0

    lax.fori_loop(0, n, assemble, 0)
    slot_masks(counts, lengths, keys_mask, rows_mask)

    def project(r, _):
        at = pl.ds(pl.multiple_of(r * 256, 256), 256)
        x = tok[at, :]
        q = (nn(x, w_out[0]) + bias_out[0:1, 0:D]).astype(BF)
        q_out[at, :] = (q.astype(F32) * 0.125).astype(BF)
        k_out[at, :] = nn(x, w_out[1]).astype(BF)
        v_out[at, :] = (nn(x, w_out[2]) + bias_out[0:1, D : 2 * D]).astype(BF)
        return 0

    lax.fori_loop(0, 4, project, 0)
    lse_cols[...] = jnp.zeros_like(lse_cols)

    def pair(p, _):
        lanes = pl.ds(pl.multiple_of(p * 128, 128), 128)
        kp = k_out[:, lanes]
        vp = v_out[:, lanes]
        keys, values = [], []
        for parity in range(2):
            mine = half_of(parity, (ROWS, 128))
            keys.append(jnp.where(mine, kp, keys_mask[parity]))
            values.append(jnp.where(mine, vp, jnp.zeros_like(vp)))
        for r in range(4):
            at = slice(r * 256, r * 256 + 256)
            qp = q_out[at, lanes]
            total = None
            lane = lax.broadcasted_iota(jnp.int32, (256, 128), 1)
            logs = lse_cols[at, :]
            for parity in range(2):
                qa = jnp.where(half_of(parity, (256, 128)), qp, rows_mask[parity, at])
                s = nt(qa, keys[parity])
                top = jnp.max(s, axis=1, keepdims=True)
                e = jnp.exp(s - top)
                mass = jnp.sum(e, axis=1, keepdims=True)
                probs = (e * (1.0 / mass)).astype(BF)
                part = nn(probs, values[parity])
                total = part if total is None else total + part
                logs = jnp.where(lane == 2 * p + parity, top + jnp.log(mass), logs)
            ctx_out[at, lanes] = total.astype(BF)
            lse_cols[at, :] = logs
        return 0

    lax.fori_loop(0, 4, pair, 0)
    lse_out[...] = lse_cols[...].T[0:8]

    def out(r, _):
        at = pl.ds(pl.multiple_of(r * 256, 256), 256)
        branch_out[at, :] = nn(ctx_out[at, :], w_out[3]) + bias_out[0:1, 2 * D : 3 * D]
        return 0

    lax.fori_loop(0, 4, out, 0)


def feed_body(
    n, place, gates, tok, branch, cot, ctx, w_out, bias, gathered,
    layer_out, gm_out, gctx_out, keep_out, send_out, wo_out, sums_out, gate_out,
    w1, w2, mlow, gbr, gs_all, active_all, gh_all,
):
    rows_up = D // (n // 2)
    rows_down = FF // (n // 2)
    tiles = rows_down // 16 * 4

    def assemble_up(o, _):
        piece = o ^ place[0]
        for i in range(rows_up // 16):
            for j in range(16):
                w1[pl.ds(pl.multiple_of(o * rows_up + 16 * i, 16), 16), 128 * j : 128 * j + 128] = (
                    gathered[piece, 16 * i + j]
                )
        return 0

    def assemble_down(o, _):
        piece = (o + n // 2) ^ place[0]
        for i in range(rows_down // 16):
            for j in range(4):
                w2[pl.ds(pl.multiple_of(o * rows_down + 16 * i, 16), 16), 128 * j : 128 * j + 128] = (
                    gathered[piece, 4 * i + j]
                )
        return 0

    lax.fori_loop(0, n // 2, assemble_up, 0)
    lax.fori_loop(0, n // 2, assemble_down, 0)
    ga, gf = gates[0], gates[1]
    sums_out[...] = jnp.zeros_like(sums_out)
    c1 = 0.7978845608028654
    c2 = 0.044715

    def rows(r, carry):
        attend_sum, feed_sum = carry
        at = pl.ds(pl.multiple_of(r * 256, 256), 256)
        br = branch[at, :]
        middle = tok[at, :].astype(F32) + ga * br
        low = middle.astype(BF)
        mlow[at, :] = low
        ct = cot[at, :].astype(F32)
        gs = (gf * ct).astype(BF)
        gs_all[at, :] = gs
        second = jnp.zeros((256, D), F32) + bias[0:1, 3 * D : 4 * D]
        gmid = ct
        for j in range(4):
            cols = slice(512 * j, 512 * j + 512)
            v = nn(low, w1[:, cols]) + bias[0:1, 4 * D + 512 * j : 4 * D + 512 * j + 512]
            back = nt(gs, w2[cols, :])
            v2 = v * v
            t = jnp.tanh(c1 * v * (1.0 + c2 * v2))
            half = 0.5 * (1.0 + t)
            active = (v * half).astype(BF)
            slope = half + (0.5 * c1) * v * (1.0 - t * t) * (1.0 + (3.0 * c2) * v2)
            gh = (slope * back).astype(BF)
            active_all[at, cols] = active
            gh_all[at, cols] = gh
            sums_out[0:1, 4 * D + 512 * j : 4 * D + 512 * j + 512] += jnp.sum(
                gh.astype(F32), axis=0, keepdims=True
            )
            second = second + nn(active, w2[cols, :])
            gmid = gmid + nt(gh, w1[:, cols])
        layer_out[at, :] = (middle + gf * second).astype(BF)
        gm_out[at, :] = gmid
        gb = (ga * gmid).astype(BF)
        gbr[at, :] = gb
        gctx_out[at, :] = nt(gb, w_out[3]).astype(BF)
        sums_out[0:1, 2 * D : 3 * D] += jnp.sum(gb.astype(F32), axis=0, keepdims=True)
        sums_out[0:1, 3 * D : 4 * D] += jnp.sum(gs.astype(F32), axis=0, keepdims=True)
        attend_sum = attend_sum + jnp.sum(br * gmid, axis=0, keepdims=True)
        feed_sum = feed_sum + jnp.sum(second * ct, axis=0, keepdims=True)
        return attend_sum, feed_sum

    zero = jnp.zeros((1, D), F32)
    attend_sum, feed_sum = lax.fori_loop(0, 4, rows, (zero, zero))
    gate_out[0:1, :] = attend_sum
    gate_out[1:2, :] = feed_sum
    wo_out[...] = tn(ctx[...], gbr[...])
    odd = place[1] == 1

    def store(even_owner, tile, even, other):
        keep_out[even_owner // 2, tile] = jnp.where(odd, other, even)
        send_out[even_owner // 2, tile] = jnp.where(odd, even, other).astype(send_out.dtype)

    for j in range(4):
        val = tn(mlow[...], gh_all[:, 512 * j : 512 * j + 512])
        for o in range(0, n // 2, 2):
            for i in range(rows_up // 16):
                for jj in range(4):
                    col = slice(128 * jj, 128 * jj + 128)
                    top = o * rows_up + 16 * i
                    store(o, 16 * i + 4 * j + jj, val[top : top + 16, col], val[top + rows_up : top + rows_up + 16, col])
    for j in range(4):
        val = tn(active_all[:, 512 * j : 512 * j + 512], gs_all[...])
        per = 512 // rows_down
        for o in range(0, per, 2):
            for i in range(rows_down // 16):
                for jj in range(4):
                    col = slice(128 * jj, 128 * jj + 128)
                    top = o * rows_down + 16 * i
                    store(
                        n // 2 + j * per + o, 4 * i + jj,
                        val[top : top + 16, col], val[top + rows_down : top + rows_down + 16, col],
                    )


def back_body(
    n, counts, lengths, place, tok, q_in, k_in, v_in, gctx, lse, wo_grad, sums, gate,
    dq_out, dk_out, dv_out, keep_out, send_out, keys_mask, rows_mask, k_t, dq_t, dk_acc, dv_acc, sum_row,
):
    rows_each = D * 4 // n
    tiles = rows_each // 16
    slot_masks(counts, lengths, keys_mask, rows_mask)
    k_t[...] = k_in[...].T

    def pair(p, _):
        lanes = pl.ds(pl.multiple_of(p * 128, 128), 128)
        kp = k_in[:, lanes]
        vp = v_in[:, lanes]
        dk_acc[...] = jnp.zeros_like(dk_acc)
        dv_acc[...] = jnp.zeros_like(dv_acc)
        for parity in range(2):
            mine = half_of(parity, (ROWS, 128))
            ka = jnp.where(mine, kp, keys_mask[parity])
            kt = k_t[pl.ds(pl.multiple_of(p * 128 + 64 * parity, 64), 64), :]
            logs = lse[pl.ds(2 * p + parity, 1), :]
            few = half_of(parity, (256, 128))
            for r in range(4):
                at = slice(r * 256, r * 256 + 256)
                qp = q_in[at, lanes]
                gp = gctx[at, lanes]
                none = jnp.zeros_like(qp)
                st = nt(ka, jnp.where(few, qp, rows_mask[parity, at]))
                pt = jnp.exp(st - logs[:, at])
                gp = jnp.where(few, gp, none)
                dpt = nt(vp, gp)
                delta = jnp.sum(pt * dpt, axis=0, keepdims=True)
                dst = (pt * (dpt - delta)).astype(BF)
                dk_acc[...] += nn(dst, jnp.where(few, qp, none))
                dv_acc[...] += nn(pt.astype(BF), gp)
                dq_t[pl.ds(pl.multiple_of(p * 128 + 64 * parity, 64), 64), at] = nn(kt, dst) * 0.125
        dk_out[:, lanes] = dk_acc[...].astype(BF)
        dv_out[:, lanes] = dv_acc[...].astype(BF)
        return 0

    lax.fori_loop(0, 4, pair, 0)
    dq_out[...] = dq_t[...].T.astype(BF)
    odd = place[1] == 1
    x_t = tok[...].T
    per = n // 4
    for square in range(4):
        if square == 3:
            val = wo_grad[...]
        else:
            val = nn(x_t, (dq_out, dk_out, dv_out)[square][...])
        for o in range(0, per, 2):
            for i in range(tiles):
                for j in range(4):
                    col = slice(128 * j, 128 * j + 128)
                    top = o * rows_each + 16 * i
                    even, other = val[top : top + 16, col], val[top + rows_each : top + rows_each + 16, col]
                    at = (square * per + o) // 2
                    keep_out[at, 4 * i + j] = jnp.where(odd, other, even)
                    send_out[at, 4 * i + j] = jnp.where(odd, even, other).astype(send_out.dtype)
    sum_row[...] = sums[...]
    sum_row[0:1, 0:D] = jnp.sum(dq_out[...].astype(F32), axis=0, keepdims=True)
    sum_row[0:1, D : 2 * D] = jnp.sum(dv_out[...].astype(F32), axis=0, keepdims=True)
    lane = lax.broadcasted_iota(jnp.int32, (1, 128), 1)
    gates = jnp.zeros((1, 128), F32)
    for g in range(2):
        gates = jnp.where(lane == 2 * place[2] + g, jnp.sum(gate[g : g + 1, :]), gates)
    high = gates.astype(BF).astype(F32)
    rest = gates - high
    mid = rest.astype(BF).astype(F32)
    low = rest - mid
    row = lax.broadcasted_iota(jnp.int32, (16, 128), 0)
    base = jnp.where(row == 1, high, jnp.where(row == 2, mid, jnp.where(row == 3, low, 0.0)))
    for o in range(0, n, 2):
        even = jnp.where(row == 0, sum_row[0:1, 128 * o : 128 * o + 128], base)
        other = jnp.where(row == 0, sum_row[0:1, 128 * o + 128 : 128 * o + 256], base)
        keep_out[o // 2, 4 * tiles] = jnp.where(odd, other, even)
        send_out[o // 2, 4 * tiles] = jnp.where(odd, even, other).astype(send_out.dtype)


def input_body(gm, dq, dk, dv, w, out):
    def rows(r, _):
        at = pl.ds(pl.multiple_of(r * 256, 256), 256)
        out[at, :] = gm[at, :] + nt(dq[at, :], w[0]) + nt(dk[at, :], w[1]) + nt(dv[at, :], w[2])
        return 0

    lax.fori_loop(0, 4, rows, 0)


def to_tiles(flat, rows, cols):
    return flat.reshape(rows // 16, 16, cols // 128, 128).transpose(0, 2, 1, 3).reshape(-1, 16, 128)


def from_tiles(tiles, rows, cols):
    return tiles.reshape(rows // 16, cols // 128, 16, 128).transpose(0, 2, 1, 3).reshape(-1)


def swap(x, n, bit):
    return lax.ppermute(x, AXES, [(i, i ^ bit) for i in range(n)])


def scatter(keep, send, me, n):
    got = swap(send, n, 1)
    total = keep + got.astype(F32)
    z, x, y = me // 8, (me // 4) % 2, (me // 2) % 2
    total = total.reshape((4, 2, 2) + keep.shape[1:])
    half = keep.shape[1] // 2

    def pick(v, axis, index):
        return lax.dynamic_index_in_dim(v, index, axis, keepdims=False)

    a, b = total[:, :, :, :half], total[:, :, :, half:]
    a_got = swap(pick(a, 1, 1 - x).astype(BF), n, 4)
    b_got = swap(pick(b, 2, 1 - y).astype(BF), n, 2)
    a = pick(a, 1, x) + a_got.astype(F32)
    b = pick(b, 2, y) + b_got.astype(F32)
    a_got = swap(pick(a, 1, 1 - y).astype(BF), n, 2)
    b_got = swap(pick(b, 1, 1 - x).astype(BF), n, 4)
    a = pick(a, 1, y) + a_got.astype(F32)
    b = pick(b, 1, x) + b_got.astype(F32)
    ab = jnp.concatenate([a, b], axis=1)
    parts = [swap(pick(ab, 0, z ^ s).astype(BF), n, 8 * s) for s in (1, 2, 3)]
    return pick(ab, 0, z) + (parts[0].astype(F32) + parts[1].astype(F32) + parts[2].astype(F32))


def gather(attention, feedforward, biases, n, me):
    rows_each, rows_up, rows_down = 4 * D // n, D // (n // 2), FF // (n // 2)
    tail = jnp.pad(biases[None, None, :], ((0, 0), (0, 15), (0, 0)))
    own = jnp.concatenate([to_tiles(attention, rows_each, D), tail], axis=0)
    ga_all = lax.all_gather(own, AXES, axis=0)
    own = jnp.where(
        me < n // 2, to_tiles(feedforward, rows_up, FF), to_tiles(feedforward, rows_down, D)
    )
    return ga_all, lax.all_gather(own, AXES, axis=0)


def gather_any(attention, feedforward, biases):
    rows_each, rows_up, rows_down = 4 * D // PARTS, D // (PARTS // 2), FF // (PARTS // 2)
    full = lax.all_gather(attention, AXES, axis=0, tiled=True).reshape(PARTS, -1)
    tail = lax.all_gather(biases, AXES, axis=0, tiled=True).reshape(PARTS, 1, 1, 128)
    tail = jnp.pad(tail, ((0, 0), (0, 0), (0, 15), (0, 0)))
    squares = jax.vmap(lambda f: to_tiles(f, rows_each, D))(full)
    full = lax.all_gather(feedforward, AXES, axis=0, tiled=True).reshape(PARTS, -1)
    up = jax.vmap(lambda f: to_tiles(f, rows_up, FF))(full[: PARTS // 2])
    down = jax.vmap(lambda f: to_tiles(f, rows_down, D))(full[PARTS // 2 :])
    return jnp.concatenate([squares, tail], axis=1), jnp.concatenate([up, down])


def local(direct, tokens, cotangent, attention, feedforward, biases, gates, counts, lengths):
    me = lax.axis_index(AXES)
    n = PARTS
    rows_each, rows_up, rows_down = 4 * D // n, D // (n // 2), FF // (n // 2)
    if direct:
        ga_all, gf_all = gather(attention, feedforward, biases, n, me)
        place = jnp.stack([jnp.zeros_like(me), me % 2, me]).astype(jnp.int32)
    else:
        ga_all, gf_all = gather_any(attention, feedforward, biases)
        place = jnp.zeros((3,), jnp.int32)
    row = (ROWS, D)
    tiles = 4 * rows_each // 16
    ftiles = 4 * rows_down // 16
    wire = BF if direct else F32
    q, k, v, ctx, lse, branch, w, bias = call(
        partial(attend_body, n),
        [(row, BF)] * 4 + [((8, ROWS), F32), (row, F32), ((4, D, D), BF), ((1, 8 * D), F32)],
        [SMEM, SMEM, SMEM, VMEM, VMEM],
        [((2, ROWS, 128), BF), ((2, ROWS, 128), BF), ((ROWS, 128), F32)],
        4 << 30, 16 << 20, 56,
    )(counts, lengths, place, tokens, ga_all)
    layer, gm, gctx, ff_keep, ff_send, wo_grad, sums, gate = call(
        partial(feed_body, n),
        [(row, BF), (row, F32), (row, BF), ((n // 2, ftiles, 16, 128), F32), ((n // 2, ftiles, 16, 128), wire),
         ((D, D), F32), ((1, 8 * D), F32), ((2, D), F32)],
        [SMEM, SMEM] + [VMEM] * 7,
        [((D, FF), BF), ((FF, D), BF), (row, BF), (row, BF), (row, BF), ((ROWS, FF), BF), ((ROWS, FF), BF)],
        14 << 30, 30 << 20, 60,
    )(place, gates, tokens, branch, cotangent, ctx, w, bias, gf_all)
    if direct:
        ff_shard = scatter(ff_keep, ff_send, me, n)
    dq, dk, dv, keep, send = call(
        partial(back_body, n),
        [(row, BF)] * 3 + [((n // 2, tiles + 1, 16, 128), F32), ((n // 2, tiles + 1, 16, 128), wire)],
        [SMEM, SMEM, SMEM] + [VMEM] * 9,
        [((2, ROWS, 128), BF), ((2, ROWS, 128), BF), ((D, ROWS), BF), ((D, ROWS), F32), ((ROWS, 128), F32),
         ((ROWS, 128), F32), ((1, 8 * D), F32)],
        20 << 30, 16 << 20, 56,
    )(counts, lengths, place, tokens, q, k, v, gctx, lse, wo_grad, sums, gate)
    (input_grad,) = call(
        input_body, [(row, F32)], [VMEM] * 5, [], 2 << 30, 8 << 20, 32
    )(gm, dq, dk, dv, w)
    if direct:
        att_shard = scatter(keep, send, me, n)
        ff_grad = jnp.where(
            me < n // 2, from_tiles(ff_shard, rows_up, FF), from_tiles(ff_shard, rows_down, D)
        )
        att_grad = from_tiles(att_shard[:tiles], rows_each, D)
        last = att_shard[tiles]
        gate_grad = jnp.sum((last[1] + last[2] + last[3])[: 2 * n].reshape(n, 2), axis=0)
        return layer, input_grad, att_grad, ff_grad, last[0], gate_grad
    both = jnp.stack([ff_keep, ff_send], axis=1).reshape((n,) + ff_keep.shape[1:])
    up = jax.vmap(lambda t: from_tiles(t, rows_up, FF))(both[: n // 2]).reshape(-1)
    down = jax.vmap(lambda t: from_tiles(t, rows_down, D))(both[n // 2 :]).reshape(-1)
    ff_grad = lax.psum_scatter(jnp.concatenate([up, down]), AXES, scatter_dimension=0, tiled=True)
    both = jnp.stack([keep, send], axis=1).reshape((n,) + keep.shape[1:])
    flat = jax.vmap(lambda t: from_tiles(t, rows_each, D))(both[:, :tiles]).reshape(-1)
    att_grad = lax.psum_scatter(flat, AXES, scatter_dimension=0, tiled=True)
    bias_grad = lax.psum_scatter(both[:, tiles, 0].reshape(-1), AXES, scatter_dimension=0, tiled=True)
    last = both[0, tiles]
    gate_grad = lax.psum((last[1] + last[2] + last[3])[:2], AXES)
    return layer, input_grad, att_grad, ff_grad, bias_grad, gate_grad


def solution(mesh):
    direct = dict(mesh.shape) == {"dp": 8, "fsdp": 4}
    both = P(AXES)
    rows = P(AXES, None)
    return jax.shard_map(
        partial(local, direct),
        mesh=mesh,
        in_specs=(rows, rows, both, both, both, P(), rows, rows),
        out_specs=(rows, rows, both, both, both, P()),
        check_vma=False,
    )
```

```python
from functools import partial

import jax
import jax.numpy as jnp
from jax import lax
from jax.experimental import pallas as pl
from jax.experimental.pallas import tpu as pltpu
from jax.sharding import PartitionSpec as P

D = 512
H = 8
HD = 64
FF = 2048
ROWS = 1024
SLOTS = 8
SHORT = 128
MID = 512
LONG = 1024
AXES = ("dp", "fsdp")
PARTS = 32
BF = jnp.bfloat16
F32 = jnp.float32
VMEM = pl.BlockSpec(memory_space=pltpu.VMEM)
SMEM = pl.BlockSpec(memory_space=pltpu.SMEM)


def nn(a, b):
    return lax.dot_general(a, b, (((1,), (0,)), ((), ())), preferred_element_type=F32)


def nt(a, b):
    return lax.dot_general(a, b, (((1,), (1,)), ((), ())), preferred_element_type=F32)


def tn(a, b):
    return lax.dot_general(a, b, (((0,), (0,)), ((), ())), preferred_element_type=F32)


def call(body, outs, ins, scratch, flops, moved, limit):
    return pl.pallas_call(
        body,
        out_shape=[jax.ShapeDtypeStruct(s, d) for s, d in outs],
        in_specs=ins,
        out_specs=[VMEM] * len(outs),
        scratch_shapes=[pltpu.VMEM(s, d) for s, d in scratch],
        compiler_params=pltpu.CompilerParams(vmem_limit_bytes=limit << 20),
        cost_estimate=pl.CostEstimate(flops=flops, bytes_accessed=moved, transcendentals=0),
    )


def slot_masks(counts, lengths, keys_out, rows_out):
    lane = lax.broadcasted_iota(jnp.int32, (1, 128), 1)
    slot = lane & 63
    longs, mids, shorts = counts[0, 2], counts[0, 1], counts[0, 0]
    in_long = jnp.minimum(slot, longs)
    in_mid = jnp.clip(slot - longs, 0, mids)
    in_short = jnp.clip(slot - longs - mids, 0, shorts)
    start = in_long * LONG + in_mid * MID + in_short * SHORT
    size = jnp.where(
        slot < longs,
        LONG,
        jnp.where(slot < longs + mids, MID, jnp.where(slot < longs + mids + shorts, SHORT, 0)),
    )
    valid = jnp.zeros((1, 128), jnp.int32)
    for s in range(SLOTS):
        valid = jnp.where(slot == s, lengths[0, s], valid)
    row = lax.broadcasted_iota(jnp.int32, (ROWS, 128), 0)
    member = (row >= start) & (row < start + size)
    usable = (row >= start) & (row < start + valid)
    for parity in range(2):
        here = (slot < SLOTS) & ((lane >= 64) if parity == 0 else (lane < 64))
        rows_out[parity] = jnp.where(here & member, 1.0, 0.0).astype(BF)
        keys_out[parity] = jnp.where(here & jnp.logical_not(usable), -1e30, 0.0).astype(BF)


def half_of(parity, shape):
    lane = lax.broadcasted_iota(jnp.int32, shape, len(shape) - 1)
    return (lane < 64) if parity == 0 else (lane >= 64)


def attend_body(
    n, counts, lengths, place, tok, *refs
):
    gathered, refs = refs[:8], refs[8:]
    (q_out, k_out, v_out, ctx_out, lse_out, branch_out, w_out, bias_out, keys_mask, rows_mask, lse_cols) = refs
    rows_each = D * 4 // n
    tiles = rows_each // 16

    def assemble(z, _):
        for d in range(8):
            o = (8 * z + d) ^ place[0]
            square, row = o // (n // 4), (o % (n // 4)) * rows_each
            for i in range(tiles):
                for j in range(4):
                    w_out[square, pl.ds(pl.multiple_of(row + 16 * i, 16), 16), 128 * j : 128 * j + 128] = (
                        gathered[d][z, 4 * i + j]
                    )
            tail = gathered[d][z, 4 * tiles].astype(F32)
            bias_out[0:1, pl.ds(pl.multiple_of(o * 128, 128), 128)] = tail[0:1]
        return 0

    lax.fori_loop(0, n // 8, assemble, 0)
    slot_masks(counts, lengths, keys_mask, rows_mask)

    def project(r, _):
        at = pl.ds(pl.multiple_of(r * 256, 256), 256)
        x = tok[at, :]
        q = (nn(x, w_out[0]) + bias_out[0:1, 0:D]).astype(BF)
        q_out[at, :] = (q.astype(F32) * 0.125).astype(BF)
        k_out[at, :] = nn(x, w_out[1]).astype(BF)
        v_out[at, :] = (nn(x, w_out[2]) + bias_out[0:1, D : 2 * D]).astype(BF)
        return 0

    lax.fori_loop(0, 4, project, 0)
    lse_cols[...] = jnp.zeros_like(lse_cols)

    def pair(p, _):
        lanes = pl.ds(pl.multiple_of(p * 128, 128), 128)
        kp = k_out[:, lanes]
        vp = v_out[:, lanes]
        keys, values = [], []
        for parity in range(2):
            mine = half_of(parity, (ROWS, 128))
            keys.append(jnp.where(mine, kp, keys_mask[parity]))
            values.append(jnp.where(mine, vp, jnp.zeros_like(vp)))
        for r in range(4):
            at = slice(r * 256, r * 256 + 256)
            qp = q_out[at, lanes]
            total = None
            lane = lax.broadcasted_iota(jnp.int32, (256, 128), 1)
            logs = lse_cols[at, :]
            for parity in range(2):
                qa = jnp.where(half_of(parity, (256, 128)), qp, rows_mask[parity, at])
                s = nt(qa, keys[parity])
                top = jnp.max(s, axis=1, keepdims=True)
                e = jnp.exp(s - top)
                mass = jnp.sum(e, axis=1, keepdims=True)
                probs = (e * (1.0 / mass)).astype(BF)
                part = nn(probs, values[parity])
                total = part if total is None else total + part
                logs = jnp.where(lane == 2 * p + parity, top + jnp.log(mass), logs)
            ctx_out[at, lanes] = total.astype(BF)
            lse_cols[at, :] = logs
        return 0

    lax.fori_loop(0, 4, pair, 0)
    lse_out[...] = lse_cols[...].T[0:8]

    def out(r, _):
        at = pl.ds(pl.multiple_of(r * 256, 256), 256)
        branch_out[at, :] = nn(ctx_out[at, :], w_out[3]) + bias_out[0:1, 2 * D : 3 * D]
        return 0

    lax.fori_loop(0, 4, out, 0)


def feed_body(
    n, place, gates, tok, branch, cot, ctx, w_out, bias, *refs
):
    gathered, refs = refs[:8], refs[8:]
    (layer_out, gm_out, gctx_out, keep_out, send_out, wo_out, sums_out, gate_out) = refs[:8]
    (w1, w2, mlow, gbr, gs_all, active_all, gh_all) = refs[8:]
    rows_up = D // (n // 2)
    rows_down = FF // (n // 2)
    tiles = rows_down // 16 * 4

    def assemble(z, _):
        for d in range(8):
            o = (8 * z + d) ^ place[0]

            @pl.when(o < n // 2)
            def _():
                for i in range(rows_up // 16):
                    for j in range(16):
                        row = pl.ds(pl.multiple_of(o * rows_up + 16 * i, 16), 16)
                        w1[row, 128 * j : 128 * j + 128] = gathered[d][z, 16 * i + j]

            @pl.when(o >= n // 2)
            def _():
                for i in range(rows_down // 16):
                    for j in range(4):
                        row = pl.ds(pl.multiple_of((o - n // 2) * rows_down + 16 * i, 16), 16)
                        w2[row, 128 * j : 128 * j + 128] = gathered[d][z, 4 * i + j]

        return 0

    lax.fori_loop(0, n // 8, assemble, 0)
    ga, gf = gates[0], gates[1]
    sums_out[...] = jnp.zeros_like(sums_out)
    c1 = 0.7978845608028654
    c2 = 0.044715

    def rows(r, carry):
        attend_sum, feed_sum = carry
        at = pl.ds(pl.multiple_of(r * 256, 256), 256)
        br = branch[at, :]
        middle = tok[at, :].astype(F32) + ga * br
        low = middle.astype(BF)
        mlow[at, :] = low
        ct = cot[at, :].astype(F32)
        gs = (gf * ct).astype(BF)
        gs_all[at, :] = gs
        second = jnp.zeros((256, D), F32) + bias[0:1, 3 * D : 4 * D]
        gmid = ct
        for j in range(4):
            cols = slice(512 * j, 512 * j + 512)
            v = nn(low, w1[:, cols]) + bias[0:1, 4 * D + 512 * j : 4 * D + 512 * j + 512]
            back = nt(gs, w2[cols, :])
            v2 = v * v
            t = jnp.tanh(c1 * v * (1.0 + c2 * v2))
            half = 0.5 * (1.0 + t)
            active = (v * half).astype(BF)
            slope = half + (0.5 * c1) * v * (1.0 - t * t) * (1.0 + (3.0 * c2) * v2)
            gh = (slope * back).astype(BF)
            active_all[at, cols] = active
            gh_all[at, cols] = gh
            sums_out[0:1, 4 * D + 512 * j : 4 * D + 512 * j + 512] += jnp.sum(
                gh.astype(F32), axis=0, keepdims=True
            )
            second = second + nn(active, w2[cols, :])
            gmid = gmid + nt(gh, w1[:, cols])
        layer_out[at, :] = (middle + gf * second).astype(BF)
        gm_out[at, :] = gmid
        gb = (ga * gmid).astype(BF)
        gbr[at, :] = gb
        gctx_out[at, :] = nt(gb, w_out[3]).astype(BF)
        sums_out[0:1, 2 * D : 3 * D] += jnp.sum(gb.astype(F32), axis=0, keepdims=True)
        sums_out[0:1, 3 * D : 4 * D] += jnp.sum(gs.astype(F32), axis=0, keepdims=True)
        attend_sum = attend_sum + jnp.sum(br * gmid, axis=0, keepdims=True)
        feed_sum = feed_sum + jnp.sum(second * ct, axis=0, keepdims=True)
        return attend_sum, feed_sum

    zero = jnp.zeros((1, D), F32)
    attend_sum, feed_sum = lax.fori_loop(0, 4, rows, (zero, zero))
    gate_out[0:1, :] = attend_sum
    gate_out[1:2, :] = feed_sum
    wo_out[...] = tn(ctx[...], gbr[...])
    odd = place[1] == 1

    def store(even_owner, tile, even, other):
        keep_out[even_owner // 2, tile] = jnp.where(odd, other, even)
        send_out[even_owner // 2, tile] = jnp.where(odd, even, other).astype(send_out.dtype)

    for j in range(4):
        val = tn(mlow[...], gh_all[:, 512 * j : 512 * j + 512])
        for o in range(0, n // 2, 2):
            for i in range(rows_up // 16):
                for jj in range(4):
                    col = slice(128 * jj, 128 * jj + 128)
                    top = o * rows_up + 16 * i
                    store(o, 16 * i + 4 * j + jj, val[top : top + 16, col], val[top + rows_up : top + rows_up + 16, col])
    for j in range(4):
        val = tn(active_all[:, 512 * j : 512 * j + 512], gs_all[...])
        per = 512 // rows_down
        for o in range(0, per, 2):
            for i in range(rows_down // 16):
                for jj in range(4):
                    col = slice(128 * jj, 128 * jj + 128)
                    top = o * rows_down + 16 * i
                    store(
                        n // 2 + j * per + o, 4 * i + jj,
                        val[top : top + 16, col], val[top + rows_down : top + rows_down + 16, col],
                    )


def back_body(
    n, counts, lengths, place, tok, q_in, k_in, v_in, gctx, lse, wo_grad, sums, gate,
    dq_out, dk_out, dv_out, keep_out, send_out, keys_mask, rows_mask, k_t, dq_t, dk_acc, dv_acc, sum_row,
):
    rows_each = D * 4 // n
    tiles = rows_each // 16
    slot_masks(counts, lengths, keys_mask, rows_mask)
    k_t[...] = k_in[...].T

    def pair(p, _):
        lanes = pl.ds(pl.multiple_of(p * 128, 128), 128)
        kp = k_in[:, lanes]
        vp = v_in[:, lanes]
        dk_acc[...] = jnp.zeros_like(dk_acc)
        dv_acc[...] = jnp.zeros_like(dv_acc)
        for parity in range(2):
            mine = half_of(parity, (ROWS, 128))
            ka = jnp.where(mine, kp, keys_mask[parity])
            kt = k_t[pl.ds(pl.multiple_of(p * 128 + 64 * parity, 64), 64), :]
            logs = lse[pl.ds(2 * p + parity, 1), :]
            few = half_of(parity, (256, 128))
            for r in range(4):
                at = slice(r * 256, r * 256 + 256)
                qp = q_in[at, lanes]
                gp = gctx[at, lanes]
                none = jnp.zeros_like(qp)
                st = nt(ka, jnp.where(few, qp, rows_mask[parity, at]))
                pt = jnp.exp(st - logs[:, at])
                gp = jnp.where(few, gp, none)
                dpt = nt(vp, gp)
                delta = jnp.sum(pt * dpt, axis=0, keepdims=True)
                dst = (pt * (dpt - delta)).astype(BF)
                dk_acc[...] += nn(dst, jnp.where(few, qp, none))
                dv_acc[...] += nn(pt.astype(BF), gp)
                dq_t[pl.ds(pl.multiple_of(p * 128 + 64 * parity, 64), 64), at] = nn(kt, dst) * 0.125
        dk_out[:, lanes] = dk_acc[...].astype(BF)
        dv_out[:, lanes] = dv_acc[...].astype(BF)
        return 0

    lax.fori_loop(0, 4, pair, 0)
    dq_out[...] = dq_t[...].T.astype(BF)
    odd = place[1] == 1
    x_t = tok[...].T
    per = n // 4
    for square in range(4):
        if square == 3:
            val = wo_grad[...]
        else:
            val = nn(x_t, (dq_out, dk_out, dv_out)[square][...])
        for o in range(0, per, 2):
            for i in range(tiles):
                for j in range(4):
                    col = slice(128 * j, 128 * j + 128)
                    top = o * rows_each + 16 * i
                    even, other = val[top : top + 16, col], val[top + rows_each : top + rows_each + 16, col]
                    at = (square * per + o) // 2
                    keep_out[at, 4 * i + j] = jnp.where(odd, other, even)
                    send_out[at, 4 * i + j] = jnp.where(odd, even, other).astype(send_out.dtype)
    sum_row[...] = sums[...]
    sum_row[0:1, 0:D] = jnp.sum(dq_out[...].astype(F32), axis=0, keepdims=True)
    sum_row[0:1, D : 2 * D] = jnp.sum(dv_out[...].astype(F32), axis=0, keepdims=True)
    lane = lax.broadcasted_iota(jnp.int32, (1, 128), 1)
    gates = jnp.zeros((1, 128), F32)
    for g in range(2):
        gates = jnp.where(lane == 2 * place[2] + g, jnp.sum(gate[g : g + 1, :]), gates)
    high = gates.astype(BF).astype(F32)
    rest = gates - high
    mid = rest.astype(BF).astype(F32)
    low = rest - mid
    row = lax.broadcasted_iota(jnp.int32, (16, 128), 0)
    base = jnp.where(row == 1, high, jnp.where(row == 2, mid, jnp.where(row == 3, low, 0.0)))
    for o in range(0, n, 2):
        even = jnp.where(row == 0, sum_row[0:1, 128 * o : 128 * o + 128], base)
        other = jnp.where(row == 0, sum_row[0:1, 128 * o + 128 : 128 * o + 256], base)
        keep_out[o // 2, 4 * tiles] = jnp.where(odd, other, even)
        send_out[o // 2, 4 * tiles] = jnp.where(odd, even, other).astype(send_out.dtype)


def input_body(gm, dq, dk, dv, w, out):
    def rows(r, _):
        at = pl.ds(pl.multiple_of(r * 256, 256), 256)
        out[at, :] = gm[at, :] + nt(dq[at, :], w[0]) + nt(dk[at, :], w[1]) + nt(dv[at, :], w[2])
        return 0

    lax.fori_loop(0, 4, rows, 0)


def to_tiles(flat, rows, cols):
    return flat.reshape(rows // 16, 16, cols // 128, 128).transpose(0, 2, 1, 3).reshape(-1, 16, 128)


def from_tiles(tiles, rows, cols):
    return tiles.reshape(rows // 16, cols // 128, 16, 128).transpose(0, 2, 1, 3).reshape(-1)


def swap(x, n, bit):
    return lax.ppermute(x, AXES, [(i, i ^ bit) for i in range(n)])


def scatter(keep, send, me, n):
    got = swap(send, n, 1)
    total = keep + got.astype(F32)
    z, x, y = me // 8, (me // 4) % 2, (me // 2) % 2
    total = total.reshape((4, 2, 2) + keep.shape[1:])
    half = keep.shape[1] // 2

    def pick(v, axis, index):
        return lax.dynamic_index_in_dim(v, index, axis, keepdims=False)

    a, b = total[:, :, :, :half], total[:, :, :, half:]
    a_got = swap(pick(a, 1, 1 - x).astype(BF), n, 4)
    b_got = swap(pick(b, 2, 1 - y).astype(BF), n, 2)
    a = pick(a, 1, x) + a_got.astype(F32)
    b = pick(b, 2, y) + b_got.astype(F32)
    a_got = swap(pick(a, 1, 1 - y).astype(BF), n, 2)
    b_got = swap(pick(b, 1, 1 - x).astype(BF), n, 4)
    a = pick(a, 1, y) + a_got.astype(F32)
    b = pick(b, 1, x) + b_got.astype(F32)
    ab = jnp.concatenate([a, b], axis=1)
    parts = [swap(pick(ab, 0, z ^ s).astype(BF), n, 8 * s) for s in (1, 2, 3)]
    return pick(ab, 0, z) + (parts[0].astype(F32) + parts[1].astype(F32) + parts[2].astype(F32))


def spread(own, n):
    stack = jnp.stack([own] + [swap(own, n, 8 * z) for z in (1, 2, 3)])
    chips = [stack] + [swap(stack, n, bits) for bits in (2, 4, 6)]
    return [part for chip in chips for part in (chip, swap(chip, n, 1))]


def gather(attention, feedforward, biases, n, me):
    rows_each, rows_up, rows_down = 4 * D // n, D // (n // 2), FF // (n // 2)
    tail = jnp.pad(biases[None, None, :], ((0, 0), (0, 15), (0, 0)))
    own_a = jnp.concatenate([to_tiles(attention, rows_each, D), tail], axis=0)
    own_f = jnp.where(
        me < n // 2, to_tiles(feedforward, rows_up, FF), to_tiles(feedforward, rows_down, D)
    )
    return spread(own_a, n), spread(own_f, n)


def gather_any(attention, feedforward, biases):
    rows_each, rows_up, rows_down = 4 * D // PARTS, D // (PARTS // 2), FF // (PARTS // 2)
    full = lax.all_gather(attention, AXES, axis=0, tiled=True).reshape(PARTS, -1)
    tail = lax.all_gather(biases, AXES, axis=0, tiled=True).reshape(PARTS, 1, 1, 128)
    tail = jnp.pad(tail, ((0, 0), (0, 0), (0, 15), (0, 0)))
    squares = jax.vmap(lambda f: to_tiles(f, rows_each, D))(full)
    full = lax.all_gather(feedforward, AXES, axis=0, tiled=True).reshape(PARTS, -1)
    up = jax.vmap(lambda f: to_tiles(f, rows_up, FF))(full[: PARTS // 2])
    down = jax.vmap(lambda f: to_tiles(f, rows_down, D))(full[PARTS // 2 :])
    pieces = jnp.concatenate([squares, tail], axis=1), jnp.concatenate([up, down])
    return [[p.reshape((4, 8) + p.shape[1:])[:, d] for d in range(8)] for p in pieces]


def local(direct, tokens, cotangent, attention, feedforward, biases, gates, counts, lengths):
    me = lax.axis_index(AXES)
    n = PARTS
    rows_each, rows_up, rows_down = 4 * D // n, D // (n // 2), FF // (n // 2)
    if direct:
        ga_all, gf_all = gather(attention, feedforward, biases, n, me)
        place = jnp.stack([me, me % 2, me]).astype(jnp.int32)
    else:
        ga_all, gf_all = gather_any(attention, feedforward, biases)
        place = jnp.zeros((3,), jnp.int32)
    row = (ROWS, D)
    tiles = 4 * rows_each // 16
    ftiles = 4 * rows_down // 16
    wire = BF if direct else F32
    q, k, v, ctx, lse, branch, w, bias = call(
        partial(attend_body, n),
        [(row, BF)] * 4 + [((8, ROWS), F32), (row, F32), ((4, D, D), BF), ((1, 8 * D), F32)],
        [SMEM, SMEM, SMEM] + [VMEM] * 9,
        [((2, ROWS, 128), BF), ((2, ROWS, 128), BF), ((ROWS, 128), F32)],
        4 << 30, 16 << 20, 56,
    )(counts, lengths, place, tokens, *ga_all)
    layer, gm, gctx, ff_keep, ff_send, wo_grad, sums, gate = call(
        partial(feed_body, n),
        [(row, BF), (row, F32), (row, BF), ((n // 2, ftiles, 16, 128), F32), ((n // 2, ftiles, 16, 128), wire),
         ((D, D), F32), ((1, 8 * D), F32), ((2, D), F32)],
        [SMEM, SMEM] + [VMEM] * 14,
        [((D, FF), BF), ((FF, D), BF), (row, BF), (row, BF), (row, BF), ((ROWS, FF), BF), ((ROWS, FF), BF)],
        14 << 30, 30 << 20, 60,
    )(place, gates, tokens, branch, cotangent, ctx, w, bias, *gf_all)
    if direct:
        ff_shard = scatter(ff_keep, ff_send, me, n)
    dq, dk, dv, keep, send = call(
        partial(back_body, n),
        [(row, BF)] * 3 + [((n // 2, tiles + 1, 16, 128), F32), ((n // 2, tiles + 1, 16, 128), wire)],
        [SMEM, SMEM, SMEM] + [VMEM] * 9,
        [((2, ROWS, 128), BF), ((2, ROWS, 128), BF), ((D, ROWS), BF), ((D, ROWS), F32), ((ROWS, 128), F32),
         ((ROWS, 128), F32), ((1, 8 * D), F32)],
        20 << 30, 16 << 20, 56,
    )(counts, lengths, place, tokens, q, k, v, gctx, lse, wo_grad, sums, gate)
    (input_grad,) = call(
        input_body, [(row, F32)], [VMEM] * 5, [], 2 << 30, 8 << 20, 32
    )(gm, dq, dk, dv, w)
    if direct:
        att_shard = scatter(keep, send, me, n)
        ff_grad = jnp.where(
            me < n // 2, from_tiles(ff_shard, rows_up, FF), from_tiles(ff_shard, rows_down, D)
        )
        att_grad = from_tiles(att_shard[:tiles], rows_each, D)
        last = att_shard[tiles]
        gate_grad = jnp.sum((last[1] + last[2] + last[3])[: 2 * n].reshape(n, 2), axis=0)
        return layer, input_grad, att_grad, ff_grad, last[0], gate_grad
    both = jnp.stack([ff_keep, ff_send], axis=1).reshape((n,) + ff_keep.shape[1:])
    up = jax.vmap(lambda t: from_tiles(t, rows_up, FF))(both[: n // 2]).reshape(-1)
    down = jax.vmap(lambda t: from_tiles(t, rows_down, D))(both[n // 2 :]).reshape(-1)
    ff_grad = lax.psum_scatter(jnp.concatenate([up, down]), AXES, scatter_dimension=0, tiled=True)
    both = jnp.stack([keep, send], axis=1).reshape((n,) + keep.shape[1:])
    flat = jax.vmap(lambda t: from_tiles(t, rows_each, D))(both[:, :tiles]).reshape(-1)
    att_grad = lax.psum_scatter(flat, AXES, scatter_dimension=0, tiled=True)
    bias_grad = lax.psum_scatter(both[:, tiles, 0].reshape(-1), AXES, scatter_dimension=0, tiled=True)
    last = both[0, tiles]
    gate_grad = lax.psum((last[1] + last[2] + last[3])[:2], AXES)
    return layer, input_grad, att_grad, ff_grad, bias_grad, gate_grad


def solution(mesh):
    direct = dict(mesh.shape) == {"dp": 8, "fsdp": 4}
    both = P(AXES)
    rows = P(AXES, None)
    return jax.shard_map(
        partial(local, direct),
        mesh=mesh,
        in_specs=(rows, rows, both, both, both, P(), rows, rows),
        out_specs=(rows, rows, both, both, both, P()),
        check_vma=False,
    )
```

```python
from functools import partial

import jax
import jax.numpy as jnp
from jax import lax
from jax.experimental import pallas as pl
from jax.experimental.pallas import tpu as pltpu
from jax.sharding import PartitionSpec as P

D = 512
H = 8
HD = 64
FF = 2048
ROWS = 1024
SLOTS = 8
SHORT = 128
MID = 512
LONG = 1024
AXES = ("dp", "fsdp")
PARTS = 32
BF = jnp.bfloat16
F32 = jnp.float32
VMEM = pl.BlockSpec(memory_space=pltpu.VMEM)
SMEM = pl.BlockSpec(memory_space=pltpu.SMEM)


def nn(a, b):
    return lax.dot_general(a, b, (((1,), (0,)), ((), ())), preferred_element_type=F32)


def nt(a, b):
    return lax.dot_general(a, b, (((1,), (1,)), ((), ())), preferred_element_type=F32)


def tn(a, b):
    return lax.dot_general(a, b, (((0,), (0,)), ((), ())), preferred_element_type=F32)


def call(body, outs, ins, scratch, flops, moved, limit, grid=None):
    shapes = [jax.ShapeDtypeStruct(o[0], o[1]) for o in outs]
    return pl.pallas_call(
        body,
        out_shape=shapes,
        grid=grid or (),
        in_specs=ins,
        out_specs=[o[2] if len(o) > 2 else VMEM for o in outs],
        scratch_shapes=[pltpu.VMEM(s, d) for s, d in scratch],
        compiler_params=pltpu.CompilerParams(vmem_limit_bytes=limit << 20),
        cost_estimate=pl.CostEstimate(flops=flops, bytes_accessed=moved, transcendentals=0),
    )


def slot_masks(counts, lengths, keys_out, rows_out):
    lane = lax.broadcasted_iota(jnp.int32, (1, 128), 1)
    slot = lane & 63
    longs, mids, shorts = counts[0, 2], counts[0, 1], counts[0, 0]
    in_long = jnp.minimum(slot, longs)
    in_mid = jnp.clip(slot - longs, 0, mids)
    in_short = jnp.clip(slot - longs - mids, 0, shorts)
    start = in_long * LONG + in_mid * MID + in_short * SHORT
    size = jnp.where(
        slot < longs,
        LONG,
        jnp.where(slot < longs + mids, MID, jnp.where(slot < longs + mids + shorts, SHORT, 0)),
    )
    valid = jnp.zeros((1, 128), jnp.int32)
    for s in range(SLOTS):
        valid = jnp.where(slot == s, lengths[0, s], valid)
    row = lax.broadcasted_iota(jnp.int32, (ROWS, 128), 0)
    member = (row >= start) & (row < start + size)
    usable = (row >= start) & (row < start + valid)
    for parity in range(2):
        here = (slot < SLOTS) & ((lane >= 64) if parity == 0 else (lane < 64))
        rows_out[parity] = jnp.where(here & member, 1.0, 0.0).astype(BF)
        keys_out[parity] = jnp.where(here & jnp.logical_not(usable), -1e30, 0.0).astype(BF)


def half_of(parity, shape):
    lane = lax.broadcasted_iota(jnp.int32, shape, len(shape) - 1)
    return (lane < 64) if parity == 0 else (lane >= 64)


def project_body(n, place, tok, *refs):
    gathered, (q_out, k_out, v_out, x_t, w_out, bias_out) = refs[:8], refs[8:]
    rows_each = D * 4 // n
    tiles = rows_each // 16

    def assemble(z, _):
        for d in range(8):
            o = (8 * z + d) ^ place[0]
            square, row = o // (n // 4), (o % (n // 4)) * rows_each
            for i in range(tiles):
                for j in range(4):
                    w_out[square, pl.ds(pl.multiple_of(row + 16 * i, 16), 16), 128 * j : 128 * j + 128] = (
                        gathered[d][z, 4 * i + j]
                    )
            tail = gathered[d][z, 4 * tiles].astype(F32)
            bias_out[0:1, pl.ds(pl.multiple_of(o * 128, 128), 128)] = tail[0:1]
        return 0

    lax.fori_loop(0, n // 8, assemble, 0)

    def project(r, _):
        at = pl.ds(pl.multiple_of(r * 256, 256), 256)
        x = tok[at, :]
        q = (nn(x, w_out[0]) + bias_out[0:1, 0:D]).astype(BF)
        q_out[at, :] = (q.astype(F32) * 0.125).astype(BF)
        k_out[at, :] = nn(x, w_out[1]).astype(BF)
        v_out[at, :] = (nn(x, w_out[2]) + bias_out[0:1, D : 2 * D]).astype(BF)
        return 0

    lax.fori_loop(0, 4, project, 0)
    x_t[...] = tok[...].T


def attend_body(counts, lengths, q_in, k_in, v_in, ctx_out, lse_out, keys_mask, rows_mask, lse_cols):
    p = pl.program_id(0)

    @pl.when(p == 0)
    def _():
        slot_masks(counts, lengths, keys_mask, rows_mask)
        lse_cols[...] = jnp.zeros_like(lse_cols)

    keys, values = [], []
    for parity in range(2):
        mine = half_of(parity, (ROWS, 128))
        keys.append(jnp.where(mine, k_in[...], keys_mask[parity]))
        values.append(jnp.where(mine, v_in[...], jnp.zeros((ROWS, 128), BF)))
    for r in range(4):
        at = slice(r * 256, r * 256 + 256)
        total = None
        lane = lax.broadcasted_iota(jnp.int32, (256, 128), 1)
        logs = lse_cols[at, :]
        for parity in range(2):
            qa = jnp.where(half_of(parity, (256, 128)), q_in[at, :], rows_mask[parity, at])
            s = nt(qa, keys[parity])
            top = jnp.max(s, axis=1, keepdims=True)
            e = jnp.exp(s - top)
            mass = jnp.sum(e, axis=1, keepdims=True)
            probs = (e * (1.0 / mass)).astype(BF)
            part = nn(probs, values[parity])
            total = part if total is None else total + part
            logs = jnp.where(lane == 2 * p + parity, top + jnp.log(mass), logs)
        ctx_out[at, :] = total.astype(BF)
        lse_cols[at, :] = logs

    @pl.when(p == pl.num_programs(0) - 1)
    def _():
        lse_out[...] = lse_cols[...].T[0:8]


def branch_body(ctx, w, bias, branch_out):
    for r in range(4):
        at = slice(r * 256, r * 256 + 256)
        branch_out[at, :] = nn(ctx[at, :], w[3]) + bias[0:1, 2 * D : 3 * D]


def store_square(odd, keep, send, slot, tile, val, o, width):
    for j in range(width):
        for i in range(4):
            col, top = slice(128 * j, 128 * j + 128), 64 * o + 16 * i
            even, other = val[top : top + 16, col], val[top + 64 : top + 80, col]
            keep[slot, tile + 4 * j + i] = jnp.where(odd, other, even)
            send[slot, tile + 4 * j + i] = jnp.where(odd, even, other)


def feed_body(
    n, place, gates, tok, branch, cot, ctx, w_out, bias, *refs
):
    gathered, refs = refs[:8], refs[8:]
    (layer_out, gm_out, gctx_out, keep_out, send_out, wo_keep, wo_send) = refs[:7]
    (w1, w2, mlow, gbr, gs_all, active_all, gh_all, sums_out) = refs[7:]
    rows_up = D // (n // 2)
    rows_down = FF // (n // 2)
    tiles = rows_down // 16 * 4

    def assemble(z, _):
        for d in range(8):
            o = (8 * z + d) ^ place[0]

            @pl.when(o < n // 2)
            def _():
                for i in range(rows_up // 16):
                    for j in range(16):
                        row = pl.ds(pl.multiple_of(o * rows_up + 16 * i, 16), 16)
                        w1[row, 128 * j : 128 * j + 128] = gathered[d][z, 16 * i + j]

            @pl.when(o >= n // 2)
            def _():
                for i in range(rows_down // 16):
                    for j in range(4):
                        row = pl.ds(pl.multiple_of((o - n // 2) * rows_down + 16 * i, 16), 16)
                        w2[row, 128 * j : 128 * j + 128] = gathered[d][z, 4 * i + j]

        return 0

    lax.fori_loop(0, n // 8, assemble, 0)
    ga, gf = gates[0], gates[1]
    sums_out[...] = jnp.zeros_like(sums_out)
    c1 = 0.7978845608028654
    c2 = 0.044715

    def rows(r, carry):
        attend_sum, feed_sum = carry
        at = pl.ds(pl.multiple_of(r * 256, 256), 256)
        br = branch[at, :]
        middle = tok[at, :].astype(F32) + ga * br
        low = middle.astype(BF)
        mlow[at, :] = low
        ct = cot[at, :].astype(F32)
        gs = (gf * ct).astype(BF)
        gs_all[at, :] = gs
        second = jnp.zeros((256, D), F32) + bias[0:1, 3 * D : 4 * D]
        gmid = ct
        for j in range(4):
            cols = slice(512 * j, 512 * j + 512)
            v = nn(low, w1[:, cols]) + bias[0:1, 4 * D + 512 * j : 4 * D + 512 * j + 512]
            back = nt(gs, w2[cols, :])
            v2 = v * v
            t = jnp.tanh(c1 * v * (1.0 + c2 * v2))
            half = 0.5 * (1.0 + t)
            active = (v * half).astype(BF)
            slope = half + (0.5 * c1) * v * (1.0 - t * t) * (1.0 + (3.0 * c2) * v2)
            gh = (slope * back).astype(BF)
            active_all[at, cols] = active
            gh_all[at, cols] = gh
            sums_out[0:1, 4 * D + 512 * j : 4 * D + 512 * j + 512] += jnp.sum(
                gh.astype(F32), axis=0, keepdims=True
            )
            second = second + nn(active, w2[cols, :])
            gmid = gmid + nt(gh, w1[:, cols])
        layer_out[at, :] = (middle + gf * second).astype(BF)
        gm_out[at, :] = gmid
        gb = (ga * gmid).astype(BF)
        gbr[at, :] = gb
        gctx_out[at, :] = nt(gb, w_out[3]).astype(BF)
        sums_out[0:1, 2 * D : 3 * D] += jnp.sum(gb.astype(F32), axis=0, keepdims=True)
        sums_out[0:1, 3 * D : 4 * D] += jnp.sum(gs.astype(F32), axis=0, keepdims=True)
        attend_sum = attend_sum + jnp.sum(br * gmid, axis=0, keepdims=True)
        feed_sum = feed_sum + jnp.sum(second * ct, axis=0, keepdims=True)
        return attend_sum, feed_sum

    zero = jnp.zeros((1, D), F32)
    attend_sum, feed_sum = lax.fori_loop(0, 4, rows, (zero, zero))
    odd = place[1] == 1

    def store(even_owner, tile, even, other):
        keep_out[even_owner // 2, tile] = jnp.where(odd, other, even)
        send_out[even_owner // 2, tile] = jnp.where(odd, even, other)

    lane = lax.broadcasted_iota(jnp.int32, (1, 128), 1)
    gate = jnp.where(lane == 2 * place[2], jnp.sum(attend_sum), 0.0)
    gate = jnp.where(lane == 2 * place[2] + 1, jnp.sum(feed_sum), gate)
    high = gate.astype(BF).astype(F32)
    rest = gate - high
    mid = rest.astype(BF).astype(F32)
    low = (rest - mid).astype(BF).astype(F32)
    row = lax.broadcasted_iota(jnp.int32, (16, 128), 0)
    base = jnp.where(row == 1, high, jnp.where(row == 2, mid, jnp.where(row == 3, low, 0.0)))
    for o in range(0, n, 2):
        even = jnp.where(row == 0, sums_out[0:1, 128 * o : 128 * o + 128], base)
        other = jnp.where(row == 0, sums_out[0:1, 128 * o + 128 : 128 * o + 256], base)
        store(o, tiles, even, other)
    val = tn(ctx[...], gbr[...])
    for o in range(0, n // 4, 2):
        store_square(odd, wo_keep, wo_send, o // 2, 0, val, o, 4)

    for j in range(4):
        val = tn(mlow[...], gh_all[:, 512 * j : 512 * j + 512])
        for o in range(0, n // 2, 2):
            for i in range(rows_up // 16):
                for jj in range(4):
                    col = slice(128 * jj, 128 * jj + 128)
                    top = o * rows_up + 16 * i
                    store(o, 16 * i + 4 * j + jj, val[top : top + 16, col], val[top + rows_up : top + rows_up + 16, col])
    for j in range(4):
        val = tn(active_all[:, 512 * j : 512 * j + 512], gs_all[...])
        per = 512 // rows_down
        for o in range(0, per, 2):
            for i in range(rows_down // 16):
                for jj in range(4):
                    col = slice(128 * jj, 128 * jj + 128)
                    top = o * rows_down + 16 * i
                    store(
                        n // 2 + j * per + o, 4 * i + jj,
                        val[top : top + 16, col], val[top + rows_down : top + rows_down + 16, col],
                    )


def back_body(first, counts, lengths, place, q_in, k_in, v_in, gctx, lse, x_t, *refs):
    if first:
        before, refs = refs[0], refs[1:]
    dq_out, dk_out, dv_out, keep_out, send_out, *refs = refs
    if first:
        tail_keep, tail_send, *refs = refs
    else:
        sums, *refs = refs
    keys_mask, rows_mask, k_t, dq_t, dk_acc, dv_acc, *refs = refs
    if first:
        (sums,) = refs
    p = pl.program_id(0) + first

    @pl.when(pl.program_id(0) == 0)
    def _():
        slot_masks(counts, lengths, keys_mask, rows_mask)
        sums[...] = before[...] if first else jnp.zeros_like(sums)

    k_t[...] = k_in[...].T
    dk_acc[...] = jnp.zeros_like(dk_acc)
    dv_acc[...] = jnp.zeros_like(dv_acc)
    for parity in range(2):
        mine = half_of(parity, (ROWS, 128))
        ka = jnp.where(mine, k_in[...], keys_mask[parity])
        kt = k_t[64 * parity : 64 * parity + 64, :]
        logs = lse[pl.ds(2 * p + parity, 1), :]
        few = half_of(parity, (256, 128))
        for r in range(4):
            at = slice(r * 256, r * 256 + 256)
            qp = q_in[at, :]
            none = jnp.zeros_like(qp)
            st = nt(ka, jnp.where(few, qp, rows_mask[parity, at]))
            pt = jnp.exp(st - logs[:, at])
            gp = jnp.where(few, gctx[at, :], none)
            dpt = nt(v_in[...], gp)
            delta = jnp.sum(pt * dpt, axis=0, keepdims=True)
            dst = (pt * (dpt - delta)).astype(BF)
            dk_acc[...] += nn(dst, jnp.where(few, qp, none))
            dv_acc[...] += nn(pt.astype(BF), gp)
            dq_t[64 * parity : 64 * parity + 64, at] = nn(kt, dst) * 0.125
    dq = dq_t[...].T.astype(BF)
    dk = dk_acc[...].astype(BF)
    dv = dv_acc[...].astype(BF)
    dq_out[...] = dq
    dk_out[...] = dk
    dv_out[...] = dv
    sums[pl.ds(p, 1), :] = jnp.sum(dq.astype(F32), axis=0, keepdims=True)
    sums[pl.ds(4 + p, 1), :] = jnp.sum(dv.astype(F32), axis=0, keepdims=True)
    odd = place[1] == 1
    val = nn(x_t[...], jnp.concatenate([dq, dk, dv], axis=1))
    for square in range(3):
        for o in range(0, 8, 2):
            store_square(
                odd, keep_out.at[0], send_out.at[0], 4 * square + o // 2, 0,
                val[:, 128 * square : 128 * square + 128], o, 1,
            )
    if first:

        @pl.when(pl.program_id(0) == pl.num_programs(0) - 1)
        def _():
            row = lax.broadcasted_iota(jnp.int32, (16, 128), 0)
            for o in range(0, 8, 2):
                even = jnp.where(row == 0, sums[o : o + 1, :], 0.0)
                other = jnp.where(row == 0, sums[o + 1 : o + 2, :], 0.0)
                tail_keep[o // 2] = jnp.where(odd, other, even)
                tail_send[o // 2] = jnp.where(odd, even, other)


def split_row(tile):
    row = lax.broadcasted_iota(jnp.int32, tile.shape, 0)
    rest = tile[0:1] - tile[0:1].astype(BF).astype(F32)
    return jnp.where(row == 4, rest, tile)


def join_row(tile):
    row = lax.broadcasted_iota(jnp.int32, tile.shape, 0)
    whole = tile[0:1] + tile[4:5]
    return jnp.where(row == 0, whole, jnp.where(row == 4, 0.0, tile))


def feed_xy_body(place, keep, got, wo_keep, wo_got, *outs):
    size = keep.shape[1]
    for t in range(4):
        here = place[3] ^ t
        out = outs[t]
        for z in range(4):
            total = keep[4 * z + here] + got[4 * z + here]
            out[size * z : size * z + size - 1] = total[: size - 1].astype(out.dtype)
            out[size * z + size - 1] = (split_row(total[size - 1]) if t else total[size - 1]).astype(out.dtype)
        out[4 * size :] = (wo_keep[here] + wo_got[here]).astype(out.dtype)


def feed_z_body(place, keep, g1, g2, g3, out0, out1, out2, out3, wo_out):
    size = out0.shape[0]
    for t, out in enumerate((out0, out1, out2, out3)):
        at = pl.ds((place[4] ^ t) * size, size - 1)
        total = keep[at] + g1[at].astype(F32) + g2[at].astype(F32) + g3[at].astype(F32)
        out[: size - 1] = total.astype(out.dtype)
        at = (place[4] ^ t) * size + size - 1
        total = keep[at]
        for g in (g1, g2, g3):
            total = total + join_row(g[at].astype(F32))
        out[size - 1] = (split_row(total) if t else total).astype(out.dtype)
    at = slice(4 * size, 4 * size + 16)
    wo_out[...] = keep[at] + g1[at].astype(F32) + g2[at].astype(F32) + g3[at].astype(F32)


def square_xy_body(place, keep0, got0, keep1, got1, tail_keep, tail_got, *outs):
    for t in range(4):
        here = place[3] ^ t
        out = outs[t]
        for z in range(3):
            for p in range(4):
                keep, got, at = (keep0, got0, 0) if p == 0 else (keep1, got1, p - 1)
                total = keep[at, 4 * z + here] + got[at, 4 * z + here]
                out[16 * z + 4 * p : 16 * z + 4 * p + 4] = total.astype(out.dtype)
        total = tail_keep[here] + tail_got[here]
        out[48] = (split_row(total) if t else total).astype(out.dtype)


def square_z_body(place, keep, g1, g2, g3, wo, out0, out1, out2, out3, whole):
    for z in range(3):
        at = slice(16 * z, 16 * z + 16)
        whole[z, :16] = keep[at] + g1[at].astype(F32) + g2[at].astype(F32) + g3[at].astype(F32)
        whole[z + 1, 16] = jnp.zeros((16, 128), F32)
    whole[3, :16] = wo[...]
    total = keep[48]
    for g in (g1, g2, g3):
        total = total + join_row(g[48].astype(F32))
    whole[0, 16] = total
    for t, out in enumerate((out0, out1, out2, out3)):
        at = place[4] ^ t
        out[:16] = whole[at, :16].astype(out.dtype)
        out[16] = (split_row(whole[at, 16]) if t else whole[at, 16]).astype(out.dtype)


def last_body(keep, g1, g2, g3, out):
    size = keep.shape[0]
    at = slice(0, size - 1)
    out[at] = keep[at] + g1[at].astype(F32) + g2[at].astype(F32) + g3[at].astype(F32)
    total = keep[size - 1]
    for g in (g1, g2, g3):
        total = total + join_row(g[size - 1].astype(F32))
    out[size - 1] = total


def input_body(gm, dq, dk, dv, w, out):
    def rows(r, _):
        at = pl.ds(pl.multiple_of(r * 256, 256), 256)
        out[at, :] = gm[at, :] + nt(dq[at, :], w[0]) + nt(dk[at, :], w[1]) + nt(dv[at, :], w[2])
        return 0

    lax.fori_loop(0, 4, rows, 0)


def to_tiles(flat, rows, cols):
    return flat.reshape(rows // 16, 16, cols // 128, 128).transpose(0, 2, 1, 3).reshape(-1, 16, 128)


def from_tiles(tiles, rows, cols):
    return tiles.reshape(rows // 16, cols // 128, 16, 128).transpose(0, 2, 1, 3).reshape(-1)


def from_columns(tiles, rows):
    return tiles.reshape(-1, rows // 16, 16, 128).transpose(1, 2, 0, 3).reshape(-1)


def swap(x, n, bit):
    return lax.ppermute(x, AXES, [(i, i ^ bit) for i in range(n)])


def small(body, outs, args, scratch=()):
    ins = [SMEM if arg.dtype == jnp.int32 else VMEM for arg in args]
    size = sum(arg.size for arg in args)
    return call(body, outs, ins, scratch, 2 * size, 6 * size, 16)(*args)


def blocks_of(*shape):
    return [(shape + (16, 128), F32)] + [(shape + (16, 128), BF)] * 3


def hop(parts, n, step):
    return [parts[0]] + [swap(part, n, step * t) for t, part in enumerate(parts) if t]


def along_z(own, n):
    return jnp.stack([own] + [swap(own, n, 8 * z) for z in (1, 2, 3)])


def along_xy(stack, n):
    return [stack] + [swap(stack, n, bits) for bits in (2, 4, 6)]


def along_core(chips, n):
    return [part for chip in chips for part in (chip, swap(chip, n, 1))]


def tie(values, after):
    return lax.optimization_barrier((values, after))[0]


def gather(attention, feedforward, biases, n, me):
    rows_each, rows_up, rows_down = 4 * D // n, D // (n // 2), FF // (n // 2)
    tail = jnp.pad(biases[None, None, :], ((0, 0), (0, 15), (0, 0)))
    own_a = jnp.concatenate([to_tiles(attention, rows_each, D), tail], axis=0)
    own_f = jnp.where(
        me < n // 2, to_tiles(feedforward, rows_up, FF), to_tiles(feedforward, rows_down, D)
    )
    stack_a = along_z(own_a, n)
    stack_f = along_z(tie(own_f, stack_a), n)
    return along_core(along_xy(stack_a, n), n), stack_f


def gather_any(attention, feedforward, biases):
    rows_each, rows_up, rows_down = 4 * D // PARTS, D // (PARTS // 2), FF // (PARTS // 2)
    full = lax.all_gather(attention, AXES, axis=0, tiled=True).reshape(PARTS, -1)
    tail = lax.all_gather(biases, AXES, axis=0, tiled=True).reshape(PARTS, 1, 1, 128)
    tail = jnp.pad(tail, ((0, 0), (0, 0), (0, 15), (0, 0)))
    squares = jax.vmap(lambda f: to_tiles(f, rows_each, D))(full)
    full = lax.all_gather(feedforward, AXES, axis=0, tiled=True).reshape(PARTS, -1)
    up = jax.vmap(lambda f: to_tiles(f, rows_up, FF))(full[: PARTS // 2])
    down = jax.vmap(lambda f: to_tiles(f, rows_down, D))(full[PARTS // 2 :])
    pieces = jnp.concatenate([squares, tail], axis=1), jnp.concatenate([up, down])
    return [[p.reshape((4, 8) + p.shape[1:])[:, d] for d in range(8)] for p in pieces]


def local(direct, tokens, cotangent, attention, feedforward, biases, gates, counts, lengths):
    me = lax.axis_index(AXES)
    n = PARTS
    rows_each, rows_up, rows_down = 4 * D // n, D // (n // 2), FF // (n // 2)
    tiles = 4 * rows_each // 16
    ftiles = 4 * rows_down // 16
    if direct:
        ga_all, stack_f = gather(attention, feedforward, biases, n, me)
        place = jnp.stack([me, me % 2, me, (me // 2) % 4, me // 8]).astype(jnp.int32)
    else:
        ga_all, gf_all = gather_any(attention, feedforward, biases)
        place = jnp.zeros((5,), jnp.int32)
    row = (ROWS, D)
    masks = [((2, ROWS, 128), BF), ((2, ROWS, 128), BF)]
    q, k, v, x_t, w, bias = call(
        partial(project_body, n),
        [(row, BF)] * 3 + [((D, ROWS), BF), ((4, D, D), BF), ((1, 8 * D), F32)],
        [SMEM] + [VMEM] * 9, [], 2 << 30, 10 << 20, 48,
    )(place, tokens, *ga_all)
    if direct:
        stack_f, q = lax.optimization_barrier((stack_f, q))
        chips_f = along_xy(stack_f, n)
    pair = pl.BlockSpec((ROWS, 128), lambda i: (0, i))
    ctx, lse = call(
        attend_body,
        [(row, BF, pair), ((8, ROWS), F32, pl.BlockSpec((8, ROWS), lambda i: (0, 0)))],
        [SMEM, SMEM] + [pair] * 3,
        masks + [((ROWS, 128), F32)],
        12 << 30, 4 << 20, 60, (4,),
    )(counts, lengths, q, k, v)
    if direct:
        chips_f, ctx = lax.optimization_barrier((chips_f, ctx))
        gf_all = along_core(chips_f, n)
    (branch,) = call(branch_body, [(row, F32)], [VMEM] * 3, [], 1 << 30, 4 << 20, 32)(ctx, w, bias)
    layer, gm, gctx, ff_keep, ff_send, wo_keep, wo_send = call(
        partial(feed_body, n),
        [(row, BF), (row, F32), (row, BF)] + [((n // 2, ftiles + 1, 16, 128), F32)] * 2
        + [((n // 8, 16, 16, 128), F32)] * 2,
        [SMEM, SMEM] + [VMEM] * 14,
        [((D, FF), BF), ((FF, D), BF), (row, BF), (row, BF), (row, BF), ((ROWS, FF), BF), ((ROWS, FF), BF),
         ((1, 8 * D), F32)],
        14 << 30, 30 << 20, 62,
    )(place, gates, tokens, branch, cotangent, ctx, w, bias, *gf_all)

    def back(first, pairs, q, before):
        cols = pl.BlockSpec((ROWS, 128), lambda i: (0, first + i))
        part = ((ROWS, 128 * pairs), BF, pl.BlockSpec((ROWS, 128), lambda i: (0, i)))
        sent = ((pairs, 12, 4, 16, 128), F32, pl.BlockSpec((1, 12, 4, 16, 128), lambda i: (i, 0, 0, 0, 0)))
        sums = pl.BlockSpec((8, 128), lambda i: (0, 0))
        tail = ((4, 16, 128), F32, pl.BlockSpec((4, 16, 128), lambda i: (0, 0, 0)))
        return call(
            partial(back_body, first),
            [part] * 3 + [sent] * 2 + ([tail] * 2 if first else [((8, 128), F32, sums)]),
            [SMEM] * 3 + [cols] * 4
            + [pl.BlockSpec((8, ROWS), lambda i: (0, 0)), pl.BlockSpec((D, ROWS), lambda i: (0, 0))]
            + ([sums] if first else []),
            masks + [((128, ROWS), BF), ((128, ROWS), F32), ((ROWS, 128), F32), ((ROWS, 128), F32)]
            + ([((8, 128), F32)] if first else []),
            pairs * (5 << 30), 4 << 20, 60, (pairs,),
        )(counts, lengths, place, q, k, v, gctx, lse, x_t, *([before] if first else []))

    if direct:
        got, wo_got = swap(ff_send, n, 1), swap(wo_send, n, 1)
    *part0, keep0, send0, before = back(0, 1, q, None)
    if direct:
        got, wo_got, part0, send0 = lax.optimization_barrier((got, wo_got, part0, send0))
        size = 4 * ftiles + 20
        parts = small(feed_xy_body, blocks_of(size), (place, ff_keep, got, wo_keep, wo_got))
        q, parts = lax.optimization_barrier((q, parts))
        got0 = swap(send0, n, 1)
        ff_got = hop(parts, n, 2)
    part1 = back(1, 3, q, before)
    if direct:
        ff_got, part1 = lax.optimization_barrier((ff_got, part1))
    *part1, keep1, send1, tail_keep, tail_send = part1
    dq, dk, dv = [jnp.concatenate(both, axis=1) for both in zip(part0, part1)]
    if direct:
        got1, tail_got = swap(send1, n, 1), swap(tail_send, n, 1)
        *ff_parts, wo = small(
            feed_z_body, blocks_of(ftiles + 1) + [((16, 16, 128), F32)], (place, *ff_got)
        )
        ff_got = hop(ff_parts, n, 8)
        tail_keep, ff_parts = lax.optimization_barrier((tail_keep, ff_parts))
        parts = small(square_xy_body, blocks_of(49), (place, keep0, got0, keep1, got1, tail_keep, tail_got))
        got = hop(parts, n, 2)
        gm, parts = lax.optimization_barrier((gm, parts))
    (input_grad,) = call(
        input_body, [(row, F32)], [VMEM] * 5, [], 2 << 30, 8 << 20, 32
    )(gm, dq, dk, dv, w)
    if direct:
        got, input_grad, ff_got = lax.optimization_barrier((got, input_grad, ff_got))
        parts = small(square_z_body, blocks_of(17), (place, *got, wo), [((4, 17, 16, 128), F32)])
        got = hop(parts, n, 8)
        ff_got, parts = lax.optimization_barrier((ff_got, parts))
        (ff_shard,) = small(last_body, [((ftiles + 1, 16, 128), F32)], ff_got)
        (att_shard,) = small(last_body, [((17, 16, 128), F32)], got)
        ff_grad = jnp.where(
            me < n // 2, from_tiles(ff_shard[:ftiles], rows_up, FF), from_tiles(ff_shard[:ftiles], rows_down, D)
        )
        att_grad = from_columns(att_shard[:tiles], rows_each)
        tail = ff_shard[ftiles]
        bias_grad = jnp.where(me < 8, att_shard[tiles][0], tail[0])
        gate_grad = jnp.sum((tail[1] + tail[2] + tail[3])[: 2 * n].reshape(n, 2), axis=0)
        return layer, input_grad, att_grad, ff_grad, bias_grad, gate_grad

    def owners(keep, send):
        return jnp.stack([keep, send], axis=1).reshape((-1,) + keep.shape[1:])

    def reduce(flat):
        return lax.psum_scatter(flat.reshape(-1), AXES, scatter_dimension=0, tiled=True)

    both = owners(ff_keep, ff_send)
    up = jax.vmap(lambda t: from_tiles(t, rows_up, FF))(both[: n // 2, :ftiles]).reshape(-1)
    down = jax.vmap(lambda t: from_tiles(t, rows_down, D))(both[n // 2 :, :ftiles]).reshape(-1)
    ff_grad = reduce(jnp.concatenate([up, down]))
    tail = both[0, ftiles]
    gate_grad = lax.psum((tail[1] + tail[2] + tail[3])[:2], AXES)
    bias_grad = jnp.concatenate([owners(tail_keep, tail_send)[:, 0], both[8:, ftiles, 0]])
    keep, send = jnp.concatenate([keep0, keep1]), jnp.concatenate([send0, send1])
    both = jnp.stack([keep, send], axis=2).reshape(4, 24, 4, 16, 128).transpose(1, 0, 2, 3, 4)
    both = jnp.concatenate([both.reshape(24, tiles, 16, 128), owners(wo_keep, wo_send)])
    att_grad = jax.vmap(lambda t: from_columns(t, rows_each))(both)
    return layer, input_grad, reduce(att_grad), ff_grad, reduce(bias_grad), gate_grad


def solution(mesh):
    direct = dict(mesh.shape) == {"dp": 8, "fsdp": 4}
    both = P(AXES)
    rows = P(AXES, None)
    return jax.shard_map(
        partial(local, direct),
        mesh=mesh,
        in_specs=(rows, rows, both, both, both, P(), rows, rows),
        out_specs=(rows, rows, both, both, both, P()),
        check_vma=False,
    )
```

```python
from functools import partial

import jax
import jax.numpy as jnp
from jax import lax
from jax.experimental import pallas as pl
from jax.experimental.pallas import tpu as pltpu
from jax.sharding import PartitionSpec as P

D = 512
H = 8
HD = 64
FF = 2048
ROWS = 1024
SLOTS = 8
SHORT = 128
MID = 512
LONG = 1024
AXES = ("dp", "fsdp")
PARTS = 32
A_TILES = 17
F_TILES = 32
G_TILES = 33
BF = jnp.bfloat16
F32 = jnp.float32
CHUNK = 64
BIG = 512
VMEM = pl.BlockSpec(memory_space=pltpu.VMEM)
SMEM = pl.BlockSpec(memory_space=pltpu.SMEM)
ANY = pl.BlockSpec(memory_space=pl.ANY)
DMA = pltpu.SemaphoreType.DMA


def nn(a, b):
    return lax.dot_general(a, b, (((1,), (0,)), ((), ())), preferred_element_type=F32)


def nt(a, b):
    return lax.dot_general(a, b, (((1,), (1,)), ((), ())), preferred_element_type=F32)


def call(body, outs, ins, scratch, flops, moved, limit, grid=None):
    return pl.pallas_call(
        body,
        out_shape=[jax.ShapeDtypeStruct(o[0], o[1]) for o in outs],
        grid=grid or (),
        in_specs=ins,
        out_specs=[o[2] if len(o) > 2 else VMEM for o in outs],
        scratch_shapes=[pltpu.VMEM(*s) if isinstance(s, tuple) else s for s in scratch],
        compiler_params=pltpu.CompilerParams(vmem_limit_bytes=limit << 20),
        cost_estimate=pl.CostEstimate(flops=flops, bytes_accessed=moved, transcendentals=0),
    )


def slot_masks(counts, lengths, keys_out, rows_out):
    lane = lax.broadcasted_iota(jnp.int32, (1, 128), 1)
    slot = lane & 63
    longs, mids, shorts = counts[0, 2], counts[0, 1], counts[0, 0]
    in_long = jnp.minimum(slot, longs)
    in_mid = jnp.clip(slot - longs, 0, mids)
    in_short = jnp.clip(slot - longs - mids, 0, shorts)
    start = in_long * LONG + in_mid * MID + in_short * SHORT
    size = jnp.where(
        slot < longs,
        LONG,
        jnp.where(slot < longs + mids, MID, jnp.where(slot < longs + mids + shorts, SHORT, 0)),
    )
    valid = jnp.zeros((1, 128), jnp.int32)
    for s in range(SLOTS):
        valid = jnp.where(slot == s, lengths[0, s], valid)
    row = lax.broadcasted_iota(jnp.int32, (ROWS, 128), 0)
    member = (row >= start) & (row < start + size)
    usable = (row >= start) & (row < start + valid)
    for parity in range(2):
        here = (slot < SLOTS) & ((lane >= 64) if parity == 0 else (lane < 64))
        rows_out[parity] = jnp.where(here & member, 1.0, 0.0).astype(BF)
        keys_out[parity] = jnp.where(here & jnp.logical_not(usable), -1e30, 0.0).astype(BF)


def prepare_body(counts, lengths, tok, keys_mask, rows_mask, x_t):
    slot_masks(counts, lengths, keys_mask, rows_mask)
    x_t[:D] = tok[...].T
    x_t[D:] = jnp.ones((16, ROWS), BF)


def half_of(parity, shape):
    lane = lax.broadcasted_iota(jnp.int32, shape, len(shape) - 1)
    return (lane < 64) if parity == 0 else (lane >= 64)


def assemble(pieces, dest, me):
    for c in range(2):
        for xy in range(4):
            for z in range(4):
                dest[(8 * z + 2 * xy + c) ^ me] = pieces[4 * c + xy][z]


def columns(ref, owners, tiles, each):
    parts = []
    for t in range(tiles.start, tiles.stop, each):
        part = ref[owners, t : t + each]
        parts.append(part.reshape(part.shape[0] * each * 16, 128))
    return jnp.concatenate(parts, axis=1)


def square(ref, index):
    return columns(ref, slice(8 * index, 8 * index + 8), slice(0, 16), 4)


def project_body(place, tok, keys_mask, rows_mask, *refs):
    pieces, (q_out, k_out, v_out, w_out, bias_out) = refs[:8], refs[8:]
    assemble(pieces, w_out, place[0])
    for o in range(PARTS):
        bias_out[0:1, 128 * o : 128 * o + 128] = w_out[o, A_TILES - 1].astype(F32)[0:1]
    for r in range(4):
        at = slice(256 * r, 256 * r + 256)
        x = tok[at, :]
        q = (nn(x, square(w_out, 0)) + bias_out[0:1, 0:D]).astype(BF)
        q = (q.astype(F32) * 0.125).astype(BF)
        k = nn(x, square(w_out, 1)).astype(BF)
        v_out[at, :] = (nn(x, square(w_out, 2)) + bias_out[0:1, D : 2 * D]).astype(BF)
        for h in range(H):
            mine = half_of(h % 2, (256, 128))
            lanes = slice(h // 2 * 128, h // 2 * 128 + 128)
            q_out[h, at] = jnp.where(mine, q[:, lanes], rows_mask[h % 2, at])
            k_out[h, at] = jnp.where(mine, k[:, lanes], keys_mask[h % 2, at])


def attend_body(q_all, k_all, v_all, ctx_out, ctx_t_out, lse_out, values_t, ctx_t, s0, s1, p0, p1):
    def pair(p, _):
        attend_pair(
            p, q_all.at[pl.ds(2 * p, 2)], k_all.at[pl.ds(2 * p, 2)], v_all, ctx_out, ctx_t_out, lse_out, values_t, ctx_t,
            s0, s1, p0, p1,
        )
        return 0

    lax.fori_loop(0, 4, pair, 0)


def attend_pair(p, q_in, k_in, v_all, ctx_out, ctx_t_out, lse_out, values_t, ctx_t, s0, s1, p0, p1):
    lanes = pl.ds(pl.multiple_of(p * 128, 128), 128)
    scores, probs = (s0, s1), (p0, p1)
    values_t[...] = v_all[:, lanes].T
    steps = [(parity, r) for parity in range(2) for r in range(4)]

    def score(i):
        parity, r = steps[i]

        def part(c):
            scores[i % 2][c : c + 256] = nt(k_in[parity, c : c + 256], q_in[parity, r * 256 : r * 256 + 256])

        return [partial(part, c) for c in range(0, ROWS, 256)]

    def collect(i):
        parity, r = steps[i]
        rows = slice(64 * parity, 64 * parity + 64)
        total = []

        def part(c):
            total.append(nn(values_t[rows, c : c + 256], probs[i % 2][c : c + 256]))
            if c == ROWS - 256:
                ctx_t[rows, r * 256 : r * 256 + 256] = (total[0] + total[1]) + (total[2] + total[3])

        return [partial(part, c) for c in range(0, ROWS, 256)]

    def soften(i):
        parity, r = steps[i]
        s, out = scores[i % 2], probs[i % 2]
        state = {}

        def peak(c):
            part = jnp.max(s[c : c + CHUNK].reshape(-1, 8, 256), axis=0)
            state["top"] = jnp.maximum(state["top"], part) if c else part
            if c == ROWS - CHUNK:
                state["top"] = jnp.max(state["top"], axis=0, keepdims=True)

        def power(c):
            e = jnp.exp(s[c : c + CHUNK] - state["top"])
            s[c : c + CHUNK] = e
            part = jnp.sum(e.reshape(-1, 8, 256), axis=0)
            state["mass"] = state["mass"] + part if c else part
            if c == ROWS - CHUNK:
                mass = jnp.sum(state["mass"], axis=0, keepdims=True)
                lse_out[pl.ds(2 * p + parity, 1), r * 256 : r * 256 + 256] = state["top"] + jnp.log(mass)
                state["share"] = 1.0 / mass

        def share(c):
            out[c : c + CHUNK] = (s[c : c + CHUNK] * state["share"]).astype(BF)

        at = range(0, ROWS, CHUNK)
        return [(1, partial(peak, c)) for c in at] + [(3, partial(power, c)) for c in at] + [
            (1.5, partial(share, c)) for c in at
        ]

    for task in score(0):
        task()
    for i in range(9):
        later = (score(i + 1) if i < 7 else []) + (collect(i - 1) if i else [])
        mix(soften(i) if i < 8 else [], later)
    low = ctx_t[...].astype(BF)
    ctx_t_out[lanes, :] = low
    ctx_out[:, lanes] = low.T


def mix(vector, matrix):
    whole = sum(weight for weight, _ in vector) or 1
    done, given = 0, 0
    for weight, task in vector:
        while given < len(matrix) and given * whole <= done * len(matrix):
            matrix[given]()
            given += 1
        task()
        done += weight
    for task in matrix[given:]:
        task()


def feed_body(place, gates, tok, cot, ctx, ctx_t_in, w_in, bias, *refs):
    pieces, refs = refs[:8], refs[8:]
    (layer_out, gm_out, gctx_out, keep_out, send_out, wo_keep, wo_send) = refs[:7]
    (w, low_t, ctx_t, gbr, gs_all, active_t, gh_all, v0, v1, b0, b1, active, second, gmid, sums) = refs[7:22]
    (layer, gm, gctx, both, wo_both, sems) = refs[22:]
    values, backs = (v0, v1), (b0, b1)
    wo = w_in.at[24:32]
    assemble(pieces, w, place[0])
    ctx_t[:D] = ctx_t_in[...]

    def rows_of(r):
        return pl.ds(pl.multiple_of(r * 256, 256), 256)

    ga, gf = gates[0], gates[1]
    c1 = 0.7978845608028654
    c2 = 0.044715
    ones = jnp.ones((16, ROWS), BF)
    low_t[D:] = ones
    active_t[FF:] = ones
    ctx_t[D:] = ones

    def w_up(j):
        return columns(w, slice(0, 16), slice(8 * j, 8 * j + 8), 2)

    def w_down(j):
        return columns(w, slice(16 + 4 * j, 20 + 4 * j), slice(0, 32), 8)

    def rows(r, carry):
        attend_sum, feed_sum = carry
        at = rows_of(r)
        br = nn(ctx[at, :], square(wo, 0)) + bias[0:1, 2 * D : 3 * D]
        middle = tok[at, :].astype(F32) + ga * br
        low = middle.astype(BF)
        low_t[:D, at] = low.T
        ct = cot[at, :].astype(F32)
        gs = (gf * ct).astype(BF)
        gs_all[at, :] = gs

        def first(j):
            up, down = w_up(j), w_down(j)

            def value(n):
                values[j % 2][:, n : n + 256] = nn(low, up[:, n : n + 256])

            def back(n):
                backs[j % 2][:, n : n + 256] = nt(gs, down[n : n + 256])

            return [partial(f, n) for n in (0, 256) for f in (value, back)]

        def bend(j):
            def part(c):
                lines = slice(c, c + 32)
                cols = slice(4 * D + 512 * j, 4 * D + 512 * j + 512)
                v = values[j % 2][lines] + bias[0:1, cols]
                v2 = v * v
                t = jnp.tanh(v * (c1 + (c1 * c2) * v2))
                half = 0.5 + 0.5 * t
                act = v * half
                slope = half * (1.0 + (v - act) * (2.0 * c1 + (6.0 * c1 * c2) * v2))
                active[lines, 512 * j : 512 * j + 512] = act.astype(BF)
                gh_all[pl.ds(r * 256 + c, 32), 512 * j : 512 * j + 512] = (slope * backs[j % 2][lines]).astype(BF)

            return [(1, partial(part, c)) for c in range(0, 256, 32)]

        def then(j):
            up, down = w_up(j), w_down(j)
            cols = slice(512 * j, 512 * j + 512)

            def forward(n):
                val = nn(active[:, cols], down[:, n : n + 256])
                second[:, n : n + 256] = second[:, n : n + 256] + val if j else val

            def backward(n):
                val = nt(gh_all[at, cols], up[n : n + 256])
                gmid[:, n : n + 256] = gmid[:, n : n + 256] + val if j else val

            def turn():
                active_t[cols, at] = active[:, cols].T

            return [turn] + [partial(f, n) for n in (0, 256) for f in (forward, backward)]

        for task in first(0):
            task()
        for j in range(5):
            mix(bend(j) if j < 4 else [], (first(j + 1) if j < 3 else []) + (then(j - 1) if j else []))
        out = second[...] + bias[0:1, 3 * D : 4 * D]
        layer[at, :] = (middle + gf * out).astype(BF)
        grad = ct + gmid[...]
        gm[at, :] = grad
        gb = (ga * grad).astype(BF)
        gbr[at, :] = gb
        gctx[at, :] = nt(gb, square(wo, 0)).astype(BF)
        for index, (ref, dest) in enumerate(((layer, layer_out), (gm, gm_out), (gctx, gctx_out))):
            pltpu.make_async_copy(ref.at[at], dest.at[at], sems.at[index]).start()
        attend_sum = attend_sum + jnp.sum(br * grad, axis=0, keepdims=True)
        feed_sum = feed_sum + jnp.sum(out * ct, axis=0, keepdims=True)
        return attend_sum, feed_sum

    zero = jnp.zeros((1, D), F32)
    attend_sum, feed_sum = lax.fori_loop(0, 4, rows, (zero, zero))
    odd = place[1]

    def send(slots, sem):
        copies = [
            pltpu.make_async_copy(both.at[0, slots], keep_out.at[slots], sems.at[sem]),
            pltpu.make_async_copy(both.at[1, slots], send_out.at[slots], sems.at[sem + 1]),
        ]
        for copy in copies:
            copy.start()
        return copies

    for j in range(4):
        val = nn(low_t[...], gh_all[:, 512 * j : 512 * j + 512])
        sums[0:1, 4 * D + 512 * j : 4 * D + 512 * j + 512] = val[D : D + 1]
        for o in range(16):
            for jj in range(4):
                for i in range(2):
                    top, col = 32 * o + 16 * i, slice(128 * jj, 128 * jj + 128)
                    both[(o % 2) ^ odd, o // 2, 2 * (4 * j + jj) + i] = val[top : top + 16, col]
    val = nn(ctx_t[...], gbr[...])
    sums[0:1, 2 * D : 3 * D] = val[D : D + 1]
    for o in range(8):
        for j in range(4):
            for i in range(4):
                top, col = 64 * o + 16 * i, slice(128 * j, 128 * j + 128)
                wo_both[(o % 2) ^ odd, o // 2, 4 * j + i] = val[top : top + 16, col]
    copies = [
        pltpu.make_async_copy(wo_both.at[0], wo_keep, sems.at[3]),
        pltpu.make_async_copy(wo_both.at[1], wo_send, sems.at[4]),
    ]
    for copy in copies:
        copy.start()
    lane = lax.broadcasted_iota(jnp.int32, (1, 128), 1)
    gate = jnp.where(lane == 2 * place[2], jnp.sum(attend_sum), 0.0)
    gate = jnp.where(lane == 2 * place[2] + 1, jnp.sum(feed_sum), gate)
    high = gate.astype(BF).astype(F32)
    rest = gate - high
    mid = rest.astype(BF).astype(F32)
    last = (rest - mid).astype(BF).astype(F32)
    row = lax.broadcasted_iota(jnp.int32, (16, 128), 0)
    base = jnp.where(row == 1, high, jnp.where(row == 2, mid, jnp.where(row == 3, last, 0.0)))
    sums[0:1, 0 : 2 * D] = jnp.zeros((1, 2 * D), F32)

    def tail(o):
        both[(o % 2) ^ odd, o // 2, G_TILES - 1] = jnp.where(row == 0, sums[0:1, 128 * o : 128 * o + 128], base)

    for j in (3, 2, 1, 0):
        val = nn(active_t[512 * j : 512 * j + (528 if j == 3 else 512)], gs_all[...])
        if j == 3:
            sums[0:1, 3 * D : 4 * D] = val[D : D + 1]
            for o in range(16):
                tail(o)
            copies += send(pl.ds(0, 8), 5)
        for o in range(4):
            tail(16 + 4 * j + o)
            for jj in range(4):
                for i in range(8):
                    top, col = 128 * o + 16 * i, slice(128 * jj, 128 * jj + 128)
                    both[(o % 2) ^ odd, 8 + 2 * j + o // 2, 8 * jj + i] = val[top : top + 16, col]
        copies += send(pl.ds(8 + 2 * j, 2), 7 + 2 * j)
    for index, (ref, dest) in enumerate(((layer, layer_out), (gm, gm_out), (gctx, gctx_out))):
        pltpu.make_async_copy(ref, dest, sems.at[index]).wait()
    for copy in copies:
        copy.wait()


def back_body(first, place, q_all, k_all, v_all, g_all, lse, x_t, *refs):
    if first:
        before, *refs = refs
    dq_out, dk_out, dv_out, keep_out, send_out, *refs = refs
    if first == 3:
        *refs, sums = refs
    else:
        sums, *refs = refs
    k_t, dq_t, dk_acc, dv_acc, s0, s1, g0, g1, p0, p1, d0, d1 = refs
    scores, grads, probs, diffs = (s0, s1), (g0, g1), (p0, p1), (d0, d1)
    steps = [(parity, r) for parity in range(2) for r in range(4)]
    odd = place[1] == 1
    sums[...] = before[...] if first else jnp.zeros_like(sums)

    def pair(turn, _):
        p = turn + first
        lanes = pl.ds(pl.multiple_of(p * 128, 128), 128)
        out = pl.ds(pl.multiple_of(turn * 128, 128), 128)
        q_in, k_in = q_all.at[pl.ds(2 * p, 2)], k_all.at[pl.ds(2 * p, 2)]
        for parity in range(2):
            k_t[parity] = k_in[parity].T

        def mine(block, i):
            return jnp.where(half_of(steps[i][0], (256, 128)), block, jnp.zeros_like(block))

        def score(i):
            parity, r = steps[i]
            qa = q_in[parity, r * 256 : r * 256 + 256]
            ga = mine(g_all[r * 256 : r * 256 + 256, lanes], i)

            def part(c):
                scores[i % 2][c : c + BIG] = nt(k_in[parity, c : c + BIG], qa)

            def grad(c):
                grads[i % 2][c : c + BIG] = nt(v_all[c : c + BIG, lanes], ga)

            return [task for c in range(0, ROWS, BIG) for task in (partial(part, c), partial(grad, c))]

        def soften(i):
            parity, r = steps[i]
            s, g, out, diff = scores[i % 2], grads[i % 2], probs[i % 2], diffs[i % 2]
            logs = lse[pl.ds(2 * p + parity, 1), r * 256 : r * 256 + 256]
            state = {}

            def power(c):
                e = jnp.exp(s[c : c + CHUNK] - logs)
                s[c : c + CHUNK] = e
                out[c : c + CHUNK] = e.astype(BF)
                part = jnp.sum((e * g[c : c + CHUNK]).reshape(-1, 8, 256), axis=0)
                state["inner"] = state["inner"] + part if c else part
                if c == ROWS - CHUNK:
                    state["inner"] = jnp.sum(state["inner"], axis=0, keepdims=True)

            def minus(c):
                diff[c : c + CHUNK] = (s[c : c + CHUNK] * (g[c : c + CHUNK] - state["inner"])).astype(BF)

            at = range(0, ROWS, CHUNK)
            return [(5.5, partial(power, c)) for c in at] + [(2.5, partial(minus, c)) for c in at]

        def collect(i):
            parity, r = steps[i]
            rows = slice(64 * parity, 64 * parity + 64)
            at = slice(r * 256, r * 256 + 256)
            qz, gz = mine(q_in[parity, at], i), mine(g_all[at, lanes], i)
            total = []

            def part(c):
                total.append(nn(k_t[parity, rows, c : c + 256], diffs[i % 2][c : c + 256]))
                if c == ROWS - 256:
                    dq_t[rows, r * 256 : r * 256 + 256] = ((total[0] + total[1]) + (total[2] + total[3])) * 0.125

            def add(acc, ref, z, c):
                val = nn(ref[c : c + BIG], z)
                acc[c : c + BIG] = acc[c : c + BIG] + val if i else val

            tasks = []
            for c in range(0, ROWS, 256):
                if c % BIG == 0:
                    tasks += [partial(add, dv_acc, probs[i % 2], gz, c), partial(add, dk_acc, diffs[i % 2], qz, c)]
                tasks += [partial(part, c)]
            return tasks

        for task in score(0):
            task()
        for i in range(9):
            later = (score(i + 1) if i < 7 else []) + (collect(i - 1) if i else [])
            mix(soften(i) if i < 8 else [], later)
        dq = dq_t[...].astype(BF).T
        dk = dk_acc[...].astype(BF)
        dv = dv_acc[...].astype(BF)
        dq_out[:, out] = dq
        dk_out[:, out] = dk
        dv_out[:, out] = dv
        val = nn(x_t[...], jnp.concatenate([dq, dk, dv, dv], axis=1))
        sums[pl.ds(p, 1), :] = val[D : D + 1, 0:128]
        sums[pl.ds(4 + p, 1), :] = val[D : D + 1, 256:384]
        for index in range(3):
            for o in range(0, 8, 2):
                for i in range(4):
                    col, top = slice(128 * index, 128 * index + 128), 64 * o + 16 * i
                    even, other = val[top : top + 16, col], val[top + 64 : top + 80, col]
                    keep_out[12 * turn + 4 * index + o // 2, i] = jnp.where(odd, other, even)
                    send_out[12 * turn + 4 * index + o // 2, i] = jnp.where(odd, even, other)
        return 0

    lax.fori_loop(0, dq_out.shape[1] // 128, pair, 0)
    if first == 3:
        row = lax.broadcasted_iota(jnp.int32, (16, 128), 0)
        for o in range(0, 8, 2):
            even = jnp.where(row == 0, sums[o : o + 1, :], 0.0)
            other = jnp.where(row == 0, sums[o + 1 : o + 2, :], 0.0)
            keep_out[12, o // 2] = jnp.where(odd, other, even)
            send_out[12, o // 2] = jnp.where(odd, even, other)


def split_row(tile):
    row = lax.broadcasted_iota(jnp.int32, tile.shape, 0)
    rest = tile[0:1] - tile[0:1].astype(BF).astype(F32)
    return jnp.where(row == 4, rest, tile)


def join_row(tile):
    row = lax.broadcasted_iota(jnp.int32, tile.shape, 0)
    whole = tile[0:1] + tile[4:5]
    return jnp.where(row == 0, whole, jnp.where(row == 4, 0.0, tile))


def feed_xy_body(place, keep, got, wo_keep, wo_got, *outs):
    size = keep.shape[1]
    for t in range(4):
        here = place[3] ^ t
        out = outs[t]
        for z in range(4):
            total = keep[4 * z + here] + got[4 * z + here]
            out[size * z : size * z + size - 1] = total[: size - 1].astype(out.dtype)
            out[size * z + size - 1] = (split_row(total[size - 1]) if t else total[size - 1]).astype(out.dtype)
        out[4 * size :] = (wo_keep[here] + wo_got[here]).astype(out.dtype)


def feed_z_body(place, keep, g1, g2, g3, out0, out1, out2, out3, wo_out):
    size = out0.shape[0]
    for t, out in enumerate((out0, out1, out2, out3)):
        at = pl.ds((place[4] ^ t) * size, size - 1)
        total = keep[at] + g1[at].astype(F32) + g2[at].astype(F32) + g3[at].astype(F32)
        out[: size - 1] = total.astype(out.dtype)
        at = (place[4] ^ t) * size + size - 1
        total = keep[at]
        for g in (g1, g2, g3):
            total = total + join_row(g[at].astype(F32))
        out[size - 1] = (split_row(total) if t else total).astype(out.dtype)
    at = slice(4 * size, 4 * size + 16)
    wo_out[...] = keep[at] + g1[at].astype(F32) + g2[at].astype(F32) + g3[at].astype(F32)


def square_xy_body(place, *refs):
    keeps, gots, outs = refs[:3], refs[3:6], refs[6:]
    for t in range(4):
        here = place[3] ^ t
        out = outs[t]
        for z in range(3):
            for p in range(4):
                call, at = ((0, 0), (1, 0), (1, 12), (2, 0))[p]
                total = keeps[call][at + 4 * z + here] + gots[call][at + 4 * z + here]
                out[16 * z + 4 * p : 16 * z + 4 * p + 4] = total.astype(out.dtype)
        total = keeps[2][12, here] + gots[2][12, here]
        out[48] = (split_row(total) if t else total).astype(out.dtype)


def square_z_body(place, keep, g1, g2, g3, wo, out0, out1, out2, out3, whole):
    for z in range(3):
        at = slice(16 * z, 16 * z + 16)
        whole[z, :16] = keep[at] + g1[at].astype(F32) + g2[at].astype(F32) + g3[at].astype(F32)
        whole[z + 1, 16] = jnp.zeros((16, 128), F32)
    whole[3, :16] = wo[...]
    total = keep[48]
    for g in (g1, g2, g3):
        total = total + join_row(g[48].astype(F32))
    whole[0, 16] = total
    for t, out in enumerate((out0, out1, out2, out3)):
        at = place[4] ^ t
        out[:16] = whole[at, :16].astype(out.dtype)
        out[16] = (split_row(whole[at, 16]) if t else whole[at, 16]).astype(out.dtype)


def last_body(keep, g1, g2, g3, out):
    size = keep.shape[0]
    at = slice(0, size - 1)
    out[at] = keep[at] + g1[at].astype(F32) + g2[at].astype(F32) + g3[at].astype(F32)
    total = keep[size - 1]
    for g in (g1, g2, g3):
        total = total + join_row(g[size - 1].astype(F32))
    out[size - 1] = total


def input_body(gm, *refs):
    w, out = refs[9:]
    for r in range(4):
        at = slice(256 * r, 256 * r + 256)
        total = gm[at, :]
        for index in range(3):
            total = total + nt(jnp.concatenate([ref[at, :] for ref in refs[index:9:3]], axis=1), square(w, index))
        out[at, :] = total


def to_columns(flat, rows):
    return flat.reshape(rows // 16, 16, -1, 128).transpose(2, 0, 1, 3).reshape(-1, 16, 128)


def from_columns(tiles, rows):
    return tiles.reshape(-1, rows // 16, 16, 128).transpose(1, 2, 0, 3).reshape(-1)


def swap(x, n, bit):
    return lax.ppermute(x, AXES, [(i, i ^ bit) for i in range(n)])


def small(body, outs, args, scratch=()):
    ins = [SMEM if arg.dtype == jnp.int32 else VMEM for arg in args]
    size = sum(arg.size for arg in args)
    return call(body, outs, ins, scratch, 2 * size, 6 * size, 16)(*args)


def blocks_of(*shape):
    return [(shape + (16, 128), F32)] + [(shape + (16, 128), BF)] * 3


def hop(parts, n, step):
    return [parts[0]] + [swap(part, n, step * t) for t, part in enumerate(parts) if t]


def tie(values, after):
    return lax.optimization_barrier((values, after))[0]


def along_z(own, n):
    return jnp.stack([own] + [swap(own, n, 8 * z) for z in (1, 2, 3)])


def along_xy(stack, n):
    return [stack] + [swap(stack, n, 2 * xy) for xy in (1, 2, 3)]


def across(chips, n):
    return chips + [swap(part, n, 1) for part in chips]


def own_pieces(attention, feedforward, biases, upper, parts):
    tail = jnp.pad(biases.reshape(1, 1, 128), ((0, 0), (0, 15), (0, 0)))
    own_a = jnp.concatenate([to_columns(attention, 4 * D // parts), tail], axis=0)
    up = to_columns(feedforward, 2 * D // parts)
    down = to_columns(feedforward, 2 * FF // parts)
    return own_a, jnp.where(upper, up, down)


def pieces_any(attention, feedforward, biases):
    full = [lax.all_gather(x, AXES, axis=0, tiled=True).reshape(PARTS, -1) for x in (attention, feedforward, biases)]
    upper = jnp.arange(PARTS) < PARTS // 2
    a, f = jax.vmap(lambda *x: own_pieces(*x, PARTS))(*full, upper)
    a, f = a.reshape((4, 4, 2) + a.shape[1:]), f.reshape((4, 4, 2) + f.shape[1:])

    return [[x[:, xy, c] for c in range(2) for xy in range(4)] for x in (a, f)]


def local(direct, tokens, cotangent, attention, feedforward, biases, gates, counts, lengths):
    me = lax.axis_index(AXES)
    n = PARTS
    *masks, x_t = call(
        prepare_body,
        [((2, ROWS, 128), BF), ((2, ROWS, 128), BF), ((D + 16, ROWS), BF)],
        [SMEM, SMEM, VMEM], [], 1 << 20, 3 << 20, 16,
    )(counts, lengths, tokens)
    if direct:
        own_a, own_f = own_pieces(attention, feedforward, biases, me < n // 2, n)
        stack_a, masks = lax.optimization_barrier((along_z(own_a, n), masks))
        stack_f = along_z(own_f, n)
        chips_a = along_xy(stack_a, n)
        ga_all = across(chips_a, n)
        chips_f = along_xy(stack_f, n)
        place = jnp.stack([me, me % 2, me, (me // 2) % 4, me // 8]).astype(jnp.int32)
    else:
        ga_all, gf_all = pieces_any(attention, feedforward, biases)
        place = jnp.zeros((5,), jnp.int32)
    row = (ROWS, D)
    q, k, v, w, bias = call(
        project_body,
        [((H, ROWS, 128), BF)] * 2 + [(row, BF), ((PARTS, A_TILES, 16, 128), BF), ((1, 8 * D), F32)],
        [SMEM] + [VMEM] * 11, [], 2 << 30, 10 << 20, 20,
    )(place, tokens, *masks, *ga_all)
    ctx, ctx_t, lse = call(
        attend_body,
        [(row, BF), ((D, ROWS), BF), ((8, ROWS), F32)],
        [VMEM] * 3,
        [((128, ROWS), BF), ((128, ROWS), F32)] + [((ROWS, 256), F32)] * 2 + [((ROWS, 256), BF)] * 2,
        12 << 30, 4 << 20, 20,
    )(q, k, v)
    if direct:
        chips_f, ctx = lax.optimization_barrier((chips_f, ctx))
        gf_all = across(chips_f, n)
    layer, gm, gctx, ff_keep, ff_send, wo_keep, wo_send = call(
        feed_body,
        [(row, BF, ANY), (row, F32, ANY), (row, BF, ANY)] + [((n // 2, G_TILES, 16, 128), F32, ANY)] * 2
        + [((4, 16, 16, 128), F32, ANY)] * 2,
        [SMEM, SMEM] + [VMEM] * 14,
        [((PARTS, F_TILES, 16, 128), BF), ((D + 16, ROWS), BF), ((D + 16, ROWS), BF), (row, BF), (row, BF),
         ((FF + 16, ROWS), BF), ((ROWS, FF), BF)]
        + [((256, D), F32)] * 4 + [((256, FF), BF)] + [((256, D), F32)] * 2 + [((1, 8 * D), F32)]
        + [(row, BF), (row, F32), (row, BF), ((2, n // 2, G_TILES, 16, 128), F32), ((2, 4, 16, 16, 128), F32), DMA((16,))],
        16 << 30, 30 << 20, 46,
    )(place, gates, tokens, cotangent, ctx, ctx_t, w, bias, *gf_all)

    def back(first, pairs, q, before):
        last = first == 3
        return call(
            partial(back_body, first),
            [((ROWS, 128 * pairs), BF)] * 3 + [((12 * pairs + last, 4, 16, 128), F32)] * 2
            + ([] if last else [((8, 128), F32)]),
            [SMEM] + [VMEM] * (7 if first else 6),
            [((2, 128, ROWS), BF), ((128, ROWS), F32), ((ROWS, 128), F32), ((ROWS, 128), F32)]
            + [((ROWS, 256), F32)] * 4 + [((ROWS, 256), BF)] * 4 + ([((8, 128), F32)] if last else []),
            1000, 1000, 28,
        )(place, q, k, v, gctx, lse, x_t, *([before] if first else []))

    barrier = lax.optimization_barrier
    if direct:
        got, wo_got = swap(ff_send, n, 1), swap(wo_send, n, 1)
    *parts, keep, send, before = back(0, 1, q, None)
    grads, keeps, sends, gots = parts, [keep], [send], []
    if direct:
        got, wo_got, grads, sends = barrier((got, wo_got, grads, sends))
        parts = small(feed_xy_body, blocks_of(4 * G_TILES + 16), (place, ff_keep, got, wo_keep, wo_got))
        q, parts = barrier((q, parts))
        ff_got = hop(parts, n, 2)
        gots = [swap(sends[0], n, 1)]
    for first in (1, 3):
        *parts, keep, send = back(first, 2 if first == 1 else 1, q, before)
        if first == 1:
            *parts, keep, send, before = *parts, keep, send
        if direct:
            gots.append(swap(send, n, 1))
        grads, keeps, sends = grads + parts, keeps + [keep], sends + [send]
    (input_grad,) = call(
        input_body, [(row, F32)], [VMEM] * 11, [], 1000, 1000, 24
    )(gm, *grads, w)
    if direct:
        gots, input_grad, ff_got = barrier((gots, input_grad, ff_got))
        parts = small(square_xy_body, blocks_of(49), (place, *keeps, *gots))
        ff_got, parts = barrier((ff_got, parts))
        got = hop(parts, n, 2)
        *ff_parts, wo = small(feed_z_body, blocks_of(G_TILES) + [((16, 16, 128), F32)], (place, *ff_got))
        ff_got = hop(ff_parts, n, 8)
        got, ff_parts = barrier((got, ff_parts))
    if direct:
        parts = small(square_z_body, blocks_of(17), (place, *got, wo), [((4, 17, 16, 128), F32)])
        got = hop(parts, n, 8)
        ff_got, parts = lax.optimization_barrier((ff_got, parts))
        (ff_shard,) = small(last_body, [((G_TILES, 16, 128), F32)], ff_got)
        (att_shard,) = small(last_body, [((17, 16, 128), F32)], got)
        ff_grad = jnp.where(
            me < n // 2, from_columns(ff_shard[:F_TILES], 2 * D // n), from_columns(ff_shard[:F_TILES], 2 * FF // n)
        )
        att_grad = from_columns(att_shard[:16], 4 * D // n)
        tail = ff_shard[F_TILES]
        bias_grad = jnp.where(me < 8, att_shard[16][0], tail[0])
        gate_grad = jnp.sum((tail[1] + tail[2] + tail[3])[: 2 * n].reshape(n, 2), axis=0)
        return layer, input_grad, att_grad, ff_grad, bias_grad, gate_grad

    def owners(keep, send):
        return jnp.stack([keep, send], axis=1).reshape((-1,) + keep.shape[1:])

    def reduce(flat):
        return lax.psum_scatter(flat.reshape(-1), AXES, scatter_dimension=0, tiled=True)

    both = owners(ff_keep, ff_send)
    up = jax.vmap(lambda t: from_columns(t, 2 * D // n))(both[: n // 2, :F_TILES]).reshape(-1)
    down = jax.vmap(lambda t: from_columns(t, 2 * FF // n))(both[n // 2 :, :F_TILES]).reshape(-1)
    ff_grad = reduce(jnp.concatenate([up, down]))
    tail = both[0, F_TILES]
    gate_grad = lax.psum((tail[1] + tail[2] + tail[3])[:2], AXES)
    bias_grad = jnp.concatenate([owners(keeps[2][12], sends[2][12])[:, 0], both[8:, F_TILES, 0]])
    both = jnp.stack([jnp.concatenate([x[: len(x) // 12 * 12] for x in xs]).reshape(4, 12, 4, 16, 128) for xs in (keeps, sends)], axis=2).reshape(4, 24, 4, 16, 128).transpose(1, 0, 2, 3, 4)
    both = jnp.concatenate([both.reshape(24, 16, 16, 128), owners(wo_keep, wo_send)])
    att_grad = jax.vmap(lambda t: from_columns(t, 4 * D // n))(both)
    return layer, input_grad, reduce(att_grad), ff_grad, reduce(bias_grad), gate_grad


def solution(mesh):
    direct = dict(mesh.shape) == {"dp": 8, "fsdp": 4}
    both = P(AXES)
    rows = P(AXES, None)
    return jax.shard_map(
        partial(local, direct),
        mesh=mesh,
        in_specs=(rows, rows, both, both, both, P(), rows, rows),
        out_specs=(rows, rows, both, both, both, P()),
        check_vma=False,
    )
```

```python
from functools import partial

import jax
import jax.numpy as jnp
from jax import lax
from jax.experimental import pallas as pl
from jax.experimental.pallas import tpu as pltpu
from jax.sharding import PartitionSpec as P

D = 512
H = 8
HD = 64
FF = 2048
ROWS = 1024
SLOTS = 8
SHORT = 128
MID = 512
LONG = 1024
AXES = ("dp", "fsdp")
PARTS = 32
A_TILES = 17
F_TILES = 32
G_TILES = 33
BF = jnp.bfloat16
F32 = jnp.float32
CHUNK = 64
SHARE = 6 * 64
BIG = 512
VMEM = pl.BlockSpec(memory_space=pltpu.VMEM)
SMEM = pl.BlockSpec(memory_space=pltpu.SMEM)
ANY = pl.BlockSpec(memory_space=pl.ANY)
DMA = pltpu.SemaphoreType.DMA


def nn(a, b):
    return lax.dot_general(a, b, (((1,), (0,)), ((), ())), preferred_element_type=F32)


def nt(a, b):
    return lax.dot_general(a, b, (((1,), (1,)), ((), ())), preferred_element_type=F32)


def call(body, outs, ins, scratch, flops, moved, limit, grid=None):
    return pl.pallas_call(
        body,
        out_shape=[jax.ShapeDtypeStruct(o[0], o[1]) for o in outs],
        grid=grid or (),
        in_specs=ins,
        out_specs=[o[2] if len(o) > 2 else VMEM for o in outs],
        scratch_shapes=[pltpu.VMEM(*s) if isinstance(s, tuple) else s for s in scratch],
        compiler_params=pltpu.CompilerParams(vmem_limit_bytes=limit << 20),
        cost_estimate=pl.CostEstimate(flops=flops, bytes_accessed=moved, transcendentals=0),
    )


def slot_masks(counts, lengths, keys_out, rows_out):
    lane = lax.broadcasted_iota(jnp.int32, (1, 128), 1)
    slot = lane & 63
    longs, mids, shorts = counts[0, 2], counts[0, 1], counts[0, 0]
    in_long = jnp.minimum(slot, longs)
    in_mid = jnp.clip(slot - longs, 0, mids)
    in_short = jnp.clip(slot - longs - mids, 0, shorts)
    start = in_long * LONG + in_mid * MID + in_short * SHORT
    size = jnp.where(
        slot < longs,
        LONG,
        jnp.where(slot < longs + mids, MID, jnp.where(slot < longs + mids + shorts, SHORT, 0)),
    )
    valid = jnp.zeros((1, 128), jnp.int32)
    for s in range(SLOTS):
        valid = jnp.where(slot == s, lengths[0, s], valid)
    row = lax.broadcasted_iota(jnp.int32, (ROWS, 128), 0)
    member = (row >= start) & (row < start + size)
    usable = (row >= start) & (row < start + valid)
    for parity in range(2):
        here = (slot < SLOTS) & ((lane >= 64) if parity == 0 else (lane < 64))
        rows_out[parity] = jnp.where(here & member, 1.0, 0.0).astype(BF)
        keys_out[parity] = jnp.where(here & jnp.logical_not(usable), -1e30, 0.0).astype(BF)


def prepare_body(counts, lengths, tok, keys_mask, rows_mask, x_t):
    slot_masks(counts, lengths, keys_mask, rows_mask)
    x_t[:D] = tok[...].T
    x_t[D:] = jnp.ones((16, ROWS), BF)


def half_of(parity, shape):
    lane = lax.broadcasted_iota(jnp.int32, shape, len(shape) - 1)
    return (lane < 64) if parity == 0 else (lane >= 64)


def assemble(pieces, dest, me):
    for c in range(2):
        for xy in range(4):
            for z in range(4):
                dest[(8 * z + 2 * xy + c) ^ me] = pieces[4 * c + xy][z]


def columns(ref, owners, tiles, each):
    parts = []
    for t in range(tiles.start, tiles.stop, each):
        part = ref[owners, t : t + each]
        parts.append(part.reshape(part.shape[0] * each * 16, 128))
    return jnp.concatenate(parts, axis=1)


def square(ref, index):
    return columns(ref, slice(8 * index, 8 * index + 8), slice(0, 16), 4)


def project_body(place, tok, keys_mask, rows_mask, *refs):
    pieces, (q_out, k_out, v_out, w_out, bias_out) = refs[:8], refs[8:]
    assemble(pieces, w_out, place[0])
    for o in range(PARTS):
        bias_out[0:1, 128 * o : 128 * o + 128] = w_out[o, A_TILES - 1].astype(F32)[0:1]
    for r in range(4):
        at = slice(256 * r, 256 * r + 256)
        x = tok[at, :]
        q = (nn(x, square(w_out, 0)) + bias_out[0:1, 0:D]).astype(BF)
        q = (q.astype(F32) * 0.125).astype(BF)
        k = nn(x, square(w_out, 1)).astype(BF)
        v_out[at, :] = (nn(x, square(w_out, 2)) + bias_out[0:1, D : 2 * D]).astype(BF)
        for h in range(H):
            mine = half_of(h % 2, (256, 128))
            lanes = slice(h // 2 * 128, h // 2 * 128 + 128)
            q_out[h, at] = jnp.where(mine, q[:, lanes], rows_mask[h % 2, at])
            k_out[h, at] = jnp.where(mine, k[:, lanes], keys_mask[h % 2, at])


def attend_body(q_all, k_all, v_all, ctx_out, ctx_t_out, lse_out, values_t, ctx_t, s0, s1, p0, p1):
    def pair(p, _):
        attend_pair(
            p, q_all.at[pl.ds(2 * p, 2)], k_all.at[pl.ds(2 * p, 2)], v_all, ctx_out, ctx_t_out, lse_out, values_t, ctx_t,
            s0, s1, p0, p1,
        )
        return 0

    lax.fori_loop(0, 4, pair, 0)
    ctx_t_out[D:] = jnp.ones((16, ROWS), BF)


def attend_pair(p, q_in, k_in, v_all, ctx_out, ctx_t_out, lse_out, values_t, ctx_t, s0, s1, p0, p1):
    lanes = pl.ds(pl.multiple_of(p * 128, 128), 128)
    scores, probs = (s0, s1), (p0, p1)
    values_t[...] = v_all[:, lanes].T
    steps = [(parity, r) for parity in range(2) for r in range(4)]

    def score(i):
        parity, r = steps[i]

        def part(c):
            scores[i % 2][c : c + 256] = nt(k_in[parity, c : c + 256], q_in[parity, r * 256 : r * 256 + 256])

        return [partial(part, c) for c in range(0, ROWS, 256)]

    def collect(i):
        parity, r = steps[i]
        rows = slice(64 * parity, 64 * parity + 64)
        total = []

        def part(c):
            total.append(nn(values_t[rows, c : c + 256], probs[i % 2][c : c + 256]))
            if c == ROWS - 256:
                ctx_t[rows, r * 256 : r * 256 + 256] = (total[0] + total[1]) + (total[2] + total[3])

        return [partial(part, c) for c in range(0, ROWS, 256)]

    def soften(i):
        parity, r = steps[i]
        s, out = scores[i % 2], probs[i % 2]
        state = {}

        def peak(c):
            part = jnp.max(s[c : c + CHUNK].reshape(-1, 8, 256), axis=0)
            state["top"] = jnp.maximum(state["top"], part) if c else part
            if c == ROWS - CHUNK:
                state["top"] = jnp.max(state["top"], axis=0, keepdims=True)

        def power(c):
            e = jnp.exp(s[c : c + CHUNK] - state["top"])
            s[c : c + CHUNK] = e
            part = jnp.sum(e.reshape(-1, 8, 256), axis=0)
            state["mass"] = state["mass"] + part if c else part
            if c == ROWS - CHUNK:
                mass = jnp.sum(state["mass"], axis=0, keepdims=True)
                lse_out[pl.ds(2 * p + parity, 1), r * 256 : r * 256 + 256] = state["top"] + jnp.log(mass)
                state["share"] = 1.0 / mass

        def share(c):
            out[c : c + CHUNK] = (s[c : c + CHUNK] * state["share"]).astype(BF)

        at = range(0, ROWS, CHUNK)
        return [(1, partial(peak, c)) for c in at] + [(3, partial(power, c)) for c in at] + [
            (1.5, partial(share, c)) for c in at
        ]

    for task in score(0):
        task()
    for i in range(9):
        later = (score(i + 1) if i < 7 else []) + (collect(i - 1) if i else [])
        mix(soften(i) if i < 8 else [], later)
    low = ctx_t[...].astype(BF)
    ctx_t_out[lanes, :] = low
    ctx_out[:, lanes] = low.T


def mix(vector, matrix):
    whole = sum(weight for weight, _ in vector) or 1
    done, given = 0, 0
    for weight, task in vector:
        while given < len(matrix) and given * whole <= done * len(matrix):
            matrix[given]()
            given += 1
        task()
        done += weight
    for task in matrix[given:]:
        task()


def feed_body(place, gates, tok, cot, ctx, ctx_t, w_in, bias, *refs):
    pieces, refs = refs[:8], refs[8:]
    (layer_out, gm, gctx, keep_out, send_out, wo_keep, wo_send) = refs[:7]
    (w, low_t, gbr, gs_all, active_t, gh_all, v0, v1, b0, b1, active, second, gmid, sums) = refs[7:21]
    (layer, both, sems) = refs[21:]
    values, backs = (v0, v1), (b0, b1)
    wo = w_in.at[24:32]
    assemble(pieces, w, place[0])

    def rows_of(r):
        return pl.ds(pl.multiple_of(r * 256, 256), 256)

    ga, gf = gates[0], gates[1]
    c1 = 0.7978845608028654
    c2 = 0.044715
    ones = jnp.ones((16, ROWS), BF)
    low_t[D:] = ones
    active_t[FF:] = ones

    def w_up(j):
        return columns(w, slice(0, 16), slice(8 * j, 8 * j + 8), 2)

    def w_down(j):
        return columns(w, slice(16 + 4 * j, 20 + 4 * j), slice(0, 32), 8)

    def rows(r, carry):
        attend_sum, feed_sum = carry
        at = rows_of(r)
        br = nn(ctx[at, :], square(wo, 0)) + bias[0:1, 2 * D : 3 * D]
        middle = tok[at, :].astype(F32) + ga * br
        low = middle.astype(BF)
        low_t[:D, at] = low.T
        ct = cot[at, :].astype(F32)
        gs = (gf * ct).astype(BF)
        gs_all[at, :] = gs

        def first(j):
            up, down = w_up(j), w_down(j)

            def value(n):
                values[j % 2][:, n : n + 256] = nn(low, up[:, n : n + 256])

            def back(n):
                backs[j % 2][:, n : n + 256] = nt(gs, down[n : n + 256])

            return [partial(f, n) for n in (0, 256) for f in (value, back)]

        def bend(j):
            def part(c):
                lines = slice(c, c + 32)
                cols = slice(4 * D + 512 * j, 4 * D + 512 * j + 512)
                v = values[j % 2][lines] + bias[0:1, cols]
                v2 = v * v
                t = jnp.tanh(v * (c1 + (c1 * c2) * v2))
                half = 0.5 + 0.5 * t
                act = v * half
                slope = half * (1.0 + (v - act) * (2.0 * c1 + (6.0 * c1 * c2) * v2))
                active[lines, 512 * j : 512 * j + 512] = act.astype(BF)
                gh_all[pl.ds(r * 256 + c, 32), 512 * j : 512 * j + 512] = (slope * backs[j % 2][lines]).astype(BF)

            return [(1, partial(part, c)) for c in range(0, 256, 32)]

        def then(j):
            up, down = w_up(j), w_down(j)
            cols = slice(512 * j, 512 * j + 512)

            def forward(n):
                val = nn(active[:, cols], down[:, n : n + 256])
                second[:, n : n + 256] = second[:, n : n + 256] + val if j else val

            def backward(n):
                val = nt(gh_all[at, cols], up[n : n + 256])
                gmid[:, n : n + 256] = gmid[:, n : n + 256] + val if j else val

            def turn():
                active_t[cols, at] = active[:, cols].T

            return [turn] + [partial(f, n) for n in (0, 256) for f in (forward, backward)]

        for task in first(0):
            task()
        for j in range(5):
            mix(bend(j) if j < 4 else [], (first(j + 1) if j < 3 else []) + (then(j - 1) if j else []))
        out = second[...] + bias[0:1, 3 * D : 4 * D]
        layer[at, :] = (middle + gf * out).astype(BF)
        grad = ct + gmid[...]
        gm[at, :] = grad
        gb = (ga * grad).astype(BF)
        gbr[at, :] = gb
        gctx[at, :] = nt(gb, square(wo, 0)).astype(BF)
        pltpu.make_async_copy(layer.at[at], layer_out.at[at], sems.at[0]).start()
        attend_sum = attend_sum + jnp.sum(br * grad, axis=0, keepdims=True)
        feed_sum = feed_sum + jnp.sum(out * ct, axis=0, keepdims=True)
        return attend_sum, feed_sum

    zero = jnp.zeros((1, D), F32)
    attend_sum, feed_sum = lax.fori_loop(0, 4, rows, (zero, zero))
    odd = place[1]

    def send(slots, sem):
        copies = [
            pltpu.make_async_copy(both.at[0, slots], keep_out.at[slots], sems.at[sem]),
            pltpu.make_async_copy(both.at[1, slots], send_out.at[slots], sems.at[sem + 1]),
        ]
        for copy in copies:
            copy.start()
        return copies

    for j in range(4):
        val = nn(low_t[...], gh_all[:, 512 * j : 512 * j + 512])
        sums[0:1, 4 * D + 512 * j : 4 * D + 512 * j + 512] = val[D : D + 1]
        for o in range(16):
            for jj in range(4):
                for i in range(2):
                    top, col = 32 * o + 16 * i, slice(128 * jj, 128 * jj + 128)
                    both[(o % 2) ^ odd, o // 2, 2 * (4 * j + jj) + i] = val[top : top + 16, col]
    val = nn(ctx_t[...], gbr[...])
    sums[0:1, 2 * D : 3 * D] = val[D : D + 1]
    for o in range(0, 8, 2):
        for j in range(4):
            for i in range(4):
                top, col = 64 * o + 16 * i, slice(128 * j, 128 * j + 128)
                even, other = val[top : top + 16, col], val[top + 64 : top + 80, col]
                wo_keep[o // 2, 4 * j + i] = jnp.where(odd == 1, other, even)
                wo_send[o // 2, 4 * j + i] = jnp.where(odd == 1, even, other)
    copies = []
    lane = lax.broadcasted_iota(jnp.int32, (1, 128), 1)
    gate = jnp.where(lane == 2 * place[2], jnp.sum(attend_sum), 0.0)
    gate = jnp.where(lane == 2 * place[2] + 1, jnp.sum(feed_sum), gate)
    high = gate.astype(BF).astype(F32)
    rest = gate - high
    mid = rest.astype(BF).astype(F32)
    last = (rest - mid).astype(BF).astype(F32)
    row = lax.broadcasted_iota(jnp.int32, (16, 128), 0)
    base = jnp.where(row == 1, high, jnp.where(row == 2, mid, jnp.where(row == 3, last, 0.0)))
    sums[0:1, 0 : 2 * D] = jnp.zeros((1, 2 * D), F32)

    def tail(o):
        both[(o % 2) ^ odd, o // 2, G_TILES - 1] = jnp.where(row == 0, sums[0:1, 128 * o : 128 * o + 128], base)

    for j in (3, 2, 1, 0):
        val = nn(active_t[512 * j : 512 * j + (528 if j == 3 else 512)], gs_all[...])
        if j == 3:
            sums[0:1, 3 * D : 4 * D] = val[D : D + 1]
            for o in range(16):
                tail(o)
            copies += send(pl.ds(0, 8), 5)
        for o in range(4):
            tail(16 + 4 * j + o)
            for jj in range(4):
                for i in range(8):
                    top, col = 128 * o + 16 * i, slice(128 * jj, 128 * jj + 128)
                    both[(o % 2) ^ odd, 8 + 2 * j + o // 2, 8 * jj + i] = val[top : top + 16, col]
        copies += send(pl.ds(8 + 2 * j, 2), 7 + 2 * j)
    pltpu.make_async_copy(layer, layer_out, sems.at[0]).wait()
    for copy in copies:
        copy.wait()


def back_body(first, place, q_all, k_all, v_all, g_all, lse, x_t, *refs):
    if first:
        before, *refs = refs
    dq_out, dk_out, dv_out, *refs = refs
    if first:
        keeps, sends, refs, sums = refs[:2], refs[2:4], refs[4:-1], refs[-1]
    else:
        keep, send, sums, *refs = refs
        keeps, sends = [(ref.at[:SHARE], ref.at[SHARE:]) for ref in (keep, send)]
    k_t, dq_t, dk_acc, dv_acc, s0, s1, g0, g1, p0, p1, d0, d1 = refs
    scores, grads, probs, diffs = (s0, s1), (g0, g1), (p0, p1), (d0, d1)
    steps = [(parity, r) for parity in range(2) for r in range(4)]
    odd = place[1] == 1
    sums[...] = before[...] if first else jnp.zeros_like(sums)

    def pair(turn, _):
        p = turn + first
        lanes = pl.ds(pl.multiple_of(p * 128, 128), 128)
        out = pl.ds(pl.multiple_of(turn * 128, 128), 128)
        q_in, k_in = q_all.at[pl.ds(2 * p, 2)], k_all.at[pl.ds(2 * p, 2)]
        for parity in range(2):
            k_t[parity] = k_in[parity].T

        def mine(block, i):
            return jnp.where(half_of(steps[i][0], (256, 128)), block, jnp.zeros_like(block))

        def score(i):
            parity, r = steps[i]
            qa = q_in[parity, r * 256 : r * 256 + 256]
            ga = mine(g_all[r * 256 : r * 256 + 256, lanes], i)

            def part(c):
                scores[i % 2][c : c + BIG] = nt(k_in[parity, c : c + BIG], qa)

            def grad(c):
                grads[i % 2][c : c + BIG] = nt(v_all[c : c + BIG, lanes], ga)

            return [task for c in range(0, ROWS, BIG) for task in (partial(part, c), partial(grad, c))]

        def soften(i):
            parity, r = steps[i]
            s, g, out, diff = scores[i % 2], grads[i % 2], probs[i % 2], diffs[i % 2]
            logs = lse[pl.ds(2 * p + parity, 1), r * 256 : r * 256 + 256]
            state = {}

            def power(c):
                e = jnp.exp(s[c : c + CHUNK] - logs)
                s[c : c + CHUNK] = e
                out[c : c + CHUNK] = e.astype(BF)
                part = jnp.sum((e * g[c : c + CHUNK]).reshape(-1, 8, 256), axis=0)
                state["inner"] = state["inner"] + part if c else part
                if c == ROWS - CHUNK:
                    state["inner"] = jnp.sum(state["inner"], axis=0, keepdims=True)

            def minus(c):
                diff[c : c + CHUNK] = (s[c : c + CHUNK] * (g[c : c + CHUNK] - state["inner"])).astype(BF)

            at = range(0, ROWS, CHUNK)
            return [(5.5, partial(power, c)) for c in at] + [(2.5, partial(minus, c)) for c in at]

        def collect(i):
            parity, r = steps[i]
            rows = slice(64 * parity, 64 * parity + 64)
            at = slice(r * 256, r * 256 + 256)
            qz, gz = mine(q_in[parity, at], i), mine(g_all[at, lanes], i)
            total = []

            def part(c):
                total.append(nn(k_t[parity, rows, c : c + 256], diffs[i % 2][c : c + 256]))
                if c == ROWS - 256:
                    dq_t[rows, r * 256 : r * 256 + 256] = ((total[0] + total[1]) + (total[2] + total[3])) * 0.125

            def add(acc, ref, z, c):
                val = nn(ref[c : c + BIG], z)
                acc[c : c + BIG] = acc[c : c + BIG] + val if i else val

            tasks = []
            for c in range(0, ROWS, 256):
                if c % BIG == 0:
                    tasks += [partial(add, dv_acc, probs[i % 2], gz, c), partial(add, dk_acc, diffs[i % 2], qz, c)]
                tasks += [partial(part, c)]
            return tasks

        for task in score(0):
            task()
        for i in range(9):
            later = (score(i + 1) if i < 7 else []) + (collect(i - 1) if i else [])
            mix(soften(i) if i < 8 else [], later)
        dq = dq_t[...].astype(BF).T
        dk = dk_acc[...].astype(BF)
        dv = dv_acc[...].astype(BF)
        dq_out[:, out] = dq
        dk_out[:, out] = dk
        dv_out[:, out] = dv
        val = nn(x_t[...], jnp.concatenate([dq, dk, dv, dv], axis=1))
        sums[pl.ds(p, 1), :] = val[D : D + 1, 0:128]
        sums[pl.ds(4 + p, 1), :] = val[D : D + 1, 256:384]
        for index in range(3):
            for o in range(0, 8, 2):
                for i in range(4):
                    col, top = slice(128 * index, 128 * index + 128), 64 * o + 16 * i
                    even, other = val[top : top + 16, col], val[top + 64 : top + 80, col]
                    part, at = part_of(index, o // 2)
                    at = pl.ds(pl.multiple_of(SHARE * turn + 64 * at + 16 * i, 16), 16)
                    keeps[part][at] = jnp.where(odd, other, even)
                    sends[part][at] = jnp.where(odd, even, other)
        return 0

    lax.fori_loop(0, dq_out.shape[1] // 128, pair, 0)
    if first:
        row = lax.broadcasted_iota(jnp.int32, (8, 128), 0)
        even, other = jnp.zeros((8, 128), F32), jnp.zeros((8, 128), F32)
        for o in range(0, 8, 2):
            even = jnp.where(row == o // 2, sums[o : o + 1, :], even)
            other = jnp.where(row == o // 2, sums[o + 1 : o + 2, :], other)
        keeps[1][3 * SHARE :] = jnp.where(odd, other, even)
        sends[1][3 * SHARE :] = jnp.where(odd, even, other)


def part_of(index, slot):
    return (index, slot) if index < 2 else (slot // 2, 4 + slot % 2)


def split_row(tile):
    row = lax.broadcasted_iota(jnp.int32, tile.shape, 0)
    rest = tile[0:1] - tile[0:1].astype(BF).astype(F32)
    return jnp.where(row == 4, rest, tile)


def join_row(tile):
    row = lax.broadcasted_iota(jnp.int32, tile.shape, 0)
    whole = tile[0:1] + tile[4:5]
    return jnp.where(row == 0, whole, jnp.where(row == 4, 0.0, tile))


def feed_xy_body(place, keep, got, wo_keep, wo_got, *outs):
    size = keep.shape[1]
    for t in range(4):
        here = place[3] ^ t
        out = outs[t]
        for z in range(4):
            total = keep[4 * z + here] + got[4 * z + here]
            out[size * z : size * z + size - 1] = total[: size - 1].astype(out.dtype)
            out[size * z + size - 1] = (split_row(total[size - 1]) if t else total[size - 1]).astype(out.dtype)
        out[4 * size :] = (wo_keep[here] + wo_got[here]).astype(out.dtype)


def feed_z_body(place, keep, g1, g2, g3, out0, out1, out2, out3, wo_out):
    size = out0.shape[0]
    for t, out in enumerate((out0, out1, out2, out3)):
        at = pl.ds((place[4] ^ t) * size, size - 1)
        total = keep[at] + g1[at].astype(F32) + g2[at].astype(F32) + g3[at].astype(F32)
        out[: size - 1] = total.astype(out.dtype)
        at = (place[4] ^ t) * size + size - 1
        total = keep[at]
        for g in (g1, g2, g3):
            total = total + join_row(g[at].astype(F32))
        out[size - 1] = (split_row(total) if t else total).astype(out.dtype)
    at = slice(4 * size, 4 * size + 16)
    wo_out[...] = keep[at] + g1[at].astype(F32) + g2[at].astype(F32) + g3[at].astype(F32)


def square_xy_body(place, first, first_got, a, b, a_got, b_got, *outs):
    def added(p, part, at):
        rows = pl.ds(pl.multiple_of(at * 64, 64), 64)
        if p == 0:
            rows = pl.ds(pl.multiple_of(SHARE * part + at * 64, 64), 64)
            return first[rows] + first_got[rows]
        rows = pl.ds(pl.multiple_of(SHARE * (p - 1) + at * 64, 64), 64)
        return ((a, b)[part])[rows] + ((a_got, b_got)[part])[rows]

    for t in range(4):
        here = place[3] ^ t
        out = outs[t]
        for z in range(3):
            for p in range(4):
                if z < 2:
                    total = added(p, z, here)
                else:
                    total = jnp.where(here < 2, added(p, 0, 4 + here % 2), added(p, 1, 4 + here % 2))
                out[16 * z + 4 * p : 16 * z + 4 * p + 4] = total.reshape(4, 16, 128).astype(out.dtype)
        row = lax.broadcasted_iota(jnp.int32, (16, 128), 0)
        total = b[pl.ds(3 * SHARE + here, 1)] + b_got[pl.ds(3 * SHARE + here, 1)]
        total = jnp.where(row == 0, total, 0.0)
        out[48] = (split_row(total) if t else total).astype(out.dtype)


def square_z_body(place, keep, g1, g2, g3, wo, out0, out1, out2, out3, whole):
    for z in range(3):
        at = slice(16 * z, 16 * z + 16)
        whole[z, :16] = keep[at] + g1[at].astype(F32) + g2[at].astype(F32) + g3[at].astype(F32)
        whole[z + 1, 16] = jnp.zeros((16, 128), F32)
    whole[3, :16] = wo[...]
    total = keep[48]
    for g in (g1, g2, g3):
        total = total + join_row(g[48].astype(F32))
    whole[0, 16] = total
    for t, out in enumerate((out0, out1, out2, out3)):
        at = place[4] ^ t
        out[:16] = whole[at, :16].astype(out.dtype)
        out[16] = (split_row(whole[at, 16]) if t else whole[at, 16]).astype(out.dtype)


def input_body(gm, *refs):
    w, out = refs[6:]
    for r in range(4):
        at = slice(256 * r, 256 * r + 256)
        total = gm[at, :]
        for index in range(3):
            total = total + nt(jnp.concatenate([ref[at, :] for ref in refs[index:6:3]], axis=1), square(w, index))
        out[at, :] = total


def to_columns(flat, rows):
    return flat.reshape(rows // 16, 16, -1, 128).transpose(2, 0, 1, 3).reshape(-1, 16, 128)


def from_columns(tiles, rows):
    return tiles.reshape(-1, rows // 16, 16, 128).transpose(1, 2, 0, 3).reshape(-1)


def swap(x, n, bit):
    return lax.ppermute(x, AXES, [(i, i ^ bit) for i in range(n)])


def small(body, outs, args, scratch=()):
    ins = [SMEM if arg.dtype == jnp.int32 else VMEM for arg in args]
    size = sum(arg.size for arg in args)
    return call(body, outs, ins, scratch, 2 * size, 6 * size, 16)(*args)


def blocks_of(*shape):
    return [(shape + (16, 128), F32)] + [(shape + (16, 128), BF)] * 3


def hop(parts, n, step):
    return [parts[0]] + [swap(part, n, step * t) for t, part in enumerate(parts) if t]


def tie(values, after):
    return lax.optimization_barrier((values, after))[0]


def along_z(own, n):
    return jnp.stack([own] + [swap(own, n, 8 * z) for z in (1, 2, 3)])


def along_xy(stack, n):
    return [stack] + [swap(stack, n, 2 * xy) for xy in (1, 2, 3)]


def across(chips, n):
    return chips + [swap(part, n, 1) for part in chips]


def pack_square_body(flat, biases, out, wide):
    wide[...] = flat[...].astype(F32)
    for j in range(4):
        for i in range(4):
            out[4 * j + i] = wide[pl.ds(64 * i + j, 16, stride=4), :].astype(BF)
    row = lax.broadcasted_iota(jnp.int32, (16, 128), 0)
    out[16] = jnp.where(row == 0, biases[...].astype(F32), 0.0).astype(BF)


def pack_feed_body(place, flat, out, wide):
    wide[...] = flat[...].astype(F32)

    @pl.when(place[0] < PARTS // 2)
    def _():
        for j in range(16):
            for i in range(2):
                out[2 * j + i] = wide[pl.ds(256 * i + j, 16, stride=16), :].astype(BF)

    @pl.when(place[0] >= PARTS // 2)
    def _():
        for j in range(4):
            for i in range(8):
                out[8 * j + i] = wide[pl.ds(64 * i + j, 16, stride=4), :].astype(BF)


def finish_body(place, keep_f, f1, f2, f3, keep_a, a1, a2, a3, att, ff, bias, gate):
    def added(keep, gots, at):
        total = keep[at]
        for g in gots:
            total = total + g[at].astype(F32)
        return total

    def added_tail(keep, gots, at):
        total = keep[at]
        for g in gots:
            total = total + join_row(g[at].astype(F32))
        return total

    for j in range(4):
        for i in range(4):
            att[pl.ds(64 * i + j, 16, stride=4), :] = added(keep_a, (a1, a2, a3), 4 * j + i)
    gots = (f1, f2, f3)

    @pl.when(place[0] < PARTS // 2)
    def _():
        for j in range(16):
            for i in range(2):
                ff[pl.ds(256 * i + j, 16, stride=16), :] = added(keep_f, gots, 2 * j + i)

    @pl.when(place[0] >= PARTS // 2)
    def _():
        for j in range(4):
            for i in range(8):
                ff[pl.ds(64 * i + j, 16, stride=4), :] = added(keep_f, gots, 8 * j + i)

    tail = added_tail(keep_f, gots, F_TILES)
    own = added_tail(keep_a, (a1, a2, a3), 16)
    bias[...] = jnp.where(place[0] < 8, own[0:1], tail[0:1])
    gates = tail[1:2] + tail[2:3] + tail[3:4]
    lane = lax.broadcasted_iota(jnp.int32, (1, 128), 1)
    for g in range(2):
        gate[g] = jnp.sum(jnp.where((lane < 2 * PARTS) & (lane % 2 == g), gates, 0.0))


def own_pieces(attention, feedforward, biases, upper, parts):
    tail = jnp.pad(biases.reshape(1, 1, 128), ((0, 0), (0, 15), (0, 0)))
    own_a = jnp.concatenate([to_columns(attention, 4 * D // parts), tail], axis=0)
    up = to_columns(feedforward, 2 * D // parts)
    down = to_columns(feedforward, 2 * FF // parts)
    return own_a, jnp.where(upper, up, down)


def pieces_any(attention, feedforward, biases):
    full = [lax.all_gather(x, AXES, axis=0, tiled=True).reshape(PARTS, -1) for x in (attention, feedforward, biases)]
    upper = jnp.arange(PARTS) < PARTS // 2
    a, f = jax.vmap(lambda *x: own_pieces(*x, PARTS))(*full, upper)
    a, f = a.reshape((4, 4, 2) + a.shape[1:]), f.reshape((4, 4, 2) + f.shape[1:])

    return [[x[:, xy, c] for c in range(2) for xy in range(4)] for x in (a, f)]


def local(direct, tokens, cotangent, attention, feedforward, biases, gates, counts, lengths):
    me = lax.axis_index(AXES)
    n = PARTS
    *masks, x_t = call(
        prepare_body,
        [((2, ROWS, 128), BF), ((2, ROWS, 128), BF), ((D + 16, ROWS), BF)],
        [SMEM, SMEM, VMEM], [], 1 << 20, 3 << 20, 16,
    )(counts, lengths, tokens)
    if direct:
        place = jnp.stack([me, me % 2, me, (me // 2) % 4, me // 8]).astype(jnp.int32)
        (own_a,) = small(
            pack_square_body, [((A_TILES, 16, 128), BF)], (attention.reshape(-1, 128), biases.reshape(1, 128)), [((256, 128), F32)]
        )
        (own_f,) = small(
            pack_feed_body, [((F_TILES, 16, 128), BF)], (place, feedforward.reshape(-1, 128)), [((512, 128), F32)]
        )
        stack_a, masks = lax.optimization_barrier((along_z(own_a, n), masks))
        stack_f = along_z(own_f, n)
        chips_a = along_xy(stack_a, n)
        ga_all = across(chips_a, n)
        chips_f = along_xy(stack_f, n)
    else:
        ga_all, gf_all = pieces_any(attention, feedforward, biases)
        place = jnp.zeros((5,), jnp.int32)
    row = (ROWS, D)
    q, k, v, w, bias = call(
        project_body,
        [((H, ROWS, 128), BF)] * 2 + [(row, BF), ((PARTS, A_TILES, 16, 128), BF), ((1, 8 * D), F32)],
        [SMEM] + [VMEM] * 11, [], 2 << 30, 10 << 20, 20,
    )(place, tokens, *masks, *ga_all)
    ctx, ctx_t, lse = call(
        attend_body,
        [(row, BF), ((D + 16, ROWS), BF), ((8, ROWS), F32)],
        [VMEM] * 3,
        [((128, ROWS), BF), ((128, ROWS), F32)] + [((ROWS, 256), F32)] * 2 + [((ROWS, 256), BF)] * 2,
        12 << 30, 4 << 20, 20,
    )(q, k, v)
    if direct:
        chips_f, ctx = lax.optimization_barrier((chips_f, ctx))
        gf_all = across(chips_f, n)
    layer, gm, gctx, ff_keep, ff_send, wo_keep, wo_send = call(
        feed_body,
        [(row, BF, ANY), (row, F32), (row, BF)] + [((n // 2, G_TILES, 16, 128), F32, ANY)] * 2
        + [((4, 16, 16, 128), F32)] * 2,
        [SMEM, SMEM] + [VMEM] * 14,
        [((PARTS, F_TILES, 16, 128), BF), ((D + 16, ROWS), BF), (row, BF), (row, BF),
         ((FF + 16, ROWS), BF), ((ROWS, FF), BF)]
        + [((256, D), F32)] * 4 + [((256, FF), BF)] + [((256, D), F32)] * 2 + [((1, 8 * D), F32)]
        + [(row, BF), ((2, n // 2, G_TILES, 16, 128), F32), DMA((16,))],
        16 << 30, 30 << 20, 36,
    )(place, gates, tokens, cotangent, ctx, ctx_t, w, bias, *gf_all)

    def back(first, pairs, q, before):
        shares = [((3 * SHARE, 128), F32), ((3 * SHARE + 8, 128), F32)] * 2 if first else [((2 * SHARE, 128), F32)] * 2
        return call(
            partial(back_body, first),
            [((ROWS, 128 * pairs), BF)] * 3 + shares + ([] if first else [((8, 128), F32)]),
            [SMEM] + [VMEM] * (7 if first else 6),
            [((2, 128, ROWS), BF), ((128, ROWS), F32), ((ROWS, 128), F32), ((ROWS, 128), F32)]
            + [((ROWS, 256), F32)] * 4 + [((ROWS, 256), BF)] * 4 + ([((8, 128), F32)] if first else []),
            1000, 1000, 28,
        )(place, q, k, v, gctx, lse, x_t, *([before] if first else []))

    barrier = lax.optimization_barrier
    if direct:
        got, wo_got = swap(ff_send, n, 1), swap(wo_send, n, 1)
    *grads, keep, send, before = back(0, 1, q, None)
    if direct:
        got, wo_got, grads, send = barrier((got, wo_got, grads, send))
        parts = small(feed_xy_body, blocks_of(4 * G_TILES + 16), (place, ff_keep, got, wo_keep, wo_got))
        q, parts = barrier((q, parts))
        ff_got = hop(parts, n, 2)
        got = swap(send, n, 1)
    *parts, keep_a, keep_b, send_a, send_b = back(1, 3, q, before)
    grads += parts
    (input_grad,) = call(
        input_body, [(row, F32)], [VMEM] * 8, [], 1000, 1000, 24
    )(gm, *grads, w)
    if direct:
        gots = [got, swap(send_a, n, 1), swap(send_b, n, 1)]
        gots, input_grad, ff_got = barrier((gots, input_grad, ff_got))
        parts = small(square_xy_body, blocks_of(49), (place, keep, gots[0], keep_a, keep_b, *gots[1:]))
        ff_got, parts = barrier((ff_got, parts))
        got = hop(parts, n, 2)
        *ff_parts, wo = small(feed_z_body, blocks_of(G_TILES) + [((16, 16, 128), F32)], (place, *ff_got))
        ff_got = hop(ff_parts, n, 8)
        got, ff_parts = barrier((got, ff_parts))
    if direct:
        parts = small(square_z_body, blocks_of(17), (place, *got, wo), [((4, 17, 16, 128), F32)])
        got = hop(parts, n, 8)
        att_grad, ff_grad, bias_grad, gate_grad = call(
            finish_body,
            [((256, 128), F32), ((512, 128), F32), ((1, 128), F32), ((2,), F32, SMEM)],
            [SMEM] + [VMEM] * 8, [], 1 << 20, 1 << 20, 16,
        )(place, *ff_got, *got)
        att_grad, ff_grad, bias_grad = att_grad.reshape(-1), ff_grad.reshape(-1), bias_grad.reshape(-1)
        return layer, input_grad, att_grad, ff_grad, bias_grad, gate_grad

    def owners(keep, send):
        return jnp.stack([keep, send], axis=1).reshape((-1,) + keep.shape[1:])

    def reduce(flat):
        return lax.psum_scatter(flat.reshape(-1), AXES, scatter_dimension=0, tiled=True)

    both = owners(ff_keep, ff_send)
    up = jax.vmap(lambda t: from_columns(t, 2 * D // n))(both[: n // 2, :F_TILES]).reshape(-1)
    down = jax.vmap(lambda t: from_columns(t, 2 * FF // n))(both[n // 2 :, :F_TILES]).reshape(-1)
    ff_grad = reduce(jnp.concatenate([up, down]))
    tail = both[0, F_TILES]
    gate_grad = lax.psum((tail[1] + tail[2] + tail[3])[:2], AXES)
    bias_grad = owners(keep_b[3 * SHARE : 3 * SHARE + 4], send_b[3 * SHARE : 3 * SHARE + 4])
    bias_grad = jnp.concatenate([bias_grad, both[8:, F_TILES, 0]])
    both = []
    for own, x_a, x_b in ((keep, keep_a, keep_b), (send, send_a, send_b)):
        x_a, x_b = [jnp.concatenate(x).reshape(4, 6, 64, 128) for x in ((own[:SHARE], x_a), (own[SHARE:], x_b[: 3 * SHARE]))]
        both.append(jnp.concatenate([x_a[:, :4], x_b[:, :4], x_a[:, 4:], x_b[:, 4:]], axis=1))
    both = jnp.stack(both, axis=2).reshape(4, 24, 4, 16, 128).transpose(1, 0, 2, 3, 4)
    both = jnp.concatenate([both.reshape(24, 16, 16, 128), owners(wo_keep, wo_send)])
    att_grad = jax.vmap(lambda t: from_columns(t, 4 * D // n))(both)
    return layer, input_grad, reduce(att_grad), ff_grad, reduce(bias_grad), gate_grad


def solution(mesh):
    direct = dict(mesh.shape) == {"dp": 8, "fsdp": 4}
    both = P(AXES)
    rows = P(AXES, None)
    return jax.shard_map(
        partial(local, direct),
        mesh=mesh,
        in_specs=(rows, rows, both, both, both, P(), rows, rows),
        out_specs=(rows, rows, both, both, both, P()),
        check_vma=False,
    )
```

```python
from functools import partial

import jax
import jax.numpy as jnp
from jax import lax
from jax.experimental import pallas as pl
from jax.experimental.pallas import tpu as pltpu
from jax.sharding import PartitionSpec as P

D = 512
H = 8
HD = 64
FF = 2048
ROWS = 1024
SLOTS = 8
SHORT = 128
MID = 512
LONG = 1024
AXES = ("dp", "fsdp")
PARTS = 32
A_TILES = 17
F_TILES = 32
G_TILES = 33
BF = jnp.bfloat16
F32 = jnp.float32
CHUNK = 64
SHARE = 12 * 64
BIG = 512
VMEM = pl.BlockSpec(memory_space=pltpu.VMEM)
SMEM = pl.BlockSpec(memory_space=pltpu.SMEM)
ANY = pl.BlockSpec(memory_space=pl.ANY)
DMA = pltpu.SemaphoreType.DMA


def nn(a, b):
    return lax.dot_general(a, b, (((1,), (0,)), ((), ())), preferred_element_type=F32)


def nt(a, b):
    return lax.dot_general(a, b, (((1,), (1,)), ((), ())), preferred_element_type=F32)


def call(body, outs, ins, scratch, flops, moved, limit, grid=None):
    return pl.pallas_call(
        body,
        out_shape=[jax.ShapeDtypeStruct(o[0], o[1]) for o in outs],
        grid=grid or (),
        in_specs=ins,
        out_specs=[o[2] if len(o) > 2 else VMEM for o in outs],
        scratch_shapes=[pltpu.VMEM(*s) if isinstance(s, tuple) else s for s in scratch],
        compiler_params=pltpu.CompilerParams(vmem_limit_bytes=limit << 20),
        cost_estimate=pl.CostEstimate(flops=flops, bytes_accessed=moved, transcendentals=0),
    )


def slot_masks(counts, lengths, keys_out, rows_out):
    lane = lax.broadcasted_iota(jnp.int32, (1, 128), 1)
    slot = lane & 63
    longs, mids, shorts = counts[0, 2], counts[0, 1], counts[0, 0]
    in_long = jnp.minimum(slot, longs)
    in_mid = jnp.clip(slot - longs, 0, mids)
    in_short = jnp.clip(slot - longs - mids, 0, shorts)
    start = in_long * LONG + in_mid * MID + in_short * SHORT
    size = jnp.where(
        slot < longs,
        LONG,
        jnp.where(slot < longs + mids, MID, jnp.where(slot < longs + mids + shorts, SHORT, 0)),
    )
    valid = jnp.zeros((1, 128), jnp.int32)
    for s in range(SLOTS):
        valid = jnp.where(slot == s, lengths[0, s], valid)
    row = lax.broadcasted_iota(jnp.int32, (ROWS, 128), 0)
    member = (row >= start) & (row < start + size)
    usable = (row >= start) & (row < start + valid)
    for parity in range(2):
        here = (slot < SLOTS) & ((lane >= 64) if parity == 0 else (lane < 64))
        rows_out[parity] = jnp.where(here & member, 1.0, 0.0).astype(BF)
        keys_out[parity] = jnp.where(here & jnp.logical_not(usable), -1e30, 0.0).astype(BF)


def prepare_body(counts, lengths, tok, keys_mask, rows_mask, x_t):
    slot_masks(counts, lengths, keys_mask, rows_mask)
    x_t[:D] = tok[...].T
    x_t[D:] = jnp.ones((16, ROWS), BF)


def half_of(parity, shape):
    lane = lax.broadcasted_iota(jnp.int32, shape, len(shape) - 1)
    return (lane < 64) if parity == 0 else (lane >= 64)


def assemble(pieces, dest, me):
    for c in range(2):
        for xy in range(4):
            for z in range(4):
                dest[(8 * z + 2 * xy + c) ^ me] = pieces[4 * c + xy][z]


def columns(ref, owners, tiles, each):
    parts = []
    for t in range(tiles.start, tiles.stop, each):
        part = ref[owners, t : t + each]
        parts.append(part.reshape(part.shape[0] * each * 16, 128))
    return jnp.concatenate(parts, axis=1)


def square(ref, index):
    return columns(ref, slice(8 * index, 8 * index + 8), slice(0, 16), 4)


def project_body(place, tok, keys_mask, rows_mask, *refs):
    pieces, (q_out, k_out, v_out, w_out, bias_out) = refs[:8], refs[8:]
    assemble(pieces, w_out, place[0])
    for o in range(PARTS):
        bias_out[0:1, 128 * o : 128 * o + 128] = w_out[o, A_TILES - 1].astype(F32)[0:1]
    for r in range(4):
        at = slice(256 * r, 256 * r + 256)
        x = tok[at, :]
        q = (nn(x, square(w_out, 0)) + bias_out[0:1, 0:D]).astype(BF)
        q = (q.astype(F32) * 0.125).astype(BF)
        k = nn(x, square(w_out, 1)).astype(BF)
        v_out[at, :] = (nn(x, square(w_out, 2)) + bias_out[0:1, D : 2 * D]).astype(BF)
        for h in range(H):
            mine = half_of(h % 2, (256, 128))
            lanes = slice(h // 2 * 128, h // 2 * 128 + 128)
            q_out[h, at] = jnp.where(mine, q[:, lanes], rows_mask[h % 2, at])
            k_out[h, at] = jnp.where(mine, k[:, lanes], keys_mask[h % 2, at])


def attend_body(q_all, k_all, v_all, ctx_out, ctx_t_out, lse_out, values_t, ctx_t, s0, s1, p0, p1):
    def pair(p, _):
        attend_pair(
            p, q_all.at[pl.ds(2 * p, 2)], k_all.at[pl.ds(2 * p, 2)], v_all, ctx_out, ctx_t_out, lse_out, values_t, ctx_t,
            s0, s1, p0, p1,
        )
        return 0

    lax.fori_loop(0, 4, pair, 0)
    ctx_t_out[D:] = jnp.ones((16, ROWS), BF)


def attend_pair(p, q_in, k_in, v_all, ctx_out, ctx_t_out, lse_out, values_t, ctx_t, s0, s1, p0, p1):
    lanes = pl.ds(pl.multiple_of(p * 128, 128), 128)
    scores, probs = (s0, s1), (p0, p1)
    values_t[...] = v_all[:, lanes].T
    steps = [(parity, r) for parity in range(2) for r in range(4)]

    def score(i):
        parity, r = steps[i]

        def part(c):
            scores[i % 2][c : c + 256] = nt(k_in[parity, c : c + 256], q_in[parity, r * 256 : r * 256 + 256])

        return [partial(part, c) for c in range(0, ROWS, 256)]

    def collect(i):
        parity, r = steps[i]
        rows = slice(64 * parity, 64 * parity + 64)
        total = []

        def part(c):
            total.append(nn(values_t[rows, c : c + 256], probs[i % 2][c : c + 256]))
            if c == ROWS - 256:
                ctx_t[rows, r * 256 : r * 256 + 256] = (total[0] + total[1]) + (total[2] + total[3])

        return [partial(part, c) for c in range(0, ROWS, 256)]

    def soften(i):
        parity, r = steps[i]
        s, out = scores[i % 2], probs[i % 2]
        state = {}

        def peak(c):
            part = jnp.max(s[c : c + CHUNK].reshape(-1, 8, 256), axis=0)
            state["top"] = jnp.maximum(state["top"], part) if c else part
            if c == ROWS - CHUNK:
                state["top"] = jnp.max(state["top"], axis=0, keepdims=True)

        def power(c):
            e = jnp.exp(s[c : c + CHUNK] - state["top"])
            s[c : c + CHUNK] = e
            part = jnp.sum(e.reshape(-1, 8, 256), axis=0)
            state["mass"] = state["mass"] + part if c else part
            if c == ROWS - CHUNK:
                mass = jnp.sum(state["mass"], axis=0, keepdims=True)
                lse_out[pl.ds(2 * p + parity, 1), r * 256 : r * 256 + 256] = state["top"] + jnp.log(mass)
                state["share"] = 1.0 / mass

        def share(c):
            out[c : c + CHUNK] = (s[c : c + CHUNK] * state["share"]).astype(BF)

        at = range(0, ROWS, CHUNK)
        return [(1, partial(peak, c)) for c in at] + [(3, partial(power, c)) for c in at] + [
            (1.5, partial(share, c)) for c in at
        ]

    for task in score(0):
        task()
    for i in range(9):
        later = (score(i + 1) if i < 7 else []) + (collect(i - 1) if i else [])
        mix(soften(i) if i < 8 else [], later)
    low = ctx_t[...].astype(BF)
    ctx_t_out[lanes, :] = low
    ctx_out[:, lanes] = low.T


def mix(vector, matrix):
    whole = sum(weight for weight, _ in vector) or 1
    done, given = 0, 0
    for weight, task in vector:
        while given < len(matrix) and given * whole <= done * len(matrix):
            matrix[given]()
            given += 1
        task()
        done += weight
    for task in matrix[given:]:
        task()


def feed_body(place, gates, tok, cot, ctx, ctx_t, w_in, bias, *refs):
    pieces, refs = refs[:8], refs[8:]
    (layer_out, gm, gctx, keep_out, send_out, wo_keep, wo_send) = refs[:7]
    (w, low_t, gbr, gs_all, active_t, gh_all, v0, v1, b0, b1, active, second, gmid, sums) = refs[7:21]
    (layer, keep, send, sems) = refs[21:]
    values, backs = (v0, v1), (b0, b1)
    wo = w_in.at[24:32]
    assemble(pieces, w, place[0])

    def rows_of(r):
        return pl.ds(pl.multiple_of(r * 256, 256), 256)

    ga, gf = gates[0], gates[1]
    c1 = 0.7978845608028654
    c2 = 0.044715
    ones = jnp.ones((16, ROWS), BF)
    low_t[D:] = ones
    active_t[FF:] = ones

    def w_up(j):
        return columns(w, slice(0, 16), slice(8 * j, 8 * j + 8), 2)

    def w_down(j):
        return columns(w, slice(16 + 4 * j, 20 + 4 * j), slice(0, 32), 8)

    def rows(r, carry):
        attend_sum, feed_sum = carry
        at = rows_of(r)
        br = nn(ctx[at, :], square(wo, 0)) + bias[0:1, 2 * D : 3 * D]
        middle = tok[at, :].astype(F32) + ga * br
        low = middle.astype(BF)
        low_t[:D, at] = low.T
        ct = cot[at, :].astype(F32)
        gs = (gf * ct).astype(BF)
        gs_all[at, :] = gs

        def first(j):
            up, down = w_up(j), w_down(j)

            def value(n):
                values[j % 2][:, n : n + 256] = nn(low, up[:, n : n + 256])

            def back(n):
                backs[j % 2][:, n : n + 256] = nt(gs, down[n : n + 256])

            return [partial(f, n) for n in (0, 256) for f in (value, back)]

        def bend(j):
            def part(c):
                lines = slice(c, c + 32)
                cols = slice(4 * D + 512 * j, 4 * D + 512 * j + 512)
                v = values[j % 2][lines] + bias[0:1, cols]
                v2 = v * v
                t = jnp.tanh(v * (c1 + (c1 * c2) * v2))
                half = 0.5 + 0.5 * t
                act = v * half
                slope = half * (1.0 + (v - act) * (2.0 * c1 + (6.0 * c1 * c2) * v2))
                active[lines, 512 * j : 512 * j + 512] = act.astype(BF)
                gh_all[pl.ds(r * 256 + c, 32), 512 * j : 512 * j + 512] = (slope * backs[j % 2][lines]).astype(BF)

            return [(1, partial(part, c)) for c in range(0, 256, 32)]

        def then(j):
            up, down = w_up(j), w_down(j)
            cols = slice(512 * j, 512 * j + 512)

            def forward(n):
                val = nn(active[:, cols], down[:, n : n + 256])
                second[:, n : n + 256] = second[:, n : n + 256] + val if j else val

            def backward(n):
                val = nt(gh_all[at, cols], up[n : n + 256])
                gmid[:, n : n + 256] = gmid[:, n : n + 256] + val if j else val

            def turn():
                active_t[cols, at] = active[:, cols].T

            return [turn] + [partial(f, n) for n in (0, 256) for f in (forward, backward)]

        for task in first(0):
            task()
        for j in range(5):
            mix(bend(j) if j < 4 else [], (first(j + 1) if j < 3 else []) + (then(j - 1) if j else []))
        out = second[...] + bias[0:1, 3 * D : 4 * D]
        layer[at, :] = (middle + gf * out).astype(BF)
        grad = ct + gmid[...]
        gm[at, :] = grad
        gb = (ga * grad).astype(BF)
        gbr[at, :] = gb
        gctx[at, :] = nt(gb, square(wo, 0)).astype(BF)
        pltpu.make_async_copy(layer.at[at], layer_out.at[at], sems.at[0]).start()
        attend_sum = attend_sum + jnp.sum(br * grad, axis=0, keepdims=True)
        feed_sum = feed_sum + jnp.sum(out * ct, axis=0, keepdims=True)
        return attend_sum, feed_sum

    zero = jnp.zeros((1, D), F32)
    attend_sum, feed_sum = lax.fori_loop(0, 4, rows, (zero, zero))
    odd = place[1] == 1

    def store(o, tile, even, other):
        keep[o // 2, tile] = jnp.where(odd, other, even)
        mail = jnp.where(odd, even, other)
        send[o // 2, tile] = (split_row(mail) if tile == G_TILES - 1 else mail).astype(BF)

    def post(slots, sem):
        copies = [
            pltpu.make_async_copy(keep.at[slots], keep_out.at[slots], sems.at[sem]),
            pltpu.make_async_copy(send.at[slots], send_out.at[slots], sems.at[sem + 1]),
        ]
        for copy in copies:
            copy.start()
        return copies

    for j in range(4):
        val = nn(low_t[...], gh_all[:, 512 * j : 512 * j + 512])
        sums[0:1, 4 * D + 512 * j : 4 * D + 512 * j + 512] = val[D : D + 1]
        for o in range(0, 16, 2):
            for jj in range(4):
                for i in range(2):
                    top, col = 32 * o + 16 * i, slice(128 * jj, 128 * jj + 128)
                    store(o, 2 * (4 * j + jj) + i, val[top : top + 16, col], val[top + 32 : top + 48, col])
    val = nn(ctx_t[...], gbr[...])
    sums[0:1, 2 * D : 3 * D] = val[D : D + 1]
    for o in range(0, 8, 2):
        for j in range(4):
            for i in range(4):
                top, col = 64 * o + 16 * i, slice(128 * j, 128 * j + 128)
                even, other = val[top : top + 16, col], val[top + 64 : top + 80, col]
                wo_keep[o // 2, 4 * j + i] = jnp.where(odd, other, even)
                wo_send[o // 2, 4 * j + i] = jnp.where(odd, even, other)
    copies = []
    lane = lax.broadcasted_iota(jnp.int32, (1, 128), 1)
    gate = jnp.where(lane == 2 * place[2], jnp.sum(attend_sum), 0.0)
    gate = jnp.where(lane == 2 * place[2] + 1, jnp.sum(feed_sum), gate)
    high = gate.astype(BF).astype(F32)
    rest = gate - high
    mid = rest.astype(BF).astype(F32)
    last = (rest - mid).astype(BF).astype(F32)
    row = lax.broadcasted_iota(jnp.int32, (16, 128), 0)
    base = jnp.where(row == 1, high, jnp.where(row == 2, mid, jnp.where(row == 3, last, 0.0)))
    sums[0:1, 0 : 2 * D] = jnp.zeros((1, 2 * D), F32)

    def tail(o):
        even = jnp.where(row == 0, sums[0:1, 128 * o : 128 * o + 128], base)
        other = jnp.where(row == 0, sums[0:1, 128 * o + 128 : 128 * o + 256], base)
        store(o, G_TILES - 1, even, other)

    for j in (3, 2, 1, 0):
        val = nn(active_t[512 * j : 512 * j + (528 if j == 3 else 512)], gs_all[...])
        if j == 3:
            sums[0:1, 3 * D : 4 * D] = val[D : D + 1]
            for o in range(0, 16, 2):
                tail(o)
            copies += post(pl.ds(0, 8), 5)
        for o in (0, 2):
            tail(16 + 4 * j + o)
            for jj in range(4):
                for i in range(8):
                    top, col = 128 * o + 16 * i, slice(128 * jj, 128 * jj + 128)
                    store(16 + 4 * j + o, 8 * jj + i, val[top : top + 16, col], val[top + 128 : top + 144, col])
        copies += post(pl.ds(8 + 2 * j, 2), 7 + 2 * j)
    pltpu.make_async_copy(layer, layer_out, sems.at[0]).wait()
    for copy in copies:
        copy.wait()


def pair_back(p, parities, q_all, k_all, v_all, g_all, lse, dq_t, dk_acc, dv_acc, firsts, buffers):
    k_t, s0, s1, g0, g1, p0, p1, d0, d1 = buffers
    scores, grads, probs, diffs = (s0, s1), (g0, g1), (p0, p1), (d0, d1)
    steps = [(parity, r) for parity in parities for r in range(4)]
    lanes = pl.ds(pl.multiple_of(p * 128, 128), 128)
    q_in, k_in = q_all.at[pl.ds(2 * p, 2)], k_all.at[pl.ds(2 * p, 2)]
    for parity in parities:
        k_t[parity] = k_in[parity].T

    def mine(block, i):
        return jnp.where(half_of(steps[i][0], (256, 128)), block, jnp.zeros_like(block))

    def score(i):
        parity, r = steps[i]
        qa = q_in[parity, r * 256 : r * 256 + 256]
        ga = mine(g_all[r * 256 : r * 256 + 256, lanes], i)

        def part(c):
            scores[i % 2][c : c + BIG] = nt(k_in[parity, c : c + BIG], qa)

        def grad(c):
            grads[i % 2][c : c + BIG] = nt(v_all[c : c + BIG, lanes], ga)

        return [task for c in range(0, ROWS, BIG) for task in (partial(part, c), partial(grad, c))]

    def soften(i):
        parity, r = steps[i]
        s, g, out, diff = scores[i % 2], grads[i % 2], probs[i % 2], diffs[i % 2]
        logs = lse[pl.ds(2 * p + parity, 1), r * 256 : r * 256 + 256]
        state = {}

        def power(c):
            e = jnp.exp(s[c : c + CHUNK] - logs)
            s[c : c + CHUNK] = e
            out[c : c + CHUNK] = e.astype(BF)
            part = jnp.sum((e * g[c : c + CHUNK]).reshape(-1, 8, 256), axis=0)
            state["inner"] = state["inner"] + part if c else part
            if c == ROWS - CHUNK:
                state["inner"] = jnp.sum(state["inner"], axis=0, keepdims=True)

        def minus(c):
            diff[c : c + CHUNK] = (s[c : c + CHUNK] * (g[c : c + CHUNK] - state["inner"])).astype(BF)

        at = range(0, ROWS, CHUNK)
        return [(5.5, partial(power, c)) for c in at] + [(2.5, partial(minus, c)) for c in at]

    def collect(i):
        parity, r = steps[i]
        rows = slice(64 * parity, 64 * parity + 64)
        at = slice(r * 256, r * 256 + 256)
        qz, gz = mine(q_in[parity, at], i), mine(g_all[at, lanes], i)
        total = []

        def part(c):
            total.append(nn(k_t[parity, rows, c : c + 256], diffs[i % 2][c : c + 256]))
            if c == ROWS - 256:
                dq_t[rows, r * 256 : r * 256 + 256] = ((total[0] + total[1]) + (total[2] + total[3])) * 0.125

        def add(acc, first, ref, z, c):
            val = nn(ref[c : c + BIG], z)
            base = acc if i else first
            acc[c : c + BIG] = val if base is None else base[c : c + BIG] + val

        tasks = []
        for c in range(0, ROWS, 256):
            if c % BIG == 0:
                tasks += [partial(add, dv_acc, firsts[1], probs[i % 2], gz, c), partial(add, dk_acc, firsts[0], diffs[i % 2], qz, c)]
            tasks += [partial(part, c)]
        return tasks

    for task in score(0):
        task()
    last = len(steps) - 1
    for i in range(last + 2):
        later = (score(i + 1) if i < last else []) + (collect(i - 1) if i else [])
        mix(soften(i) if i <= last else [], later)


def back_first_body(q_all, k_all, v_all, g_all, lse, dq_t, dk_acc, dv_acc, *buffers):
    pair_back(0, (0,), q_all, k_all, v_all, g_all, lse, dq_t, dk_acc, dv_acc, (None, None), buffers)


def back_body(place, q_all, k_all, v_all, g_all, lse, x_t, dq_first, dk_first, dv_first, *refs):
    (dq_out, dk_out, dv_out, keep, send), refs = refs[:5], refs[5:]
    dq_t, dk_acc, dv_acc, sums, *buffers = refs
    odd = place[1] == 1

    def finish(p):
        out = pl.ds(pl.multiple_of(p * 128, 128), 128)
        dq = dq_t[...].astype(BF).T
        dk = dk_acc[...].astype(BF)
        dv = dv_acc[...].astype(BF)
        dq_out[:, out] = dq
        dk_out[:, out] = dk
        dv_out[:, out] = dv
        val = nn(x_t[...], jnp.concatenate([dq, dk, dv, dv], axis=1))
        sums[pl.ds(p, 1), :] = val[D : D + 1, 0:128]
        sums[pl.ds(4 + p, 1), :] = val[D : D + 1, 256:384]
        for index in range(3):
            for o in range(0, 8, 2):
                for i in range(4):
                    col, top = slice(128 * index, 128 * index + 128), 64 * o + 16 * i
                    even, other = val[top : top + 16, col], val[top + 64 : top + 80, col]
                    at = pl.ds(pl.multiple_of(SHARE * p + 64 * (4 * index + o // 2) + 16 * i, 16), 16)
                    keep[at] = jnp.where(odd, other, even)
                    send[at] = jnp.where(odd, even, other)

    def pair(p, _):
        pair_back(p, (0, 1), q_all, k_all, v_all, g_all, lse, dq_t, dk_acc, dv_acc, (None, None), buffers)
        finish(p)
        return 0

    dq_t[:64] = dq_first[...]
    pair_back(0, (1,), q_all, k_all, v_all, g_all, lse, dq_t, dk_acc, dv_acc, (dk_first, dv_first), buffers)
    finish(0)
    lax.fori_loop(1, 4, pair, 0)
    row = lax.broadcasted_iota(jnp.int32, (8, 128), 0)
    even, other = jnp.zeros((8, 128), F32), jnp.zeros((8, 128), F32)
    for o in range(0, 8, 2):
        even = jnp.where(row == o // 2, sums[o : o + 1, :], even)
        other = jnp.where(row == o // 2, sums[o + 1 : o + 2, :], other)
    keep[4 * SHARE :] = jnp.where(odd, other, even)
    send[4 * SHARE :] = jnp.where(odd, even, other)


def split_row(tile):
    row = lax.broadcasted_iota(jnp.int32, tile.shape, 0)
    rest = tile[0:1] - tile[0:1].astype(BF).astype(F32)
    return jnp.where(row == 4, rest, tile)


def join_row(tile):
    row = lax.broadcasted_iota(jnp.int32, tile.shape, 0)
    whole = tile[0:1] + tile[4:5]
    return jnp.where(row == 0, whole, jnp.where(row == 4, 0.0, tile))


def feed_xy_body(place, keep, got, wo_keep, wo_got, *outs):
    size = keep.shape[1]
    for t in range(4):
        here = place[3] ^ t
        out = outs[t]
        for z in range(4):
            at = 4 * z + here
            out[size * z : size * z + size - 1] = (keep[at, : size - 1] + got[at, : size - 1].astype(F32)).astype(out.dtype)
            total = keep[at, size - 1] + join_row(got[at, size - 1].astype(F32))
            out[size * z + size - 1] = (split_row(total) if t else total).astype(out.dtype)
        out[4 * size :] = (wo_keep[here] + wo_got[here]).astype(out.dtype)


def feed_z_body(place, keep, g1, g2, g3, out0, out1, out2, out3, wo_out):
    size = out0.shape[0]
    for t, out in enumerate((out0, out1, out2, out3)):
        at = pl.ds((place[4] ^ t) * size, size - 1)
        total = keep[at] + g1[at].astype(F32) + g2[at].astype(F32) + g3[at].astype(F32)
        out[: size - 1] = total.astype(out.dtype)
        at = (place[4] ^ t) * size + size - 1
        total = keep[at]
        for g in (g1, g2, g3):
            total = total + join_row(g[at].astype(F32))
        out[size - 1] = (split_row(total) if t else total).astype(out.dtype)
    at = slice(4 * size, 4 * size + 16)
    wo_out[...] = keep[at] + g1[at].astype(F32) + g2[at].astype(F32) + g3[at].astype(F32)


def square_xy_body(place, keep, got, *outs):
    for t in range(4):
        here = place[3] ^ t
        out = outs[t]
        for z in range(3):
            for p in range(4):
                rows = pl.ds(pl.multiple_of(SHARE * p + 64 * (4 * z + here), 64), 64)
                total = keep[rows] + got[rows]
                out[16 * z + 4 * p : 16 * z + 4 * p + 4] = total.reshape(4, 16, 128).astype(out.dtype)
        row = lax.broadcasted_iota(jnp.int32, (16, 128), 0)
        total = keep[pl.ds(4 * SHARE + here, 1)] + got[pl.ds(4 * SHARE + here, 1)]
        total = jnp.where(row == 0, total, 0.0)
        out[48] = (split_row(total) if t else total).astype(out.dtype)


def square_z_body(place, keep, g1, g2, g3, wo, out0, out1, out2, out3, whole):
    for z in range(3):
        at = slice(16 * z, 16 * z + 16)
        whole[z, :16] = keep[at] + g1[at].astype(F32) + g2[at].astype(F32) + g3[at].astype(F32)
        whole[z + 1, 16] = jnp.zeros((16, 128), F32)
    whole[3, :16] = wo[...]
    total = keep[48]
    for g in (g1, g2, g3):
        total = total + join_row(g[48].astype(F32))
    whole[0, 16] = total
    for t, out in enumerate((out0, out1, out2, out3)):
        at = place[4] ^ t
        out[:16] = whole[at, :16].astype(out.dtype)
        out[16] = (split_row(whole[at, 16]) if t else whole[at, 16]).astype(out.dtype)


def input_body(gm, dq, dk, dv, w, out):
    for r in range(4):
        at = slice(256 * r, 256 * r + 256)
        total = gm[at, :]
        for index in range(3):
            total = total + nt((dq, dk, dv)[index][at, :], square(w, index))
        out[at, :] = total


def to_columns(flat, rows):
    return flat.reshape(rows // 16, 16, -1, 128).transpose(2, 0, 1, 3).reshape(-1, 16, 128)


def from_columns(tiles, rows):
    return tiles.reshape(-1, rows // 16, 16, 128).transpose(1, 2, 0, 3).reshape(-1)


def swap(x, n, bit):
    return lax.ppermute(x, AXES, [(i, i ^ bit) for i in range(n)])


def small(body, outs, args, scratch=()):
    ins = [SMEM if arg.dtype == jnp.int32 else VMEM for arg in args]
    size = sum(arg.size for arg in args)
    return call(body, outs, ins, scratch, 2 * size, 6 * size, 16)(*args)


def blocks_of(*shape):
    return [(shape + (16, 128), F32)] + [(shape + (16, 128), BF)] * 3


def hop(parts, n, step):
    return [parts[0]] + [swap(part, n, step * t) for t, part in enumerate(parts) if t]


def tie(values, after):
    return lax.optimization_barrier((values, after))[0]


def along_z(own, n):
    return jnp.stack([own] + [swap(own, n, 8 * z) for z in (1, 2, 3)])


def along_xy(stack, n):
    return [stack] + [swap(stack, n, 2 * xy) for xy in (1, 2, 3)]


def across(chips, n):
    return chips + [swap(part, n, 1) for part in chips]


def pack_square_body(flat, biases, out, wide):
    wide[...] = flat[...].astype(F32)
    for j in range(4):
        for i in range(4):
            out[4 * j + i] = wide[pl.ds(64 * i + j, 16, stride=4), :].astype(BF)
    row = lax.broadcasted_iota(jnp.int32, (16, 128), 0)
    out[16] = jnp.where(row == 0, biases[...].astype(F32), 0.0).astype(BF)


def pack_feed_body(place, flat, out, wide):
    wide[...] = flat[...].astype(F32)

    @pl.when(place[0] < PARTS // 2)
    def _():
        for j in range(16):
            for i in range(2):
                out[2 * j + i] = wide[pl.ds(256 * i + j, 16, stride=16), :].astype(BF)

    @pl.when(place[0] >= PARTS // 2)
    def _():
        for j in range(4):
            for i in range(8):
                out[8 * j + i] = wide[pl.ds(64 * i + j, 16, stride=4), :].astype(BF)


def copy_body(ref, out):
    for i in range(5):
        out[i] = ref[i]


def finish_body(place, keep_f, f1, f2, f3, keep_a, a1, a2, a3, att, ff, bias, gate):
    def added(keep, gots, at):
        total = keep[at]
        for g in gots:
            total = total + g[at].astype(F32)
        return total

    def added_tail(keep, gots, at):
        total = keep[at]
        for g in gots:
            total = total + join_row(g[at].astype(F32))
        return total

    for j in range(4):
        for i in range(4):
            att[pl.ds(64 * i + j, 16, stride=4), :] = added(keep_a, (a1, a2, a3), 4 * j + i)
    gots = (f1, f2, f3)

    @pl.when(place[0] < PARTS // 2)
    def _():
        for j in range(16):
            for i in range(2):
                ff[pl.ds(256 * i + j, 16, stride=16), :] = added(keep_f, gots, 2 * j + i)

    @pl.when(place[0] >= PARTS // 2)
    def _():
        for j in range(4):
            for i in range(8):
                ff[pl.ds(64 * i + j, 16, stride=4), :] = added(keep_f, gots, 8 * j + i)

    tail = added_tail(keep_f, gots, F_TILES)
    own = added_tail(keep_a, (a1, a2, a3), 16)
    bias[...] = jnp.where(place[0] < 8, own[0:1], tail[0:1])
    gates = tail[1:2] + tail[2:3] + tail[3:4]
    lane = lax.broadcasted_iota(jnp.int32, (1, 128), 1)
    for g in range(2):
        gate[g] = jnp.sum(jnp.where((lane < 2 * PARTS) & (lane % 2 == g), gates, 0.0))


def own_pieces(attention, feedforward, biases, upper, parts):
    tail = jnp.pad(biases.reshape(1, 1, 128), ((0, 0), (0, 15), (0, 0)))
    own_a = jnp.concatenate([to_columns(attention, 4 * D // parts), tail], axis=0)
    up = to_columns(feedforward, 2 * D // parts)
    down = to_columns(feedforward, 2 * FF // parts)
    return own_a, jnp.where(upper, up, down)


def pieces_any(attention, feedforward, biases):
    full = [lax.all_gather(x, AXES, axis=0, tiled=True).reshape(PARTS, -1) for x in (attention, feedforward, biases)]
    upper = jnp.arange(PARTS) < PARTS // 2
    a, f = jax.vmap(lambda *x: own_pieces(*x, PARTS))(*full, upper)
    a, f = a.reshape((4, 4, 2) + a.shape[1:]), f.reshape((4, 4, 2) + f.shape[1:])

    return [[x[:, xy, c] for c in range(2) for xy in range(4)] for x in (a, f)]


def local(direct, tokens, cotangent, attention, feedforward, biases, gates, counts, lengths):
    me = lax.axis_index(AXES)
    n = PARTS
    *masks, x_t = call(
        prepare_body,
        [((2, ROWS, 128), BF), ((2, ROWS, 128), BF), ((D + 16, ROWS), BF)],
        [SMEM, SMEM, VMEM], [], 1 << 20, 3 << 20, 16,
    )(counts, lengths, tokens)
    if direct:
        place = jnp.stack([me, me % 2, me, (me // 2) % 4, me // 8]).astype(jnp.int32)
        (own_a,) = small(
            pack_square_body, [((A_TILES, 16, 128), BF)], (attention.reshape(-1, 128), biases.reshape(1, 128)), [((256, 128), F32)]
        )
        (own_f,) = small(
            pack_feed_body, [((F_TILES, 16, 128), BF)], (place, feedforward.reshape(-1, 128)), [((512, 128), F32)]
        )
        stack_a, masks = lax.optimization_barrier((along_z(own_a, n), masks))
        far = [swap(own_f, n, 16), swap(own_f, n, 24)]
        chips_a = along_xy(stack_a, n)
        far, own_f, place = lax.optimization_barrier((far, own_f, place))
        near = swap(own_f, n, 8)
        (place,) = call(copy_body, [((5,), jnp.int32, SMEM)], [SMEM], [], 8 << 30, 1000, 16)(place)
        chips_a, place = lax.optimization_barrier((chips_a, place))
        ga_all = across(chips_a, n)
        chips_f = along_xy(jnp.stack([own_f, near] + far), n)
    else:
        ga_all, gf_all = pieces_any(attention, feedforward, biases)
        place = jnp.zeros((5,), jnp.int32)
    row = (ROWS, D)
    q, k, v, w, bias = call(
        project_body,
        [((H, ROWS, 128), BF)] * 2 + [(row, BF), ((PARTS, A_TILES, 16, 128), BF), ((1, 8 * D), F32)],
        [SMEM] + [VMEM] * 11, [], 1000, 1000, 20,
    )(place, tokens, *masks, *ga_all)
    ctx, ctx_t, lse = call(
        attend_body,
        [(row, BF), ((D + 16, ROWS), BF), ((8, ROWS), F32)],
        [VMEM] * 3,
        [((128, ROWS), BF), ((128, ROWS), F32)] + [((ROWS, 256), F32)] * 2 + [((ROWS, 256), BF)] * 2,
        1000, 1000, 20,
    )(q, k, v)
    if direct:
        chips_f, ctx = lax.optimization_barrier((chips_f, ctx))
        gf_all = across(chips_f, n)
    layer, gm, gctx, ff_keep, ff_send, wo_keep, wo_send = call(
        feed_body,
        [(row, BF, ANY), (row, F32), (row, BF)]
        + [((n // 2, G_TILES, 16, 128), F32, ANY), ((n // 2, G_TILES, 16, 128), BF, ANY)]
        + [((4, 16, 16, 128), F32)] * 2,
        [SMEM, SMEM] + [VMEM] * 14,
        [((PARTS, F_TILES, 16, 128), BF), ((D + 16, ROWS), BF), (row, BF), (row, BF),
         ((FF + 16, ROWS), BF), ((ROWS, FF), BF)]
        + [((256, D), F32)] * 4 + [((256, FF), BF)] + [((256, D), F32)] * 2 + [((1, 8 * D), F32)]
        + [(row, BF), ((n // 2, G_TILES, 16, 128), F32), ((n // 2, G_TILES, 16, 128), BF), DMA((16,))],
        16 << 30, 30 << 20, 36,
    )(place, gates, tokens, cotangent, ctx, ctx_t, w, bias, *gf_all)

    half, whole = (ROWS // 16, ROWS), (128, ROWS)
    buffers = [((2, 128, ROWS), BF)] + [((ROWS, 256), F32)] * 4 + [((ROWS, 256), BF)] * 4
    sums = [((ROWS, 128), F32)] * 2
    barrier = lax.optimization_barrier
    if direct:
        got, wo_got = swap(ff_send, n, 1), swap(wo_send, n, 1)
    begun = call(
        back_first_body, [(half, F32)] + sums, [VMEM] * 5, buffers, 1000, 1000, 28
    )(q, k, v, gctx, lse)
    if direct:
        got, wo_got, begun = barrier((got, wo_got, begun))
        parts = small(feed_xy_body, blocks_of(4 * G_TILES + 16), (place, ff_keep, got, wo_keep, wo_got))
        q, parts = barrier((q, parts))
        ff_got = hop(parts, n, 2)
    *grads, keep, send = call(
        back_body,
        [(row, BF)] * 3 + [((4 * SHARE + 8, 128), F32)] * 2,
        [SMEM] + [VMEM] * 9,
        [(whole, F32)] + sums + [((8, 128), F32)] + buffers,
        1000, 1000, 28,
    )(place, q, k, v, gctx, lse, x_t, *begun)
    if direct:
        got = swap(send, n, 1)
    (input_grad,) = call(
        input_body, [(row, F32)], [VMEM] * 5, [], 32 << 30, 1000, 24
    )(gm, *grads, w)
    if direct:
        got, input_grad, ff_got = barrier((got, input_grad, ff_got))
        parts = small(square_xy_body, blocks_of(49), (place, keep, got))
        ff_got, parts = barrier((ff_got, parts))
        got = hop(parts, n, 2)
        *ff_parts, wo = small(feed_z_body, blocks_of(G_TILES) + [((16, 16, 128), F32)], (place, *ff_got))
        ff_got = hop(ff_parts, n, 8)
        got, ff_parts = barrier((got, ff_parts))
    if direct:
        parts = small(square_z_body, blocks_of(17), (place, *got, wo), [((4, 17, 16, 128), F32)])
        got = hop(parts, n, 8)
        att_grad, ff_grad, bias_grad, gate_grad = call(
            finish_body,
            [((256, 128), F32), ((512, 128), F32), ((1, 128), F32), ((2,), F32, SMEM)],
            [SMEM] + [VMEM] * 8, [], 1 << 20, 1 << 20, 16,
        )(place, *ff_got, *got)
        att_grad, ff_grad, bias_grad = att_grad.reshape(-1), ff_grad.reshape(-1), bias_grad.reshape(-1)
        return layer, input_grad, att_grad, ff_grad, bias_grad, gate_grad

    def owners(keep, send):
        return jnp.stack([keep, send], axis=1).reshape((-1,) + keep.shape[1:])

    def reduce(flat):
        return lax.psum_scatter(flat.reshape(-1), AXES, scatter_dimension=0, tiled=True)

    mail = ff_send.astype(F32)
    mail = mail.at[:, F_TILES, 0].add(mail[:, F_TILES, 4])
    both = owners(ff_keep, mail)
    up = jax.vmap(lambda t: from_columns(t, 2 * D // n))(both[: n // 2, :F_TILES]).reshape(-1)
    down = jax.vmap(lambda t: from_columns(t, 2 * FF // n))(both[n // 2 :, :F_TILES]).reshape(-1)
    ff_grad = reduce(jnp.concatenate([up, down]))
    tail = both[0, F_TILES]
    gate_grad = lax.psum((tail[1] + tail[2] + tail[3])[:2], AXES)
    bias_grad = owners(keep[4 * SHARE : 4 * SHARE + 4], send[4 * SHARE : 4 * SHARE + 4])
    bias_grad = jnp.concatenate([bias_grad, both[8:, F_TILES, 0]])
    both = jnp.stack([x[: 4 * SHARE].reshape(4, 12, 4, 16, 128) for x in (keep, send)], axis=2)
    both = both.reshape(4, 24, 4, 16, 128).transpose(1, 0, 2, 3, 4)
    both = jnp.concatenate([both.reshape(24, 16, 16, 128), owners(wo_keep, wo_send)])
    att_grad = jax.vmap(lambda t: from_columns(t, 4 * D // n))(both)
    return layer, input_grad, reduce(att_grad), ff_grad, reduce(bias_grad), gate_grad


def solution(mesh):
    direct = dict(mesh.shape) == {"dp": 8, "fsdp": 4}
    both = P(AXES)
    rows = P(AXES, None)
    return jax.shard_map(
        partial(local, direct),
        mesh=mesh,
        in_specs=(rows, rows, both, both, both, P(), rows, rows),
        out_specs=(rows, rows, both, both, both, P()),
        check_vma=False,
    )
```

```python
from functools import partial

import jax
import jax.numpy as jnp
from jax import lax
from jax.experimental import pallas as pl
from jax.experimental.pallas import tpu as pltpu
from jax.sharding import PartitionSpec as P

D = 512
H = 8
HD = 64
FF = 2048
ROWS = 1024
SLOTS = 8
SHORT = 128
MID = 512
LONG = 1024
AXES = ("dp", "fsdp")
PARTS = 32
A_TILES = 17
F_TILES = 32
G_TILES = 33
BF = jnp.bfloat16
F32 = jnp.float32
CHUNK = 64
SHARE = 12 * 64
BIG = 512
VMEM = pl.BlockSpec(memory_space=pltpu.VMEM)
SMEM = pl.BlockSpec(memory_space=pltpu.SMEM)
ANY = pl.BlockSpec(memory_space=pl.ANY)
DMA = pltpu.SemaphoreType.DMA


def nn(a, b):
    return lax.dot_general(a, b, (((1,), (0,)), ((), ())), preferred_element_type=F32)


def nt(a, b):
    return lax.dot_general(a, b, (((1,), (1,)), ((), ())), preferred_element_type=F32)


def call(body, outs, ins, scratch, flops, moved, limit, grid=None):
    return pl.pallas_call(
        body,
        out_shape=[jax.ShapeDtypeStruct(o[0], o[1]) for o in outs],
        grid=grid or (),
        in_specs=ins,
        out_specs=[o[2] if len(o) > 2 else VMEM for o in outs],
        scratch_shapes=[pltpu.VMEM(*s) if isinstance(s, tuple) else s for s in scratch],
        compiler_params=pltpu.CompilerParams(vmem_limit_bytes=limit << 20),
        cost_estimate=pl.CostEstimate(flops=flops, bytes_accessed=moved, transcendentals=0),
    )


def slot_masks(counts, lengths, keys_out, rows_out):
    lane = lax.broadcasted_iota(jnp.int32, (1, 128), 1)
    slot = lane & 63
    longs, mids, shorts = counts[0, 2], counts[0, 1], counts[0, 0]
    in_long = jnp.minimum(slot, longs)
    in_mid = jnp.clip(slot - longs, 0, mids)
    in_short = jnp.clip(slot - longs - mids, 0, shorts)
    start = in_long * LONG + in_mid * MID + in_short * SHORT
    size = jnp.where(
        slot < longs,
        LONG,
        jnp.where(slot < longs + mids, MID, jnp.where(slot < longs + mids + shorts, SHORT, 0)),
    )
    valid = jnp.zeros((1, 128), jnp.int32)
    for s in range(SLOTS):
        valid = jnp.where(slot == s, lengths[0, s], valid)
    row = lax.broadcasted_iota(jnp.int32, (ROWS, 128), 0)
    member = (row >= start) & (row < start + size)
    usable = (row >= start) & (row < start + valid)
    for parity in range(2):
        here = (slot < SLOTS) & ((lane >= 64) if parity == 0 else (lane < 64))
        rows_out[parity] = jnp.where(here & member, 1.0, 0.0).astype(BF)
        keys_out[parity] = jnp.where(here & jnp.logical_not(usable), -1e30, 0.0).astype(BF)


def prepare_body(counts, lengths, tok, keys_mask, rows_mask, x_t):
    slot_masks(counts, lengths, keys_mask, rows_mask)
    x_t[:D] = tok[...].T
    x_t[D:] = jnp.ones((16, ROWS), BF)


def half_of(parity, shape):
    lane = lax.broadcasted_iota(jnp.int32, shape, len(shape) - 1)
    return (lane < 64) if parity == 0 else (lane >= 64)


def assemble(pieces, dest, me):
    for c in range(2):
        for xy in range(4):
            for z in range(4):
                dest[(8 * z + 2 * xy + c) ^ me] = pieces[4 * c + xy][z]


def columns(ref, owners, tiles, each):
    parts = []
    for t in range(tiles.start, tiles.stop, each):
        part = ref[owners, t : t + each]
        parts.append(part.reshape(part.shape[0] * each * 16, 128))
    return jnp.concatenate(parts, axis=1)


def square(ref, index):
    return columns(ref, slice(8 * index, 8 * index + 8), slice(0, 16), 4)


def project_body(place, tok, keys_mask, rows_mask, *refs):
    pieces, (q_out, k_out, v_out, w_out, bias_out) = refs[:8], refs[8:]
    assemble(pieces, w_out, place[0])
    for o in range(PARTS):
        bias_out[0:1, 128 * o : 128 * o + 128] = w_out[o, A_TILES - 1].astype(F32)[0:1]
    for r in range(4):
        at = slice(256 * r, 256 * r + 256)
        x = tok[at, :]
        q = (nn(x, square(w_out, 0)) + bias_out[0:1, 0:D]).astype(BF)
        q = (q.astype(F32) * 0.125).astype(BF)
        k = nn(x, square(w_out, 1)).astype(BF)
        v_out[at, :] = (nn(x, square(w_out, 2)) + bias_out[0:1, D : 2 * D]).astype(BF)
        for h in range(H):
            mine = half_of(h % 2, (256, 128))
            lanes = slice(h // 2 * 128, h // 2 * 128 + 128)
            q_out[h, at] = jnp.where(mine, q[:, lanes], rows_mask[h % 2, at])
            k_out[h, at] = jnp.where(mine, k[:, lanes], keys_mask[h % 2, at])


def attend_body(q_all, k_all, v_all, ctx_out, ctx_t_out, lse_out, values_t, ctx_t, s0, s1, p0, p1):
    def pair(p, _):
        attend_pair(
            p, q_all.at[pl.ds(2 * p, 2)], k_all.at[pl.ds(2 * p, 2)], v_all, ctx_out, ctx_t_out, lse_out, values_t, ctx_t,
            s0, s1, p0, p1,
        )
        return 0

    lax.fori_loop(0, 4, pair, 0)
    ctx_t_out[D:] = jnp.ones((16, ROWS), BF)


def attend_pair(p, q_in, k_in, v_all, ctx_out, ctx_t_out, lse_out, values_t, ctx_t, s0, s1, p0, p1):
    lanes = pl.ds(pl.multiple_of(p * 128, 128), 128)
    scores, probs = (s0, s1), (p0, p1)
    values_t[...] = v_all[:, lanes].T
    steps = [(parity, r) for parity in range(2) for r in range(4)]

    def score(i):
        parity, r = steps[i]

        def part(c):
            scores[i % 2][c : c + 256] = nt(k_in[parity, c : c + 256], q_in[parity, r * 256 : r * 256 + 256])

        return [partial(part, c) for c in range(0, ROWS, 256)]

    def collect(i):
        parity, r = steps[i]
        rows = slice(64 * parity, 64 * parity + 64)
        total = []

        def part(c):
            total.append(nn(values_t[rows, c : c + 256], probs[i % 2][c : c + 256]))
            if c == ROWS - 256:
                ctx_t[rows, r * 256 : r * 256 + 256] = (total[0] + total[1]) + (total[2] + total[3])

        return [partial(part, c) for c in range(0, ROWS, 256)]

    def soften(i):
        parity, r = steps[i]
        s, out = scores[i % 2], probs[i % 2]
        state = {}

        def peak(c):
            part = jnp.max(s[c : c + CHUNK].reshape(-1, 8, 256), axis=0)
            state["top"] = jnp.maximum(state["top"], part) if c else part
            if c == ROWS - CHUNK:
                state["top"] = jnp.max(state["top"], axis=0, keepdims=True)

        def power(c):
            e = jnp.exp(s[c : c + CHUNK] - state["top"])
            s[c : c + CHUNK] = e
            part = jnp.sum(e.reshape(-1, 8, 256), axis=0)
            state["mass"] = state["mass"] + part if c else part
            if c == ROWS - CHUNK:
                mass = jnp.sum(state["mass"], axis=0, keepdims=True)
                lse_out[pl.ds(2 * p + parity, 1), r * 256 : r * 256 + 256] = state["top"] + jnp.log(mass)
                state["share"] = 1.0 / mass

        def share(c):
            out[c : c + CHUNK] = (s[c : c + CHUNK] * state["share"]).astype(BF)

        at = range(0, ROWS, CHUNK)
        return [(1, partial(peak, c)) for c in at] + [(3, partial(power, c)) for c in at] + [
            (1.5, partial(share, c)) for c in at
        ]

    for task in score(0):
        task()
    for i in range(9):
        later = (score(i + 1) if i < 7 else []) + (collect(i - 1) if i else [])
        mix(soften(i) if i < 8 else [], later)
    low = ctx_t[...].astype(BF)
    ctx_t_out[lanes, :] = low
    ctx_out[:, lanes] = low.T


def mix(vector, matrix):
    whole = sum(weight for weight, _ in vector) or 1
    done, given = 0, 0
    for weight, task in vector:
        while given < len(matrix) and given * whole <= done * len(matrix):
            matrix[given]()
            given += 1
        task()
        done += weight
    for task in matrix[given:]:
        task()


def branch_body(gates, tok, cot, ctx, w, bias, branch, low, low_t, gs):
    wo = square(w, 3)
    for r in range(4):
        at = slice(256 * r, 256 * r + 256)
        out = nn(ctx[at, :], wo) + bias[0:1, 2 * D : 3 * D]
        branch[at, :] = out
        low[at, :] = (tok[at, :].astype(F32) + gates[0] * out).astype(BF)
        gs[at, :] = (gates[1] * cot[at, :].astype(F32)).astype(BF)
    low_t[:D] = low[...].T
    low_t[D:] = jnp.ones((16, ROWS), BF)


def feed_body(place, gates, tok, cot, branch, low_all, low_t, gs_all, ctx_t, w_in, bias, *refs):
    pieces, refs = refs[:8], refs[8:]
    (layer_out, gm, gctx, keep_out, send_out, wo_keep, wo_send) = refs[:7]
    (w, gbr, active_t, gh_all, v0, v1, b0, b1, active, second, gmid, sums) = refs[7:19]
    (layer, keep, send, sems) = refs[19:]
    values, backs = (v0, v1), (b0, b1)
    wo = w_in.at[24:32]
    assemble(pieces, w, place[0])

    def rows_of(r):
        return pl.ds(pl.multiple_of(r * 256, 256), 256)

    ga, gf = gates[0], gates[1]
    c1 = 0.7978845608028654
    c2 = 0.044715
    active_t[FF:] = jnp.ones((16, ROWS), BF)

    def w_up(j):
        return columns(w, slice(0, 16), slice(8 * j, 8 * j + 8), 2)

    def w_down(j):
        return columns(w, slice(16 + 4 * j, 20 + 4 * j), slice(0, 32), 8)

    def rows(r, carry):
        attend_sum, feed_sum = carry
        at = rows_of(r)
        low, gs = low_all[at, :], gs_all[at, :]

        def first(j):
            up, down = w_up(j), w_down(j)

            def value(n):
                values[j % 2][:, n : n + 256] = nn(low, up[:, n : n + 256])

            def back(n):
                backs[j % 2][:, n : n + 256] = nt(gs, down[n : n + 256])

            return [partial(f, n) for n in (0, 256) for f in (value, back)]

        def bend(j):
            def part(c):
                lines = slice(c, c + 32)
                cols = slice(4 * D + 512 * j, 4 * D + 512 * j + 512)
                v = values[j % 2][lines] + bias[0:1, cols]
                v2 = v * v
                t = jnp.tanh(v * (c1 + (c1 * c2) * v2))
                half = 0.5 + 0.5 * t
                act = v * half
                slope = half * (1.0 + (v - act) * (2.0 * c1 + (6.0 * c1 * c2) * v2))
                active[lines, 512 * j : 512 * j + 512] = act.astype(BF)
                gh_all[pl.ds(r * 256 + c, 32), 512 * j : 512 * j + 512] = (slope * backs[j % 2][lines]).astype(BF)

            return [(1, partial(part, c)) for c in range(0, 256, 32)]

        def then(j):
            up, down = w_up(j), w_down(j)
            cols = slice(512 * j, 512 * j + 512)

            def forward(n):
                val = nn(active[:, cols], down[:, n : n + 256])
                second[:, n : n + 256] = second[:, n : n + 256] + val if j else val

            def backward(n):
                val = nt(gh_all[at, cols], up[n : n + 256])
                gmid[:, n : n + 256] = gmid[:, n : n + 256] + val if j else val

            def turn():
                active_t[cols, at] = active[:, cols].T

            return [turn] + [partial(f, n) for n in (0, 256) for f in (forward, backward)]

        for task in first(0):
            task()
        for j in range(5):
            mix(bend(j) if j < 4 else [], (first(j + 1) if j < 3 else []) + (then(j - 1) if j else []))
        out = second[...] + bias[0:1, 3 * D : 4 * D]
        br, ct = branch[at, :], cot[at, :].astype(F32)
        layer[at, :] = (tok[at, :].astype(F32) + ga * br + gf * out).astype(BF)
        grad = ct + gmid[...]
        gm[at, :] = grad
        gb = (ga * grad).astype(BF)
        gbr[at, :] = gb
        pltpu.make_async_copy(layer.at[at], layer_out.at[at], sems.at[0]).start()
        attend_sum = attend_sum + jnp.sum(br * grad, axis=0, keepdims=True)
        feed_sum = feed_sum + jnp.sum(out * ct, axis=0, keepdims=True)
        return attend_sum, feed_sum

    zero = jnp.zeros((1, D), F32)
    attend_sum, feed_sum = lax.fori_loop(0, 4, rows, (zero, zero))
    odd = place[1] == 1

    def store(o, tile, even, other):
        keep[o // 2, tile] = jnp.where(odd, other, even)
        mail = jnp.where(odd, even, other)
        send[o // 2, tile] = (split_row(mail) if tile == G_TILES - 1 else mail).astype(BF)

    def post(slots, sem):
        copies = [
            pltpu.make_async_copy(keep.at[slots], keep_out.at[slots], sems.at[sem]),
            pltpu.make_async_copy(send.at[slots], send_out.at[slots], sems.at[sem + 1]),
        ]
        for copy in copies:
            copy.start()
        return copies

    def up_grad(j):
        return nn(low_t[...], gh_all[:, 512 * j : 512 * j + 512])

    def up_store(j, val):
        sums[0:1, 4 * D + 512 * j : 4 * D + 512 * j + 512] = val[D : D + 1]
        for o in range(0, 16, 2):
            for jj in range(4):
                for i in range(2):
                    top, col = 32 * o + 16 * i, slice(128 * jj, 128 * jj + 128)
                    store(o, 2 * (4 * j + jj) + i, val[top : top + 16, col], val[top + 32 : top + 48, col])

    def down_grad(j):
        return nn(active_t[512 * j : 512 * j + (528 if j == 3 else 512)], gs_all[...])

    def down_store(j, val):
        if j == 3:
            sums[0:1, 3 * D : 4 * D] = val[D : D + 1]
        for o in (0, 2):
            for jj in range(4):
                for i in range(8):
                    top, col = 128 * o + 16 * i, slice(128 * jj, 128 * jj + 128)
                    store(16 + 4 * j + o, 8 * jj + i, val[top : top + 16, col], val[top + 128 : top + 144, col])

    def out_grad(_):
        return nn(ctx_t[...], gbr[...])

    def out_store(_, val):
        sums[0:1, 2 * D : 3 * D] = val[D : D + 1]
        for o in range(0, 8, 2):
            for j in range(4):
                for i in range(4):
                    top, col = 64 * o + 16 * i, slice(128 * j, 128 * j + 128)
                    even, other = val[top : top + 16, col], val[top + 64 : top + 80, col]
                    wo_keep[o // 2, 4 * j + i] = jnp.where(odd, other, even)
                    wo_send[o // 2, 4 * j + i] = jnp.where(odd, even, other)

    for r in range(4):
        at = slice(256 * r, 256 * r + 256)
        gctx[at, :] = nt(gbr[at, :], square(wo, 0)).astype(BF)
    lane = lax.broadcasted_iota(jnp.int32, (1, 128), 1)
    gate = jnp.where(lane == 2 * place[2], jnp.sum(attend_sum), 0.0)
    gate = jnp.where(lane == 2 * place[2] + 1, jnp.sum(feed_sum), gate)
    high = gate.astype(BF).astype(F32)
    rest = gate - high
    mid = rest.astype(BF).astype(F32)
    last = (rest - mid).astype(BF).astype(F32)
    row = lax.broadcasted_iota(jnp.int32, (16, 128), 0)
    base = jnp.where(row == 1, high, jnp.where(row == 2, mid, jnp.where(row == 3, last, 0.0)))
    sums[0:1, 0 : 2 * D] = jnp.zeros((1, 2 * D), F32)

    def tail(o):
        even = jnp.where(row == 0, sums[0:1, 128 * o : 128 * o + 128], base)
        other = jnp.where(row == 0, sums[0:1, 128 * o + 128 : 128 * o + 256], base)
        store(o, G_TILES - 1, even, other)

    copies, before = [], None
    blocks = [(up_grad, up_store, j) for j in range(4)] + [(out_grad, out_store, 0)]
    blocks += [(down_grad, down_store, j) for j in (3, 2, 1, 0)]
    for index, (product, put, j) in enumerate(blocks):
        val = product(j)
        if before:
            before[0](before[1], before[2])
        before = (put, j, val)
        if index == 6:
            for o in range(0, PARTS, 2):
                tail(o)
            copies += post(pl.ds(0, 8), 5)
        if index == 8:
            copies += post(pl.ds(12, 4), 7)
    down_store(0, val)
    copies += post(pl.ds(8, 4), 9)
    pltpu.make_async_copy(layer, layer_out, sems.at[0]).wait()
    for copy in copies:
        copy.wait()


def pair_back(p, parities, q_all, k_all, v_all, g_all, lse, dq_t, dk_acc, dv_acc, firsts, buffers):
    k_t, s0, s1, g0, g1, p0, p1, d0, d1 = buffers
    scores, grads, probs, diffs = (s0, s1), (g0, g1), (p0, p1), (d0, d1)
    steps = [(parity, r) for parity in parities for r in range(4)]
    lanes = pl.ds(pl.multiple_of(p * 128, 128), 128)
    q_in, k_in = q_all.at[pl.ds(2 * p, 2)], k_all.at[pl.ds(2 * p, 2)]
    for parity in parities:
        k_t[parity] = k_in[parity].T

    def mine(block, i):
        return jnp.where(half_of(steps[i][0], (256, 128)), block, jnp.zeros_like(block))

    def score(i):
        parity, r = steps[i]
        qa = q_in[parity, r * 256 : r * 256 + 256]
        ga = mine(g_all[r * 256 : r * 256 + 256, lanes], i)

        def part(c):
            scores[i % 2][c : c + BIG] = nt(k_in[parity, c : c + BIG], qa)

        def grad(c):
            grads[i % 2][c : c + BIG] = nt(v_all[c : c + BIG, lanes], ga)

        return [task for c in range(0, ROWS, BIG) for task in (partial(part, c), partial(grad, c))]

    def soften(i):
        parity, r = steps[i]
        s, g, out, diff = scores[i % 2], grads[i % 2], probs[i % 2], diffs[i % 2]
        logs = lse[pl.ds(2 * p + parity, 1), r * 256 : r * 256 + 256]
        state = {}

        def power(c):
            e = jnp.exp(s[c : c + CHUNK] - logs)
            s[c : c + CHUNK] = e
            out[c : c + CHUNK] = e.astype(BF)
            part = jnp.sum((e * g[c : c + CHUNK]).reshape(-1, 8, 256), axis=0)
            state["inner"] = state["inner"] + part if c else part
            if c == ROWS - CHUNK:
                state["inner"] = jnp.sum(state["inner"], axis=0, keepdims=True)

        def minus(c):
            diff[c : c + CHUNK] = (s[c : c + CHUNK] * (g[c : c + CHUNK] - state["inner"])).astype(BF)

        at = range(0, ROWS, CHUNK)
        return [(5.5, partial(power, c)) for c in at] + [(2.5, partial(minus, c)) for c in at]

    def collect(i):
        parity, r = steps[i]
        rows = slice(64 * parity, 64 * parity + 64)
        at = slice(r * 256, r * 256 + 256)
        qz, gz = mine(q_in[parity, at], i), mine(g_all[at, lanes], i)
        total = []

        def part(c):
            total.append(nn(k_t[parity, rows, c : c + 256], diffs[i % 2][c : c + 256]))
            if c == ROWS - 256:
                dq_t[rows, r * 256 : r * 256 + 256] = ((total[0] + total[1]) + (total[2] + total[3])) * 0.125

        def add(acc, first, ref, z, c):
            val = nn(ref[c : c + BIG], z)
            base = acc if i else first
            acc[c : c + BIG] = val if base is None else base[c : c + BIG] + val

        tasks = []
        for c in range(0, ROWS, 256):
            if c % BIG == 0:
                tasks += [partial(add, dv_acc, firsts[1], probs[i % 2], gz, c), partial(add, dk_acc, firsts[0], diffs[i % 2], qz, c)]
            tasks += [partial(part, c)]
        return tasks

    for task in score(0):
        task()
    last = len(steps) - 1
    for i in range(last + 2):
        later = (score(i + 1) if i < last else []) + (collect(i - 1) if i else [])
        mix(soften(i) if i <= last else [], later)


def back_first_body(q_all, k_all, v_all, g_all, lse, dq_t, dk_acc, dv_acc, *buffers):
    pair_back(0, (0,), q_all, k_all, v_all, g_all, lse, dq_t, dk_acc, dv_acc, (None, None), buffers)


def back_body(place, q_all, k_all, v_all, g_all, lse, x_t, dq_first, dk_first, dv_first, *refs):
    (dq_out, dk_out, dv_out, keep, send), refs = refs[:5], refs[5:]
    dq_t, dk_acc, dv_acc, sums, *buffers = refs
    odd = place[1] == 1

    def finish(p):
        out = pl.ds(pl.multiple_of(p * 128, 128), 128)
        dq = dq_t[...].astype(BF).T
        dk = dk_acc[...].astype(BF)
        dv = dv_acc[...].astype(BF)
        dq_out[:, out] = dq
        dk_out[:, out] = dk
        dv_out[:, out] = dv
        val = nn(x_t[...], jnp.concatenate([dq, dk, dv, dv], axis=1))
        sums[pl.ds(p, 1), :] = val[D : D + 1, 0:128]
        sums[pl.ds(4 + p, 1), :] = val[D : D + 1, 256:384]
        for index in range(3):
            for o in range(0, 8, 2):
                for i in range(4):
                    col, top = slice(128 * index, 128 * index + 128), 64 * o + 16 * i
                    even, other = val[top : top + 16, col], val[top + 64 : top + 80, col]
                    at = pl.ds(pl.multiple_of(SHARE * p + 64 * (4 * index + o // 2) + 16 * i, 16), 16)
                    keep[at] = jnp.where(odd, other, even)
                    send[at] = jnp.where(odd, even, other)

    def pair(p, _):
        pair_back(p, (0, 1), q_all, k_all, v_all, g_all, lse, dq_t, dk_acc, dv_acc, (None, None), buffers)
        finish(p)
        return 0

    dq_t[:64] = dq_first[...]
    pair_back(0, (1,), q_all, k_all, v_all, g_all, lse, dq_t, dk_acc, dv_acc, (dk_first, dv_first), buffers)
    finish(0)
    lax.fori_loop(1, 4, pair, 0)
    row = lax.broadcasted_iota(jnp.int32, (8, 128), 0)
    even, other = jnp.zeros((8, 128), F32), jnp.zeros((8, 128), F32)
    for o in range(0, 8, 2):
        even = jnp.where(row == o // 2, sums[o : o + 1, :], even)
        other = jnp.where(row == o // 2, sums[o + 1 : o + 2, :], other)
    keep[4 * SHARE :] = jnp.where(odd, other, even)
    send[4 * SHARE :] = jnp.where(odd, even, other)


def split_row(tile):
    row = lax.broadcasted_iota(jnp.int32, tile.shape, 0)
    rest = tile[0:1] - tile[0:1].astype(BF).astype(F32)
    return jnp.where(row == 4, rest, tile)


def join_row(tile):
    row = lax.broadcasted_iota(jnp.int32, tile.shape, 0)
    whole = tile[0:1] + tile[4:5]
    return jnp.where(row == 0, whole, jnp.where(row == 4, 0.0, tile))


def feed_xy_body(place, keep, got, wo_keep, wo_got, *outs):
    size = keep.shape[1]
    for t in range(4):
        here = place[3] ^ t
        out = outs[t]
        for z in range(4):
            at = 4 * z + here
            out[size * z : size * z + size - 1] = (keep[at, : size - 1] + got[at, : size - 1].astype(F32)).astype(out.dtype)
            total = keep[at, size - 1] + join_row(got[at, size - 1].astype(F32))
            out[size * z + size - 1] = (split_row(total) if t else total).astype(out.dtype)
        out[4 * size :] = (wo_keep[here] + wo_got[here]).astype(out.dtype)


def feed_z_body(place, keep, g1, g2, g3, out0, out1, out2, out3, wo_out):
    size = out0.shape[0]
    for t, out in enumerate((out0, out1, out2, out3)):
        at = pl.ds((place[4] ^ t) * size, size - 1)
        total = keep[at] + g1[at].astype(F32) + g2[at].astype(F32) + g3[at].astype(F32)
        out[: size - 1] = total.astype(out.dtype)
        at = (place[4] ^ t) * size + size - 1
        total = keep[at]
        for g in (g1, g2, g3):
            total = total + join_row(g[at].astype(F32))
        out[size - 1] = (split_row(total) if t else total).astype(out.dtype)
    at = slice(4 * size, 4 * size + 16)
    wo_out[...] = keep[at] + g1[at].astype(F32) + g2[at].astype(F32) + g3[at].astype(F32)


def square_xy_body(place, keep, got, *outs):
    for t in range(4):
        here = place[3] ^ t
        out = outs[t]
        for z in range(3):
            for p in range(4):
                rows = pl.ds(pl.multiple_of(SHARE * p + 64 * (4 * z + here), 64), 64)
                total = keep[rows] + got[rows]
                out[16 * z + 4 * p : 16 * z + 4 * p + 4] = total.reshape(4, 16, 128).astype(out.dtype)
        row = lax.broadcasted_iota(jnp.int32, (16, 128), 0)
        total = keep[pl.ds(4 * SHARE + here, 1)] + got[pl.ds(4 * SHARE + here, 1)]
        total = jnp.where(row == 0, total, 0.0)
        out[48] = (split_row(total) if t else total).astype(out.dtype)


def square_z_body(place, keep, g1, g2, g3, wo, out0, out1, out2, out3, whole):
    for z in range(3):
        at = slice(16 * z, 16 * z + 16)
        whole[z, :16] = keep[at] + g1[at].astype(F32) + g2[at].astype(F32) + g3[at].astype(F32)
        whole[z + 1, 16] = jnp.zeros((16, 128), F32)
    whole[3, :16] = wo[...]
    total = keep[48]
    for g in (g1, g2, g3):
        total = total + join_row(g[48].astype(F32))
    whole[0, 16] = total
    for t, out in enumerate((out0, out1, out2, out3)):
        at = place[4] ^ t
        out[:16] = whole[at, :16].astype(out.dtype)
        out[16] = (split_row(whole[at, 16]) if t else whole[at, 16]).astype(out.dtype)


def input_body(gm, dq, dk, dv, w, out):
    for r in range(4):
        at = slice(256 * r, 256 * r + 256)
        total = gm[at, :]
        for index in range(3):
            total = total + nt((dq, dk, dv)[index][at, :], square(w, index))
        out[at, :] = total


def to_columns(flat, rows):
    return flat.reshape(rows // 16, 16, -1, 128).transpose(2, 0, 1, 3).reshape(-1, 16, 128)


def from_columns(tiles, rows):
    return tiles.reshape(-1, rows // 16, 16, 128).transpose(1, 2, 0, 3).reshape(-1)


def swap(x, n, bit):
    return lax.ppermute(x, AXES, [(i, i ^ bit) for i in range(n)])


def small(body, outs, args, scratch=()):
    ins = [SMEM if arg.dtype == jnp.int32 else VMEM for arg in args]
    size = sum(arg.size for arg in args)
    return call(body, outs, ins, scratch, 2 * size, 6 * size, 16)(*args)


def blocks_of(*shape):
    return [(shape + (16, 128), F32)] + [(shape + (16, 128), BF)] * 3


def hop(parts, n, step):
    return [parts[0]] + [swap(part, n, step * t) for t, part in enumerate(parts) if t]


def tie(values, after):
    return lax.optimization_barrier((values, after))[0]


def along_z(own, n):
    return jnp.stack([own] + [swap(own, n, 8 * z) for z in (1, 2, 3)])


def along_xy(stack, n):
    return [stack] + [swap(stack, n, 2 * xy) for xy in (1, 2, 3)]


def across(chips, n):
    return chips + [swap(part, n, 1) for part in chips]


def pack_square_body(flat, biases, out, wide):
    wide[...] = flat[...].astype(F32)
    for j in range(4):
        for i in range(4):
            out[4 * j + i] = wide[pl.ds(64 * i + j, 16, stride=4), :].astype(BF)
    row = lax.broadcasted_iota(jnp.int32, (16, 128), 0)
    out[16] = jnp.where(row == 0, biases[...].astype(F32), 0.0).astype(BF)


def pack_feed_body(place, flat, out, wide):
    wide[...] = flat[...].astype(F32)

    @pl.when(place[0] < PARTS // 2)
    def _():
        for j in range(16):
            for i in range(2):
                out[2 * j + i] = wide[pl.ds(256 * i + j, 16, stride=16), :].astype(BF)

    @pl.when(place[0] >= PARTS // 2)
    def _():
        for j in range(4):
            for i in range(8):
                out[8 * j + i] = wide[pl.ds(64 * i + j, 16, stride=4), :].astype(BF)


def copy_body(ref, out):
    for i in range(5):
        out[i] = ref[i]


def added(keep, gots, at):
    total = keep[at]
    for g in gots:
        total = total + g[at].astype(F32)
    return total


def added_tail(keep, gots, at):
    total = keep[at]
    for g in gots:
        total = total + join_row(g[at].astype(F32))
    return total


def finish_feed_body(place, keep, f1, f2, f3, ff, tail):
    gots = (f1, f2, f3)

    @pl.when(place[0] < PARTS // 2)
    def _():
        for j in range(16):
            for i in range(2):
                ff[pl.ds(256 * i + j, 16, stride=16), :] = added(keep, gots, 2 * j + i)

    @pl.when(place[0] >= PARTS // 2)
    def _():
        for j in range(4):
            for i in range(8):
                ff[pl.ds(64 * i + j, 16, stride=4), :] = added(keep, gots, 8 * j + i)

    tail[...] = added_tail(keep, gots, F_TILES)


def finish_square_body(place, keep, a1, a2, a3, tail, att, bias, gate):
    gots = (a1, a2, a3)
    for j in range(4):
        for i in range(4):
            att[pl.ds(64 * i + j, 16, stride=4), :] = added(keep, gots, 4 * j + i)
    bias[...] = jnp.where(place[0] < 8, added_tail(keep, gots, 16)[0:1], tail[0:1])
    gates = tail[1:2] + tail[2:3] + tail[3:4]
    lane = lax.broadcasted_iota(jnp.int32, (1, 128), 1)
    for g in range(2):
        gate[g] = jnp.sum(jnp.where((lane < 2 * PARTS) & (lane % 2 == g), gates, 0.0))


def own_pieces(attention, feedforward, biases, upper, parts):
    tail = jnp.pad(biases.reshape(1, 1, 128), ((0, 0), (0, 15), (0, 0)))
    own_a = jnp.concatenate([to_columns(attention, 4 * D // parts), tail], axis=0)
    up = to_columns(feedforward, 2 * D // parts)
    down = to_columns(feedforward, 2 * FF // parts)
    return own_a, jnp.where(upper, up, down)


def pieces_any(attention, feedforward, biases):
    full = [lax.all_gather(x, AXES, axis=0, tiled=True).reshape(PARTS, -1) for x in (attention, feedforward, biases)]
    upper = jnp.arange(PARTS) < PARTS // 2
    a, f = jax.vmap(lambda *x: own_pieces(*x, PARTS))(*full, upper)
    a, f = a.reshape((4, 4, 2) + a.shape[1:]), f.reshape((4, 4, 2) + f.shape[1:])

    return [[x[:, xy, c] for c in range(2) for xy in range(4)] for x in (a, f)]


def local(direct, tokens, cotangent, attention, feedforward, biases, gates, counts, lengths):
    me = lax.axis_index(AXES)
    n = PARTS
    row = (ROWS, D)

    def prepare(counts):
        *masks, x_t = call(
            prepare_body,
            [((2, ROWS, 128), BF), ((2, ROWS, 128), BF), ((D + 16, ROWS), BF)],
            [SMEM, SMEM, VMEM], [], 1000, 1000, 16,
        )(counts, lengths, tokens)
        return masks, x_t

    if direct:
        place = jnp.stack([me, me % 2, me, (me // 2) % 4, me // 8]).astype(jnp.int32)
        (own_a,) = small(
            pack_square_body, [((A_TILES, 16, 128), BF)], (attention.reshape(-1, 128), biases.reshape(1, 128)), [((256, 128), F32)]
        )
        (own_f,) = small(
            pack_feed_body, [((F_TILES, 16, 128), BF)], (place, feedforward.reshape(-1, 128)), [((512, 128), F32)]
        )
        stack_a = along_z(own_a, n)
        far = [swap(own_f, n, 16), swap(own_f, n, 24)]
        chips_a = along_xy(stack_a, n)
        near = swap(own_f, n, 8)
        far, near, place, counts = lax.optimization_barrier((far, near, place, counts))
        masks, x_t = prepare(counts)
        (place,) = call(copy_body, [((5,), jnp.int32, SMEM)], [SMEM], [], 8 << 30, 1000, 16)(place)
        stack_f = jnp.stack([own_f, near] + far)
        chips_a, stack_f, place, masks = lax.optimization_barrier((chips_a, stack_f, place, masks))
        ga_all = across(chips_a, n)
        chips_f = along_xy(stack_f, n)
    else:
        masks, x_t = prepare(counts)
        ga_all, gf_all = pieces_any(attention, feedforward, biases)
        place = jnp.zeros((5,), jnp.int32)
    row = (ROWS, D)
    q, k, v, w, bias = call(
        project_body,
        [((H, ROWS, 128), BF)] * 2 + [(row, BF), ((PARTS, A_TILES, 16, 128), BF), ((1, 8 * D), F32)],
        [SMEM] + [VMEM] * 11, [], 1000, 1000, 20,
    )(place, tokens, *masks, *ga_all)
    ctx, ctx_t, lse = call(
        attend_body,
        [(row, BF), ((D + 16, ROWS), BF), ((8, ROWS), F32)],
        [VMEM] * 3,
        [((128, ROWS), BF), ((128, ROWS), F32)] + [((ROWS, 256), F32)] * 2 + [((ROWS, 256), BF)] * 2,
        1000, 1000, 20,
    )(q, k, v)
    branch, low, low_t, gs = call(
        branch_body,
        [(row, F32), (row, BF), ((D + 16, ROWS), BF), (row, BF)],
        [SMEM] + [VMEM] * 5, [], 1000, 1000, 20,
    )(gates, tokens, cotangent, ctx, w, bias)
    if direct:
        other = swap(tie(chips_f[0], ctx), n, 1)
        chips_f, other, branch = lax.optimization_barrier((chips_f, other, branch))
        gf_all = chips_f + [other] + [swap(part, n, 1) for part in chips_f[1:]]
    layer, gm, gctx, ff_keep, ff_send, wo_keep, wo_send = call(
        feed_body,
        [(row, BF, ANY), (row, F32), (row, BF)]
        + [((n // 2, G_TILES, 16, 128), F32, ANY), ((n // 2, G_TILES, 16, 128), BF, ANY)]
        + [((4, 16, 16, 128), F32)] * 2,
        [SMEM, SMEM] + [VMEM] * 17,
        [((PARTS, F_TILES, 16, 128), BF), (row, BF),
         ((FF + 16, ROWS), BF), ((ROWS, FF), BF)]
        + [((256, D), F32)] * 4 + [((256, FF), BF)] + [((256, D), F32)] * 2 + [((1, 8 * D), F32)]
        + [(row, BF), ((n // 2, G_TILES, 16, 128), F32), ((n // 2, G_TILES, 16, 128), BF), DMA((16,))],
        16 << 30, 30 << 20, 32,
    )(place, gates, tokens, cotangent, branch, low, low_t, gs, ctx_t, w, bias, *gf_all)

    half, whole = (ROWS // 16, ROWS), (128, ROWS)
    buffers = [((2, 128, ROWS), BF)] + [((ROWS, 256), F32)] * 4 + [((ROWS, 256), BF)] * 4
    sums = [((ROWS, 128), F32)] * 2
    barrier = lax.optimization_barrier
    if direct:
        got, wo_got = swap(ff_send, n, 1), swap(wo_send, n, 1)
    begun = call(
        back_first_body, [(half, F32)] + sums, [VMEM] * 5, buffers, 1000, 1000, 28
    )(q, k, v, gctx, lse)
    if direct:
        got, wo_got, begun = barrier((got, wo_got, begun))
        parts = small(feed_xy_body, blocks_of(4 * G_TILES + 16), (place, ff_keep, got, wo_keep, wo_got))
        q, parts = barrier((q, parts))
        ff_got = hop(parts, n, 2)
    *grads, keep, send = call(
        back_body,
        [(row, BF)] * 3 + [((4 * SHARE + 8, 128), F32)] * 2,
        [SMEM] + [VMEM] * 9,
        [(whole, F32)] + sums + [((8, 128), F32)] + buffers,
        1000, 1000, 28,
    )(place, q, k, v, gctx, lse, x_t, *begun)
    if direct:
        got = swap(send, n, 1)
    (input_grad,) = call(
        input_body, [(row, F32)], [VMEM] * 5, [], 32 << 30, 1000, 24
    )(gm, *grads, w)
    if direct:
        got, input_grad, ff_got = barrier((got, input_grad, ff_got))
        parts = small(square_xy_body, blocks_of(49), (place, keep, got))
        ff_got, parts = barrier((ff_got, parts))
        got = hop(parts, n, 2)
        *ff_parts, wo = small(feed_z_body, blocks_of(G_TILES) + [((16, 16, 128), F32)], (place, *ff_got))
        ff_got = hop(ff_parts, n, 8)
        got, ff_parts = barrier((got, ff_parts))
    if direct:
        parts = small(square_z_body, blocks_of(17), (place, *got, wo), [((4, 17, 16, 128), F32)])
        got = hop(parts, n, 8)
        ff_grad, tail = call(
            finish_feed_body, [((512, 128), F32), ((16, 128), F32)], [SMEM] + [VMEM] * 4, [], 1000, 1000, 16,
        )(place, *ff_got)
        got, tail = barrier((got, tail))
        att_grad, bias_grad, gate_grad = call(
            finish_square_body,
            [((256, 128), F32), ((1, 128), F32), ((2,), F32, SMEM)],
            [SMEM] + [VMEM] * 5, [], 1000, 1000, 16,
        )(place, *got, tail)
        att_grad, ff_grad, bias_grad = att_grad.reshape(-1), ff_grad.reshape(-1), bias_grad.reshape(-1)
        return layer, input_grad, att_grad, ff_grad, bias_grad, gate_grad

    def owners(keep, send):
        return jnp.stack([keep, send], axis=1).reshape((-1,) + keep.shape[1:])

    def reduce(flat):
        return lax.psum_scatter(flat.reshape(-1), AXES, scatter_dimension=0, tiled=True)

    mail = ff_send.astype(F32)
    mail = mail.at[:, F_TILES, 0].add(mail[:, F_TILES, 4])
    both = owners(ff_keep, mail)
    up = jax.vmap(lambda t: from_columns(t, 2 * D // n))(both[: n // 2, :F_TILES]).reshape(-1)
    down = jax.vmap(lambda t: from_columns(t, 2 * FF // n))(both[n // 2 :, :F_TILES]).reshape(-1)
    ff_grad = reduce(jnp.concatenate([up, down]))
    tail = both[0, F_TILES]
    gate_grad = lax.psum((tail[1] + tail[2] + tail[3])[:2], AXES)
    bias_grad = owners(keep[4 * SHARE : 4 * SHARE + 4], send[4 * SHARE : 4 * SHARE + 4])
    bias_grad = jnp.concatenate([bias_grad, both[8:, F_TILES, 0]])
    both = jnp.stack([x[: 4 * SHARE].reshape(4, 12, 4, 16, 128) for x in (keep, send)], axis=2)
    both = both.reshape(4, 24, 4, 16, 128).transpose(1, 0, 2, 3, 4)
    both = jnp.concatenate([both.reshape(24, 16, 16, 128), owners(wo_keep, wo_send)])
    att_grad = jax.vmap(lambda t: from_columns(t, 4 * D // n))(both)
    return layer, input_grad, reduce(att_grad), ff_grad, reduce(bias_grad), gate_grad


def solution(mesh):
    direct = dict(mesh.shape) == {"dp": 8, "fsdp": 4}
    both = P(AXES)
    rows = P(AXES, None)
    return jax.shard_map(
        partial(local, direct),
        mesh=mesh,
        in_specs=(rows, rows, both, both, both, P(), rows, rows),
        out_specs=(rows, rows, both, both, both, P()),
        check_vma=False,
    )
```

```python
from functools import partial

import jax
import jax.numpy as jnp
from jax import lax
from jax.experimental import pallas as pl
from jax.experimental.pallas import tpu as pltpu
from jax.sharding import PartitionSpec as P

D = 512
H = 8
HD = 64
FF = 2048
ROWS = 1024
SLOTS = 8
SHORT = 128
MID = 512
LONG = 1024
AXES = ("dp", "fsdp")
PARTS = 32
A_TILES = 17
F_TILES = 32
G_TILES = 33
BF = jnp.bfloat16
F32 = jnp.float32
CHUNK = 64
SHARE = 12 * 64
BIG = 512
VMEM = pl.BlockSpec(memory_space=pltpu.VMEM)
SMEM = pl.BlockSpec(memory_space=pltpu.SMEM)
ANY = pl.BlockSpec(memory_space=pl.ANY)
DMA = pltpu.SemaphoreType.DMA


def nn(a, b):
    return lax.dot_general(a, b, (((1,), (0,)), ((), ())), preferred_element_type=F32)


def nt(a, b):
    return lax.dot_general(a, b, (((1,), (1,)), ((), ())), preferred_element_type=F32)


def call(body, outs, ins, scratch, flops, moved, limit, grid=None):
    return pl.pallas_call(
        body,
        out_shape=[jax.ShapeDtypeStruct(o[0], o[1]) for o in outs],
        grid=grid or (),
        in_specs=ins,
        out_specs=[o[2] if len(o) > 2 else VMEM for o in outs],
        scratch_shapes=[pltpu.VMEM(*s) if isinstance(s, tuple) else s for s in scratch],
        compiler_params=pltpu.CompilerParams(vmem_limit_bytes=limit << 20),
        cost_estimate=pl.CostEstimate(flops=flops, bytes_accessed=moved, transcendentals=0),
    )


def slot_masks(counts, lengths, keys_out, rows_out):
    lane = lax.broadcasted_iota(jnp.int32, (1, 128), 1)
    slot = lane & 63
    longs, mids, shorts = counts[0, 2], counts[0, 1], counts[0, 0]
    in_long = jnp.minimum(slot, longs)
    in_mid = jnp.clip(slot - longs, 0, mids)
    in_short = jnp.clip(slot - longs - mids, 0, shorts)
    start = in_long * LONG + in_mid * MID + in_short * SHORT
    size = jnp.where(
        slot < longs,
        LONG,
        jnp.where(slot < longs + mids, MID, jnp.where(slot < longs + mids + shorts, SHORT, 0)),
    )
    valid = jnp.zeros((1, 128), jnp.int32)
    for s in range(SLOTS):
        valid = jnp.where(slot == s, lengths[0, s], valid)
    row = lax.broadcasted_iota(jnp.int32, (ROWS, 128), 0)
    member = (row >= start) & (row < start + size)
    usable = (row >= start) & (row < start + valid)
    for parity in range(2):
        here = (slot < SLOTS) & ((lane >= 64) if parity == 0 else (lane < 64))
        rows_out[parity] = jnp.where(here & member, 1.0, 0.0).astype(BF)
        keys_out[parity] = jnp.where(here & jnp.logical_not(usable), -1e30, 0.0).astype(BF)


def prepare_body(counts, lengths, tok, keys_mask, rows_mask, x_t):
    slot_masks(counts, lengths, keys_mask, rows_mask)
    x_t[:D] = tok[...].T
    x_t[D:] = jnp.ones((16, ROWS), BF)


def half_of(parity, shape):
    lane = lax.broadcasted_iota(jnp.int32, shape, len(shape) - 1)
    return (lane < 64) if parity == 0 else (lane >= 64)


def assemble(pieces, dest, me):
    for c in range(2):
        for xy in range(4):
            for z in range(4):
                dest[(8 * z + 2 * xy + c) ^ me] = pieces[4 * c + xy][z]


def columns(ref, owners, tiles, each):
    parts = []
    for t in range(tiles.start, tiles.stop, each):
        part = ref[owners, t : t + each]
        parts.append(part.reshape(part.shape[0] * each * 16, 128))
    return jnp.concatenate(parts, axis=1)


def square(ref, index):
    return columns(ref, slice(8 * index, 8 * index + 8), slice(0, 16), 4)


def project_body(place, tok, keys_mask, rows_mask, *refs):
    pieces, (q_out, k_out, v_out, w_out, bias_out) = refs[:8], refs[8:]
    assemble(pieces, w_out, place[0])
    for o in range(PARTS):
        bias_out[0:1, 128 * o : 128 * o + 128] = w_out[o, A_TILES - 1].astype(F32)[0:1]
    for r in range(4):
        at = slice(256 * r, 256 * r + 256)
        x = tok[at, :]
        q = (nn(x, square(w_out, 0)) + bias_out[0:1, 0:D]).astype(BF)
        q = (q.astype(F32) * 0.125).astype(BF)
        k = nn(x, square(w_out, 1)).astype(BF)
        v_out[at, :] = (nn(x, square(w_out, 2)) + bias_out[0:1, D : 2 * D]).astype(BF)
        for h in range(H):
            mine = half_of(h % 2, (256, 128))
            lanes = slice(h // 2 * 128, h // 2 * 128 + 128)
            q_out[h, at] = jnp.where(mine, q[:, lanes], rows_mask[h % 2, at])
            k_out[h, at] = jnp.where(mine, k[:, lanes], keys_mask[h % 2, at])


def attend_body(q_all, k_all, v_all, ctx_out, ctx_t_out, lse_out, values_t, ctx_t, s0, s1, p0, p1):
    def pair(p, _):
        attend_pair(
            p, q_all.at[pl.ds(2 * p, 2)], k_all.at[pl.ds(2 * p, 2)], v_all, ctx_out, ctx_t_out, lse_out, values_t, ctx_t,
            s0, s1, p0, p1,
        )
        return 0

    lax.fori_loop(0, 4, pair, 0)
    ctx_t_out[D:] = jnp.ones((16, ROWS), BF)


def attend_pair(p, q_in, k_in, v_all, ctx_out, ctx_t_out, lse_out, values_t, ctx_t, s0, s1, p0, p1):
    lanes = pl.ds(pl.multiple_of(p * 128, 128), 128)
    scores, probs = (s0, s1), (p0, p1)
    values_t[...] = v_all[:, lanes].T
    steps = [(parity, r) for parity in range(2) for r in range(4)]

    def score(i):
        parity, r = steps[i]

        def part(c):
            scores[i % 2][c : c + 256] = nt(k_in[parity, c : c + 256], q_in[parity, r * 256 : r * 256 + 256])

        return [partial(part, c) for c in range(0, ROWS, 256)]

    def collect(i):
        parity, r = steps[i]
        rows = slice(64 * parity, 64 * parity + 64)
        total = []

        def part(c):
            total.append(nn(values_t[rows, c : c + 256], probs[i % 2][c : c + 256]))
            if c == ROWS - 256:
                ctx_t[rows, r * 256 : r * 256 + 256] = (total[0] + total[1]) + (total[2] + total[3])

        return [partial(part, c) for c in range(0, ROWS, 256)]

    def soften(i):
        parity, r = steps[i]
        s, out = scores[i % 2], probs[i % 2]
        state = {}

        def peak(c):
            part = jnp.max(s[c : c + CHUNK].reshape(-1, 8, 256), axis=0)
            state["top"] = jnp.maximum(state["top"], part) if c else part
            if c == ROWS - CHUNK:
                state["top"] = jnp.max(state["top"], axis=0, keepdims=True)

        def power(c):
            e = jnp.exp(s[c : c + CHUNK] - state["top"])
            s[c : c + CHUNK] = e
            part = jnp.sum(e.reshape(-1, 8, 256), axis=0)
            state["mass"] = state["mass"] + part if c else part
            if c == ROWS - CHUNK:
                mass = jnp.sum(state["mass"], axis=0, keepdims=True)
                lse_out[pl.ds(2 * p + parity, 1), r * 256 : r * 256 + 256] = state["top"] + jnp.log(mass)
                state["share"] = 1.0 / mass

        def share(c):
            out[c : c + CHUNK] = (s[c : c + CHUNK] * state["share"]).astype(BF)

        at = range(0, ROWS, CHUNK)
        return [(1, partial(peak, c)) for c in at] + [(3, partial(power, c)) for c in at] + [
            (1.5, partial(share, c)) for c in at
        ]

    for task in score(0):
        task()
    for i in range(9):
        later = (score(i + 1) if i < 7 else []) + (collect(i - 1) if i else [])
        mix(soften(i) if i < 8 else [], later)
    low = ctx_t[...].astype(BF)
    ctx_t_out[lanes, :] = low
    ctx_out[:, lanes] = low.T


def mix(vector, matrix):
    whole = sum(weight for weight, _ in vector) or 1
    done, given = 0, 0
    for weight, task in vector:
        while given < len(matrix) and given * whole <= done * len(matrix):
            matrix[given]()
            given += 1
        task()
        done += weight
    for task in matrix[given:]:
        task()


def branch_body(gates, tok, cot, ctx, w, bias, branch, low, low_t, gs):
    wo = square(w, 3)
    for r in range(4):
        at = slice(256 * r, 256 * r + 256)
        out = nn(ctx[at, :], wo) + bias[0:1, 2 * D : 3 * D]
        branch[at, :] = out
        low[at, :] = (tok[at, :].astype(F32) + gates[0] * out).astype(BF)
        gs[at, :] = (gates[1] * cot[at, :].astype(F32)).astype(BF)
    low_t[:D] = low[...].T
    low_t[D:] = jnp.ones((16, ROWS), BF)


def feed_body(place, gates, tok, cot, branch, low_all, low_t, gs_all, ctx_t, w_in, bias, *refs):
    pieces, refs = refs[:8], refs[8:]
    (layer_out, gm, gctx, keep_out, send_out, wo_keep, wo_send) = refs[:7]
    (w, gbr, active_t, gh_all, v0, v1, b0, b1, active, second, gmid, sums) = refs[7:19]
    (layer, keep, send, sems) = refs[19:]
    values, backs = (v0, v1), (b0, b1)
    wo = w_in.at[24:32]
    assemble(pieces, w, place[0])

    def rows_of(r):
        return pl.ds(pl.multiple_of(r * 256, 256), 256)

    ga, gf = gates[0], gates[1]
    c1 = 0.7978845608028654
    c2 = 0.044715
    active_t[FF:] = jnp.ones((16, ROWS), BF)

    def w_up(j):
        return columns(w, slice(0, 16), slice(8 * j, 8 * j + 8), 2)

    def w_down(j):
        return columns(w, slice(16 + 4 * j, 20 + 4 * j), slice(0, 32), 8)

    def rows(r, carry):
        attend_sum, feed_sum = carry
        at = rows_of(r)
        low, gs = low_all[at, :], gs_all[at, :]

        def first(j):
            up, down = w_up(j), w_down(j)

            def value(n):
                values[j % 2][:, n : n + 256] = nn(low, up[:, n : n + 256])

            def back(n):
                backs[j % 2][:, n : n + 256] = nt(gs, down[n : n + 256])

            return [partial(f, n) for n in (0, 256) for f in (value, back)]

        def bend(j):
            def part(c):
                lines = slice(c, c + 32)
                cols = slice(4 * D + 512 * j, 4 * D + 512 * j + 512)
                v = values[j % 2][lines] + bias[0:1, cols]
                v2 = v * v
                t = jnp.tanh(v * (c1 + (c1 * c2) * v2))
                half = 0.5 + 0.5 * t
                act = v * half
                slope = half * (1.0 + (v - act) * (2.0 * c1 + (6.0 * c1 * c2) * v2))
                active[lines, 512 * j : 512 * j + 512] = act.astype(BF)
                gh_all[pl.ds(r * 256 + c, 32), 512 * j : 512 * j + 512] = (slope * backs[j % 2][lines]).astype(BF)

            return [(1, partial(part, c)) for c in range(0, 256, 32)]

        def then(j):
            up, down = w_up(j), w_down(j)
            cols = slice(512 * j, 512 * j + 512)

            def forward(n):
                val = nn(active[:, cols], down[:, n : n + 256])
                second[:, n : n + 256] = second[:, n : n + 256] + val if j else val

            def backward(n):
                val = nt(gh_all[at, cols], up[n : n + 256])
                gmid[:, n : n + 256] = gmid[:, n : n + 256] + val if j else val

            def turn():
                active_t[cols, at] = active[:, cols].T

            return [turn] + [partial(f, n) for n in (0, 256) for f in (forward, backward)]

        for task in first(0):
            task()
        for j in range(5):
            mix(bend(j) if j < 4 else [], (first(j + 1) if j < 3 else []) + (then(j - 1) if j else []))
        out = second[...] + bias[0:1, 3 * D : 4 * D]
        br, ct = branch[at, :], cot[at, :].astype(F32)
        layer[at, :] = (tok[at, :].astype(F32) + ga * br + gf * out).astype(BF)
        grad = ct + gmid[...]
        gm[at, :] = grad
        gb = (ga * grad).astype(BF)
        gbr[at, :] = gb
        pltpu.make_async_copy(layer.at[at], layer_out.at[at], sems.at[0]).start()
        attend_sum = attend_sum + jnp.sum(br * grad, axis=0, keepdims=True)
        feed_sum = feed_sum + jnp.sum(out * ct, axis=0, keepdims=True)
        return attend_sum, feed_sum

    zero = jnp.zeros((1, D), F32)
    attend_sum, feed_sum = lax.fori_loop(0, 4, rows, (zero, zero))
    odd = place[1] == 1

    def store(o, tile, even, other):
        keep[o // 2, tile] = jnp.where(odd, other, even)
        mail = jnp.where(odd, even, other)
        send[o // 2, tile] = (split_row(mail) if tile == G_TILES - 1 else mail).astype(BF)

    def post(slots, sem):
        copies = [
            pltpu.make_async_copy(keep.at[slots], keep_out.at[slots], sems.at[sem]),
            pltpu.make_async_copy(send.at[slots], send_out.at[slots], sems.at[sem + 1]),
        ]
        for copy in copies:
            copy.start()
        return copies

    def up_grad(j):
        return nn(low_t[...], gh_all[:, 512 * j : 512 * j + 512])

    def up_store(j, val):
        sums[0:1, 4 * D + 512 * j : 4 * D + 512 * j + 512] = val[D : D + 1]
        for o in range(0, 16, 2):
            for jj in range(4):
                for i in range(2):
                    top, col = 32 * o + 16 * i, slice(128 * jj, 128 * jj + 128)
                    store(o, 2 * (4 * j + jj) + i, val[top : top + 16, col], val[top + 32 : top + 48, col])

    def down_grad(j):
        return nn(active_t[512 * j : 512 * j + (528 if j == 3 else 512)], gs_all[...])

    def down_store(j, val):
        if j == 3:
            sums[0:1, 3 * D : 4 * D] = val[D : D + 1]
        for o in (0, 2):
            for jj in range(4):
                for i in range(8):
                    top, col = 128 * o + 16 * i, slice(128 * jj, 128 * jj + 128)
                    store(16 + 4 * j + o, 8 * jj + i, val[top : top + 16, col], val[top + 128 : top + 144, col])

    def out_grad(_):
        return nn(ctx_t[...], gbr[...])

    def out_store(_, val):
        sums[0:1, 2 * D : 3 * D] = val[D : D + 1]
        for o in range(0, 8, 2):
            for j in range(4):
                for i in range(4):
                    top, col = 64 * o + 16 * i, slice(128 * j, 128 * j + 128)
                    even, other = val[top : top + 16, col], val[top + 64 : top + 80, col]
                    wo_keep[o // 2, 4 * j + i] = jnp.where(odd, other, even)
                    wo_send[o // 2, 4 * j + i] = jnp.where(odd, even, other)

    for r in range(4):
        at = slice(256 * r, 256 * r + 256)
        gctx[at, :] = nt(gbr[at, :], square(wo, 0)).astype(BF)
    lane = lax.broadcasted_iota(jnp.int32, (1, 128), 1)
    gate = jnp.where(lane == 2 * place[2], jnp.sum(attend_sum), 0.0)
    gate = jnp.where(lane == 2 * place[2] + 1, jnp.sum(feed_sum), gate)
    high = gate.astype(BF).astype(F32)
    rest = gate - high
    mid = rest.astype(BF).astype(F32)
    last = (rest - mid).astype(BF).astype(F32)
    row = lax.broadcasted_iota(jnp.int32, (16, 128), 0)
    base = jnp.where(row == 1, high, jnp.where(row == 2, mid, jnp.where(row == 3, last, 0.0)))
    sums[0:1, 0 : 2 * D] = jnp.zeros((1, 2 * D), F32)

    def tail(o):
        even = jnp.where(row == 0, sums[0:1, 128 * o : 128 * o + 128], base)
        other = jnp.where(row == 0, sums[0:1, 128 * o + 128 : 128 * o + 256], base)
        store(o, G_TILES - 1, even, other)

    copies, before = [], None
    blocks = [(up_grad, up_store, j) for j in range(4)] + [(out_grad, out_store, 0)]
    blocks += [(down_grad, down_store, j) for j in (3, 2, 1, 0)]
    for index, (product, put, j) in enumerate(blocks):
        val = product(j)
        if before:
            before[0](before[1], before[2])
        before = (put, j, val)
        if index == 6:
            for o in range(0, PARTS, 2):
                tail(o)
            copies += post(pl.ds(0, 8), 5)
        if index == 8:
            copies += post(pl.ds(12, 4), 7)
    down_store(0, val)
    copies += post(pl.ds(8, 4), 9)
    pltpu.make_async_copy(layer, layer_out, sems.at[0]).wait()
    for copy in copies:
        copy.wait()


def pair_back(p, parities, q_all, k_all, v_all, g_all, lse, dq_t, dk_acc, dv_acc, firsts, buffers):
    k_t, s0, s1, g0, g1, p0, p1, d0, d1 = buffers
    scores, grads, probs, diffs = (s0, s1), (g0, g1), (p0, p1), (d0, d1)
    steps = [(parity, r) for parity in parities for r in range(4)]
    lanes = pl.ds(pl.multiple_of(p * 128, 128), 128)
    q_in, k_in = q_all.at[pl.ds(2 * p, 2)], k_all.at[pl.ds(2 * p, 2)]
    for parity in parities:
        k_t[parity] = k_in[parity].T

    def mine(block, i):
        return jnp.where(half_of(steps[i][0], (256, 128)), block, jnp.zeros_like(block))

    def score(i):
        parity, r = steps[i]
        qa = q_in[parity, r * 256 : r * 256 + 256]
        ga = mine(g_all[r * 256 : r * 256 + 256, lanes], i)

        def part(c):
            scores[i % 2][c : c + BIG] = nt(k_in[parity, c : c + BIG], qa)

        def grad(c):
            grads[i % 2][c : c + BIG] = nt(v_all[c : c + BIG, lanes], ga)

        return [task for c in range(0, ROWS, BIG) for task in (partial(part, c), partial(grad, c))]

    def soften(i):
        parity, r = steps[i]
        s, g, out, diff = scores[i % 2], grads[i % 2], probs[i % 2], diffs[i % 2]
        logs = lse[pl.ds(2 * p + parity, 1), r * 256 : r * 256 + 256]
        state = {}

        def power(c):
            e = jnp.exp(s[c : c + CHUNK] - logs)
            s[c : c + CHUNK] = e
            out[c : c + CHUNK] = e.astype(BF)
            part = jnp.sum((e * g[c : c + CHUNK]).reshape(-1, 8, 256), axis=0)
            state["inner"] = state["inner"] + part if c else part
            if c == ROWS - CHUNK:
                state["inner"] = jnp.sum(state["inner"], axis=0, keepdims=True)

        def minus(c):
            diff[c : c + CHUNK] = (s[c : c + CHUNK] * (g[c : c + CHUNK] - state["inner"])).astype(BF)

        at = range(0, ROWS, CHUNK)
        return [(5.5, partial(power, c)) for c in at] + [(2.5, partial(minus, c)) for c in at]

    def collect(i):
        parity, r = steps[i]
        rows = slice(64 * parity, 64 * parity + 64)
        at = slice(r * 256, r * 256 + 256)
        qz, gz = mine(q_in[parity, at], i), mine(g_all[at, lanes], i)
        total = []

        def part(c):
            total.append(nn(k_t[parity, rows, c : c + 256], diffs[i % 2][c : c + 256]))
            if c == ROWS - 256:
                dq_t[rows, r * 256 : r * 256 + 256] = ((total[0] + total[1]) + (total[2] + total[3])) * 0.125

        def add(acc, first, ref, z, c):
            val = nn(ref[c : c + BIG], z)
            base = acc if i else first
            acc[c : c + BIG] = val if base is None else base[c : c + BIG] + val

        tasks = []
        for c in range(0, ROWS, 256):
            if c % BIG == 0:
                tasks += [partial(add, dv_acc, firsts[1], probs[i % 2], gz, c), partial(add, dk_acc, firsts[0], diffs[i % 2], qz, c)]
            tasks += [partial(part, c)]
        return tasks

    for task in score(0):
        task()
    last = len(steps) - 1
    for i in range(last + 2):
        later = (score(i + 1) if i < last else []) + (collect(i - 1) if i else [])
        mix(soften(i) if i <= last else [], later)


def back_first_body(q_all, k_all, v_all, g_all, lse, dq_t, dk_acc, dv_acc, *buffers):
    pair_back(0, (0,), q_all, k_all, v_all, g_all, lse, dq_t, dk_acc, dv_acc, (None, None), buffers)


def back_body(place, q_all, k_all, v_all, g_all, lse, x_t, dq_first, dk_first, dv_first, *refs):
    (dq_out, dk_out, dv_out, keep, send), refs = refs[:5], refs[5:]
    dq_t, dk_acc, dv_acc, sums, *buffers = refs
    odd = place[1] == 1

    def finish(p):
        out = pl.ds(pl.multiple_of(p * 128, 128), 128)
        dq = dq_t[...].astype(BF).T
        dk = dk_acc[...].astype(BF)
        dv = dv_acc[...].astype(BF)
        dq_out[:, out] = dq
        dk_out[:, out] = dk
        dv_out[:, out] = dv
        val = nn(x_t[...], jnp.concatenate([dq, dk, dv, dv], axis=1))
        sums[pl.ds(p, 1), :] = val[D : D + 1, 0:128]
        sums[pl.ds(4 + p, 1), :] = val[D : D + 1, 256:384]
        for index in range(3):
            for o in range(0, 8, 2):
                for i in range(4):
                    col, top = slice(128 * index, 128 * index + 128), 64 * o + 16 * i
                    even, other = val[top : top + 16, col], val[top + 64 : top + 80, col]
                    at = pl.ds(pl.multiple_of(SHARE * p + 64 * (4 * index + o // 2) + 16 * i, 16), 16)
                    keep[at] = jnp.where(odd, other, even)
                    send[at] = jnp.where(odd, even, other)

    def pair(p, _):
        pair_back(p, (0, 1), q_all, k_all, v_all, g_all, lse, dq_t, dk_acc, dv_acc, (None, None), buffers)
        finish(p)
        return 0

    dq_t[:64] = dq_first[...]
    pair_back(0, (1,), q_all, k_all, v_all, g_all, lse, dq_t, dk_acc, dv_acc, (dk_first, dv_first), buffers)
    finish(0)
    lax.fori_loop(1, 4, pair, 0)
    row = lax.broadcasted_iota(jnp.int32, (8, 128), 0)
    even, other = jnp.zeros((8, 128), F32), jnp.zeros((8, 128), F32)
    for o in range(0, 8, 2):
        even = jnp.where(row == o // 2, sums[o : o + 1, :], even)
        other = jnp.where(row == o // 2, sums[o + 1 : o + 2, :], other)
    keep[4 * SHARE :] = jnp.where(odd, other, even)
    send[4 * SHARE :] = jnp.where(odd, even, other)


def split_row(tile):
    row = lax.broadcasted_iota(jnp.int32, tile.shape, 0)
    rest = tile[0:1] - tile[0:1].astype(BF).astype(F32)
    return jnp.where(row == 4, rest, tile)


def join_row(tile):
    row = lax.broadcasted_iota(jnp.int32, tile.shape, 0)
    whole = tile[0:1] + tile[4:5]
    return jnp.where(row == 0, whole, jnp.where(row == 4, 0.0, tile))


def feed_xy_body(place, keep, got, wo_keep, wo_got, *outs):
    size = keep.shape[1]
    for t in range(4):
        here = place[3] ^ t
        out = outs[t]
        for z in range(4):
            at = 4 * z + here
            out[size * z : size * z + size - 1] = (keep[at, : size - 1] + got[at, : size - 1].astype(F32)).astype(out.dtype)
            total = keep[at, size - 1] + join_row(got[at, size - 1].astype(F32))
            out[size * z + size - 1] = (split_row(total) if t else total).astype(out.dtype)
        out[4 * size :] = (wo_keep[here] + wo_got[here]).astype(out.dtype)


def feed_z_body(place, keep, g1, g2, g3, out0, out1, out2, out3, wo_out):
    size = out0.shape[0]
    for t, out in enumerate((out0, out1, out2, out3)):
        at = pl.ds((place[4] ^ t) * size, size - 1)
        total = keep[at] + g1[at].astype(F32) + g2[at].astype(F32) + g3[at].astype(F32)
        out[: size - 1] = total.astype(out.dtype)
        at = (place[4] ^ t) * size + size - 1
        total = keep[at]
        for g in (g1, g2, g3):
            total = total + join_row(g[at].astype(F32))
        out[size - 1] = (split_row(total) if t else total).astype(out.dtype)
    at = slice(4 * size, 4 * size + 16)
    wo_out[...] = keep[at] + g1[at].astype(F32) + g2[at].astype(F32) + g3[at].astype(F32)


def square_xy_body(place, keep, got, *outs):
    for t in range(4):
        here = place[3] ^ t
        out = outs[t]
        for z in range(3):
            for p in range(4):
                rows = pl.ds(pl.multiple_of(SHARE * p + 64 * (4 * z + here), 64), 64)
                total = keep[rows] + got[rows]
                out[16 * z + 4 * p : 16 * z + 4 * p + 4] = total.reshape(4, 16, 128).astype(out.dtype)
        row = lax.broadcasted_iota(jnp.int32, (16, 128), 0)
        total = keep[pl.ds(4 * SHARE + here, 1)] + got[pl.ds(4 * SHARE + here, 1)]
        total = jnp.where(row == 0, total, 0.0)
        out[48] = (split_row(total) if t else total).astype(out.dtype)


def square_z_body(place, keep, g1, g2, g3, wo, out0, out1, out2, out3, whole):
    for z in range(3):
        at = slice(16 * z, 16 * z + 16)
        whole[z, :16] = keep[at] + g1[at].astype(F32) + g2[at].astype(F32) + g3[at].astype(F32)
        whole[z + 1, 16] = jnp.zeros((16, 128), F32)
    whole[3, :16] = wo[...]
    total = keep[48]
    for g in (g1, g2, g3):
        total = total + join_row(g[48].astype(F32))
    whole[0, 16] = total
    for t, out in enumerate((out0, out1, out2, out3)):
        at = place[4] ^ t
        out[:16] = whole[at, :16].astype(out.dtype)
        out[16] = (split_row(whole[at, 16]) if t else whole[at, 16]).astype(out.dtype)


def input_body(gm, dq, dk, dv, w, out):
    for r in range(4):
        at = slice(256 * r, 256 * r + 256)
        total = gm[at, :]
        for index in range(3):
            total = total + nt((dq, dk, dv)[index][at, :], square(w, index))
        out[at, :] = total


def to_columns(flat, rows):
    return flat.reshape(rows // 16, 16, -1, 128).transpose(2, 0, 1, 3).reshape(-1, 16, 128)


def from_columns(tiles, rows):
    return tiles.reshape(-1, rows // 16, 16, 128).transpose(1, 2, 0, 3).reshape(-1)


def swap(x, n, bit):
    return lax.ppermute(x, AXES, [(i, i ^ bit) for i in range(n)])


def small(body, outs, args, scratch=()):
    ins = [SMEM if arg.dtype == jnp.int32 else VMEM for arg in args]
    size = sum(arg.size for arg in args)
    return call(body, outs, ins, scratch, 2 * size, 6 * size, 16)(*args)


def blocks_of(*shape):
    return [(shape + (16, 128), F32)] + [(shape + (16, 128), BF)] * 3


def hop(parts, n, step):
    return [parts[0]] + [swap(part, n, step * t) for t, part in enumerate(parts) if t]


def tie(values, after):
    return lax.optimization_barrier((values, after))[0]


def along_z(own, n):
    return jnp.stack([own] + [swap(own, n, 8 * z) for z in (1, 2, 3)])


def along_xy(stack, n):
    return [stack] + [swap(stack, n, 2 * xy) for xy in (1, 2, 3)]


def across(chips, n):
    return chips + [swap(part, n, 1) for part in chips]


def pack_square_body(flat, biases, out, wide):
    wide[...] = flat[...].astype(F32)
    for j in range(4):
        for i in range(4):
            out[4 * j + i] = wide[pl.ds(64 * i + j, 16, stride=4), :].astype(BF)
    row = lax.broadcasted_iota(jnp.int32, (16, 128), 0)
    out[16] = jnp.where(row == 0, biases[...].astype(F32), 0.0).astype(BF)


def pack_feed_body(place, flat, out, wide):
    wide[...] = flat[...].astype(F32)

    @pl.when(place[0] < PARTS // 2)
    def _():
        for j in range(16):
            for i in range(2):
                out[2 * j + i] = wide[pl.ds(256 * i + j, 16, stride=16), :].astype(BF)

    @pl.when(place[0] >= PARTS // 2)
    def _():
        for j in range(4):
            for i in range(8):
                out[8 * j + i] = wide[pl.ds(64 * i + j, 16, stride=4), :].astype(BF)


def copy_body(ref, out):
    for i in range(5):
        out[i] = ref[i]


def added(keep, gots, at):
    total = keep[at]
    for g in gots:
        total = total + g[at].astype(F32)
    return total


def added_tail(keep, gots, at):
    total = keep[at]
    for g in gots:
        total = total + join_row(g[at].astype(F32))
    return total


def finish_feed_body(place, keep, f1, f2, f3, ff, tail):
    gots = (f1, f2, f3)

    @pl.when(place[0] < PARTS // 2)
    def _():
        for j in range(16):
            for i in range(2):
                ff[pl.ds(256 * i + j, 16, stride=16), :] = added(keep, gots, 2 * j + i)

    @pl.when(place[0] >= PARTS // 2)
    def _():
        for j in range(4):
            for i in range(8):
                ff[pl.ds(64 * i + j, 16, stride=4), :] = added(keep, gots, 8 * j + i)

    tail[...] = added_tail(keep, gots, F_TILES)


def finish_square_body(place, keep, a1, a2, a3, tail, att, bias, gate):
    gots = (a1, a2, a3)
    for j in range(4):
        for i in range(4):
            att[pl.ds(64 * i + j, 16, stride=4), :] = added(keep, gots, 4 * j + i)
    bias[...] = jnp.where(place[0] < 8, added_tail(keep, gots, 16)[0:1], tail[0:1])
    gates = tail[1:2] + tail[2:3] + tail[3:4]
    lane = lax.broadcasted_iota(jnp.int32, (1, 128), 1)
    for g in range(2):
        gate[g] = jnp.sum(jnp.where((lane < 2 * PARTS) & (lane % 2 == g), gates, 0.0))


def own_pieces(attention, feedforward, biases, upper, parts):
    tail = jnp.pad(biases.reshape(1, 1, 128), ((0, 0), (0, 15), (0, 0)))
    own_a = jnp.concatenate([to_columns(attention, 4 * D // parts), tail], axis=0)
    up = to_columns(feedforward, 2 * D // parts)
    down = to_columns(feedforward, 2 * FF // parts)
    return own_a, jnp.where(upper, up, down)


def pieces_any(attention, feedforward, biases):
    full = [lax.all_gather(x, AXES, axis=0, tiled=True).reshape(PARTS, -1) for x in (attention, feedforward, biases)]
    upper = jnp.arange(PARTS) < PARTS // 2
    a, f = jax.vmap(lambda *x: own_pieces(*x, PARTS))(*full, upper)
    a, f = a.reshape((4, 4, 2) + a.shape[1:]), f.reshape((4, 4, 2) + f.shape[1:])

    return [[x[:, xy, c] for c in range(2) for xy in range(4)] for x in (a, f)]


def local(direct, tokens, cotangent, attention, feedforward, biases, gates, counts, lengths):
    me = lax.axis_index(AXES)
    n = PARTS
    row = (ROWS, D)

    def prepare(counts):
        *masks, x_t = call(
            prepare_body,
            [((2, ROWS, 128), BF), ((2, ROWS, 128), BF), ((D + 16, ROWS), BF)],
            [SMEM, SMEM, VMEM], [], 1000, 1000, 16,
        )(counts, lengths, tokens)
        return masks, x_t

    if direct:
        place = jnp.stack([me, me % 2, me, (me // 2) % 4, me // 8]).astype(jnp.int32)
        (own_a,) = small(
            pack_square_body, [((A_TILES, 16, 128), BF)], (attention.reshape(-1, 128), biases.reshape(1, 128)), [((256, 128), F32)]
        )
        (own_f,) = small(
            pack_feed_body, [((F_TILES, 16, 128), BF)], (place, feedforward.reshape(-1, 128)), [((512, 128), F32)]
        )
        stack_a = along_z(own_a, n)
        far = [swap(own_f, n, 16), swap(own_f, n, 24)]
        chips_a = along_xy(stack_a, n)
        near = swap(own_f, n, 8)
        far, near, place, counts = lax.optimization_barrier((far, near, place, counts))
        masks, x_t = prepare(counts)
        (place,) = call(copy_body, [((5,), jnp.int32, SMEM)], [SMEM], [], 8 << 30, 1000, 16)(place)
        stack_f = jnp.stack([own_f, near] + far)
        chips_a, stack_f, place, masks = lax.optimization_barrier((chips_a, stack_f, place, masks))
        ga_all = across(chips_a, n)
        chips_f = along_xy(stack_f, n)
    else:
        masks, x_t = prepare(counts)
        ga_all, gf_all = pieces_any(attention, feedforward, biases)
        place = jnp.zeros((5,), jnp.int32)
    row = (ROWS, D)
    q, k, v, w, bias = call(
        project_body,
        [((H, ROWS, 128), BF)] * 2 + [(row, BF), ((PARTS, A_TILES, 16, 128), BF), ((1, 8 * D), F32)],
        [SMEM] + [VMEM] * 11, [], 1000, 1000, 20,
    )(place, tokens, *masks, *ga_all)
    ctx, ctx_t, lse = call(
        attend_body,
        [(row, BF), ((D + 16, ROWS), BF), ((8, ROWS), F32)],
        [VMEM] * 3,
        [((128, ROWS), BF), ((128, ROWS), F32)] + [((ROWS, 256), F32)] * 2 + [((ROWS, 256), BF)] * 2,
        1000, 1000, 20,
    )(q, k, v)
    branch, low, low_t, gs = call(
        branch_body,
        [(row, F32), (row, BF), ((D + 16, ROWS), BF), (row, BF)],
        [SMEM] + [VMEM] * 5, [], 1000, 1000, 20,
    )(gates, tokens, cotangent, ctx, w, bias)
    if direct:
        own, y, x, xy = chips_f
        xy, branch = lax.optimization_barrier((xy, branch))
        own_other, xy_other = swap(tie(own, ctx), n, 1), swap(xy, n, 1)
        y, x, own_other, xy_other = lax.optimization_barrier((y, x, own_other, xy_other))
        gf_all = [own, y, x, xy, own_other, swap(y, n, 1), swap(x, n, 1), xy_other]
    layer, gm, gctx, ff_keep, ff_send, wo_keep, wo_send = call(
        feed_body,
        [(row, BF, ANY), (row, F32), (row, BF)]
        + [((n // 2, G_TILES, 16, 128), F32, ANY), ((n // 2, G_TILES, 16, 128), BF, ANY)]
        + [((4, 16, 16, 128), F32)] * 2,
        [SMEM, SMEM] + [VMEM] * 17,
        [((PARTS, F_TILES, 16, 128), BF), (row, BF),
         ((FF + 16, ROWS), BF), ((ROWS, FF), BF)]
        + [((256, D), F32)] * 4 + [((256, FF), BF)] + [((256, D), F32)] * 2 + [((1, 8 * D), F32)]
        + [(row, BF), ((n // 2, G_TILES, 16, 128), F32), ((n // 2, G_TILES, 16, 128), BF), DMA((16,))],
        16 << 30, 30 << 20, 32,
    )(place, gates, tokens, cotangent, branch, low, low_t, gs, ctx_t, w, bias, *gf_all)

    half, whole = (ROWS // 16, ROWS), (128, ROWS)
    buffers = [((2, 128, ROWS), BF)] + [((ROWS, 256), F32)] * 4 + [((ROWS, 256), BF)] * 4
    sums = [((ROWS, 128), F32)] * 2
    barrier = lax.optimization_barrier
    if direct:
        got, wo_got = swap(ff_send, n, 1), swap(wo_send, n, 1)
    begun = call(
        back_first_body, [(half, F32)] + sums, [VMEM] * 5, buffers, 1000, 1000, 28
    )(q, k, v, gctx, lse)
    if direct:
        got, wo_got, begun = barrier((got, wo_got, begun))
        parts = small(feed_xy_body, blocks_of(4 * G_TILES + 16), (place, ff_keep, got, wo_keep, wo_got))
        q, parts = barrier((q, parts))
        ff_got = hop(parts, n, 2)
    *grads, keep, send = call(
        back_body,
        [(row, BF)] * 3 + [((4 * SHARE + 8, 128), F32)] * 2,
        [SMEM] + [VMEM] * 9,
        [(whole, F32)] + sums + [((8, 128), F32)] + buffers,
        1000, 1000, 28,
    )(place, q, k, v, gctx, lse, x_t, *begun)
    if direct:
        got = swap(send, n, 1)
    (input_grad,) = call(
        input_body, [(row, F32)], [VMEM] * 5, [], 32 << 30, 1000, 24
    )(gm, *grads, w)
    if direct:
        got, input_grad, ff_got = barrier((got, input_grad, ff_got))
        parts = small(square_xy_body, blocks_of(49), (place, keep, got))
        ff_got, parts = barrier((ff_got, parts))
        got = hop(parts, n, 2)
        *ff_parts, wo = small(feed_z_body, blocks_of(G_TILES) + [((16, 16, 128), F32)], (place, *ff_got))
        ff_got = hop(ff_parts, n, 8)
        got, ff_parts = barrier((got, ff_parts))
    if direct:
        parts = small(square_z_body, blocks_of(17), (place, *got, wo), [((4, 17, 16, 128), F32)])
        got = hop(parts, n, 8)
        ff_grad, tail = call(
            finish_feed_body, [((512, 128), F32), ((16, 128), F32)], [SMEM] + [VMEM] * 4, [], 1000, 1000, 16,
        )(place, *ff_got)
        got, tail = barrier((got, tail))
        att_grad, bias_grad, gate_grad = call(
            finish_square_body,
            [((256, 128), F32), ((1, 128), F32), ((2,), F32, SMEM)],
            [SMEM] + [VMEM] * 5, [], 1000, 1000, 16,
        )(place, *got, tail)
        att_grad, ff_grad, bias_grad = att_grad.reshape(-1), ff_grad.reshape(-1), bias_grad.reshape(-1)
        return layer, input_grad, att_grad, ff_grad, bias_grad, gate_grad

    def owners(keep, send):
        return jnp.stack([keep, send], axis=1).reshape((-1,) + keep.shape[1:])

    def reduce(flat):
        return lax.psum_scatter(flat.reshape(-1), AXES, scatter_dimension=0, tiled=True)

    mail = ff_send.astype(F32)
    mail = mail.at[:, F_TILES, 0].add(mail[:, F_TILES, 4])
    both = owners(ff_keep, mail)
    up = jax.vmap(lambda t: from_columns(t, 2 * D // n))(both[: n // 2, :F_TILES]).reshape(-1)
    down = jax.vmap(lambda t: from_columns(t, 2 * FF // n))(both[n // 2 :, :F_TILES]).reshape(-1)
    ff_grad = reduce(jnp.concatenate([up, down]))
    tail = both[0, F_TILES]
    gate_grad = lax.psum((tail[1] + tail[2] + tail[3])[:2], AXES)
    bias_grad = owners(keep[4 * SHARE : 4 * SHARE + 4], send[4 * SHARE : 4 * SHARE + 4])
    bias_grad = jnp.concatenate([bias_grad, both[8:, F_TILES, 0]])
    both = jnp.stack([x[: 4 * SHARE].reshape(4, 12, 4, 16, 128) for x in (keep, send)], axis=2)
    both = both.reshape(4, 24, 4, 16, 128).transpose(1, 0, 2, 3, 4)
    both = jnp.concatenate([both.reshape(24, 16, 16, 128), owners(wo_keep, wo_send)])
    att_grad = jax.vmap(lambda t: from_columns(t, 4 * D // n))(both)
    return layer, input_grad, reduce(att_grad), ff_grad, reduce(bias_grad), gate_grad


def solution(mesh):
    direct = dict(mesh.shape) == {"dp": 8, "fsdp": 4}
    both = P(AXES)
    rows = P(AXES, None)
    return jax.shard_map(
        partial(local, direct),
        mesh=mesh,
        in_specs=(rows, rows, both, both, both, P(), rows, rows),
        out_specs=(rows, rows, both, both, both, P()),
        check_vma=False,
    )
```

```python
from functools import partial

import jax
import jax.numpy as jnp
from jax import lax
from jax.experimental import pallas as pl
from jax.experimental.pallas import tpu as pltpu
from jax.sharding import PartitionSpec as P

D = 512
H = 8
HD = 64
FF = 2048
ROWS = 1024
SLOTS = 8
SHORT = 128
MID = 512
LONG = 1024
AXES = ("dp", "fsdp")
PARTS = 32
A_TILES = 17
F_TILES = 32
G_TILES = 33
BF = jnp.bfloat16
F32 = jnp.float32
CHUNK = 64
SHARE = 12 * 64
BIG = 1024
VMEM = pl.BlockSpec(memory_space=pltpu.VMEM)
SMEM = pl.BlockSpec(memory_space=pltpu.SMEM)
ANY = pl.BlockSpec(memory_space=pl.ANY)
DMA = pltpu.SemaphoreType.DMA


def nn(a, b):
    return lax.dot_general(a, b, (((1,), (0,)), ((), ())), preferred_element_type=F32)


def nt(a, b):
    return lax.dot_general(a, b, (((1,), (1,)), ((), ())), preferred_element_type=F32)


def call(body, outs, ins, scratch, flops, moved, limit, grid=None):
    return pl.pallas_call(
        body,
        out_shape=[jax.ShapeDtypeStruct(o[0], o[1]) for o in outs],
        grid=grid or (),
        in_specs=ins,
        out_specs=[o[2] if len(o) > 2 else VMEM for o in outs],
        scratch_shapes=[pltpu.VMEM(*s) if isinstance(s, tuple) else s for s in scratch],
        compiler_params=pltpu.CompilerParams(vmem_limit_bytes=limit << 20),
        cost_estimate=pl.CostEstimate(flops=flops, bytes_accessed=moved, transcendentals=0),
    )


def slot_masks(counts, lengths, keys_out, rows_out):
    lane = lax.broadcasted_iota(jnp.int32, (1, 128), 1)
    slot = lane & 63
    longs, mids, shorts = counts[0, 2], counts[0, 1], counts[0, 0]
    in_long = jnp.minimum(slot, longs)
    in_mid = jnp.clip(slot - longs, 0, mids)
    in_short = jnp.clip(slot - longs - mids, 0, shorts)
    start = in_long * LONG + in_mid * MID + in_short * SHORT
    size = jnp.where(
        slot < longs,
        LONG,
        jnp.where(slot < longs + mids, MID, jnp.where(slot < longs + mids + shorts, SHORT, 0)),
    )
    valid = jnp.zeros((1, 128), jnp.int32)
    for s in range(SLOTS):
        valid = jnp.where(slot == s, lengths[0, s], valid)
    row = lax.broadcasted_iota(jnp.int32, (ROWS, 128), 0)
    member = (row >= start) & (row < start + size)
    usable = (row >= start) & (row < start + valid)
    for parity in range(2):
        here = (slot < SLOTS) & ((lane >= 64) if parity == 0 else (lane < 64))
        rows_out[parity] = jnp.where(here & member, 1.0, 0.0).astype(BF)
        keys_out[parity] = jnp.where(here & jnp.logical_not(usable), -1e30, 0.0).astype(BF)


def prepare_body(counts, lengths, tok, keys_mask, rows_mask, x_t):
    slot_masks(counts, lengths, keys_mask, rows_mask)
    x_t[:D] = tok[...].T
    x_t[D:] = jnp.ones((16, ROWS), BF)


def half_of(parity, shape):
    lane = lax.broadcasted_iota(jnp.int32, shape, len(shape) - 1)
    return (lane < 64) if parity == 0 else (lane >= 64)


def assemble(pieces, dest, me):
    for c in range(2):
        for xy in range(4):
            for z in range(4):
                dest[(8 * z + 2 * xy + c) ^ me] = pieces[4 * c + xy][z]


def columns(ref, owners, tiles, each):
    parts = []
    for t in range(tiles.start, tiles.stop, each):
        part = ref[owners, t : t + each]
        parts.append(part.reshape(part.shape[0] * each * 16, 128))
    return jnp.concatenate(parts, axis=1)


def square(ref, index):
    return columns(ref, slice(8 * index, 8 * index + 8), slice(0, 16), 4)


def project_body(place, tok, keys_mask, rows_mask, *refs):
    pieces, (q_out, k_out, v_out, w_out, bias_out) = refs[:8], refs[8:]
    assemble(pieces, w_out, place[0])
    for o in range(PARTS):
        bias_out[0:1, 128 * o : 128 * o + 128] = w_out[o, A_TILES - 1].astype(F32)[0:1]
    for r in range(4):
        at = slice(256 * r, 256 * r + 256)
        x = tok[at, :]
        q = (nn(x, square(w_out, 0)) + bias_out[0:1, 0:D]).astype(BF)
        q = (q.astype(F32) * 0.125).astype(BF)
        k = nn(x, square(w_out, 1)).astype(BF)
        v_out[at, :] = (nn(x, square(w_out, 2)) + bias_out[0:1, D : 2 * D]).astype(BF)
        for h in range(H):
            mine = half_of(h % 2, (256, 128))
            lanes = slice(h // 2 * 128, h // 2 * 128 + 128)
            q_out[h, at] = jnp.where(mine, q[:, lanes], rows_mask[h % 2, at])
            k_out[h, at] = jnp.where(mine, k[:, lanes], keys_mask[h % 2, at])


def attend_body(q_all, k_all, v_all, ctx_out, ctx_t_out, lse_out, values_t, ctx_t, s0, s1, p0, p1):
    def pair(p, _):
        attend_pair(
            p, q_all.at[pl.ds(2 * p, 2)], k_all.at[pl.ds(2 * p, 2)], v_all, ctx_out, ctx_t_out, lse_out, values_t, ctx_t,
            s0, s1, p0, p1,
        )
        return 0

    lax.fori_loop(0, 4, pair, 0)
    ctx_t_out[D:] = jnp.ones((16, ROWS), BF)


def attend_pair(p, q_in, k_in, v_all, ctx_out, ctx_t_out, lse_out, values_t, ctx_t, s0, s1, p0, p1):
    lanes = pl.ds(pl.multiple_of(p * 128, 128), 128)
    scores, probs = (s0, s1), (p0, p1)
    values_t[...] = v_all[:, lanes].T
    steps = [(parity, r) for parity in range(2) for r in range(4)]

    def score(i):
        parity, r = steps[i]

        def part(c):
            scores[i % 2][c : c + 256] = nt(k_in[parity, c : c + 256], q_in[parity, r * 256 : r * 256 + 256])

        return [partial(part, c) for c in range(0, ROWS, 256)]

    def collect(i):
        parity, r = steps[i]
        rows = slice(64 * parity, 64 * parity + 64)
        total = []

        def part(c):
            total.append(nn(values_t[rows, c : c + 256], probs[i % 2][c : c + 256]))
            if c == ROWS - 256:
                ctx_t[rows, r * 256 : r * 256 + 256] = (total[0] + total[1]) + (total[2] + total[3])

        return [partial(part, c) for c in range(0, ROWS, 256)]

    def soften(i):
        parity, r = steps[i]
        s, out = scores[i % 2], probs[i % 2]
        state = {}

        def peak(c):
            part = jnp.max(s[c : c + CHUNK].reshape(-1, 8, 256), axis=0)
            state["top"] = jnp.maximum(state["top"], part) if c else part
            if c == ROWS - CHUNK:
                state["top"] = jnp.max(state["top"], axis=0, keepdims=True)

        def power(c):
            e = jnp.exp(s[c : c + CHUNK] - state["top"])
            s[c : c + CHUNK] = e
            part = jnp.sum(e.reshape(-1, 8, 256), axis=0)
            state["mass"] = state["mass"] + part if c else part
            if c == ROWS - CHUNK:
                mass = jnp.sum(state["mass"], axis=0, keepdims=True)
                lse_out[pl.ds(2 * p + parity, 1), r * 256 : r * 256 + 256] = state["top"] + jnp.log(mass)
                state["share"] = 1.0 / mass

        def share(c):
            out[c : c + CHUNK] = (s[c : c + CHUNK] * state["share"]).astype(BF)

        at = range(0, ROWS, CHUNK)
        return [(1, partial(peak, c)) for c in at] + [(3, partial(power, c)) for c in at] + [
            (1.5, partial(share, c)) for c in at
        ]

    for task in score(0):
        task()
    for i in range(9):
        later = (score(i + 1) if i < 7 else []) + (collect(i - 1) if i else [])
        mix(soften(i) if i < 8 else [], later)
    low = ctx_t[...].astype(BF)
    ctx_t_out[lanes, :] = low
    ctx_out[:, lanes] = low.T


def mix(vector, matrix):
    whole = sum(weight for weight, _ in vector) or 1
    done, given = 0, 0
    for weight, task in vector:
        while given < len(matrix) and given * whole <= done * len(matrix):
            matrix[given]()
            given += 1
        task()
        done += weight
    for task in matrix[given:]:
        task()


def branch_body(gates, tok, cot, ctx, w, bias, branch, low, low_t, gs):
    wo = square(w, 3)
    for r in range(4):
        at = slice(256 * r, 256 * r + 256)
        out = nn(ctx[at, :], wo) + bias[0:1, 2 * D : 3 * D]
        branch[at, :] = out
        low[at, :] = (tok[at, :].astype(F32) + gates[0] * out).astype(BF)
        gs[at, :] = (gates[1] * cot[at, :].astype(F32)).astype(BF)
    low_t[:D] = low[...].T
    low_t[D:] = jnp.ones((16, ROWS), BF)


def feed_body(place, gates, tok, cot, branch, low_all, low_t, gs_all, ctx_t, w_in, bias, *refs):
    pieces, refs = refs[:8], refs[8:]
    (layer_out, gm, gctx, keep_out, send_out, wo_keep, wo_send) = refs[:7]
    (w, gbr, active_t, gh_all, v0, v1, b0, b1, active, second, gmid, sums) = refs[7:19]
    (layer, keep, send, sems) = refs[19:]
    values, backs = (v0, v1), (b0, b1)
    wo = w_in.at[24:32]
    assemble(pieces, w, place[0])

    def rows_of(r):
        return pl.ds(pl.multiple_of(r * 256, 256), 256)

    ga, gf = gates[0], gates[1]
    c1 = 0.7978845608028654
    c2 = 0.044715
    active_t[FF:] = jnp.ones((16, ROWS), BF)

    def w_up(j):
        return columns(w, slice(0, 16), slice(8 * j, 8 * j + 8), 2)

    def w_down(j):
        return columns(w, slice(16 + 4 * j, 20 + 4 * j), slice(0, 32), 8)

    def rows(r, carry):
        attend_sum, feed_sum = carry
        at = rows_of(r)
        low, gs = low_all[at, :], gs_all[at, :]

        def first(j):
            up, down = w_up(j), w_down(j)

            def value(n):
                values[j % 2][:, n : n + 256] = nn(low, up[:, n : n + 256])

            def back(n):
                backs[j % 2][:, n : n + 256] = nt(gs, down[n : n + 256])

            return [partial(f, n) for n in (0, 256) for f in (value, back)]

        def bend(j):
            def part(c):
                lines = slice(c, c + 32)
                cols = slice(4 * D + 512 * j, 4 * D + 512 * j + 512)
                v = values[j % 2][lines] + bias[0:1, cols]
                v2 = v * v
                t = jnp.tanh(v * (c1 + (c1 * c2) * v2))
                half = 0.5 + 0.5 * t
                act = v * half
                slope = half * (1.0 + (v - act) * (2.0 * c1 + (6.0 * c1 * c2) * v2))
                active[lines, 512 * j : 512 * j + 512] = act.astype(BF)
                gh_all[pl.ds(r * 256 + c, 32), 512 * j : 512 * j + 512] = (slope * backs[j % 2][lines]).astype(BF)

            return [(1, partial(part, c)) for c in range(0, 256, 32)]

        def then(j):
            up, down = w_up(j), w_down(j)
            cols = slice(512 * j, 512 * j + 512)

            def forward(n):
                val = nn(active[:, cols], down[:, n : n + 256])
                second[:, n : n + 256] = second[:, n : n + 256] + val if j else val

            def backward(n):
                val = nt(gh_all[at, cols], up[n : n + 256])
                gmid[:, n : n + 256] = gmid[:, n : n + 256] + val if j else val

            def turn():
                active_t[cols, at] = active[:, cols].T

            return [turn] + [partial(f, n) for n in (0, 256) for f in (forward, backward)]

        for task in first(0):
            task()
        for j in range(5):
            mix(bend(j) if j < 4 else [], (first(j + 1) if j < 3 else []) + (then(j - 1) if j else []))
        out = second[...] + bias[0:1, 3 * D : 4 * D]
        br, ct = branch[at, :], cot[at, :].astype(F32)
        layer[at, :] = (tok[at, :].astype(F32) + ga * br + gf * out).astype(BF)
        grad = ct + gmid[...]
        gm[at, :] = grad
        gb = (ga * grad).astype(BF)
        gbr[at, :] = gb
        pltpu.make_async_copy(layer.at[at], layer_out.at[at], sems.at[0]).start()
        attend_sum = attend_sum + jnp.sum(br * grad, axis=0, keepdims=True)
        feed_sum = feed_sum + jnp.sum(out * ct, axis=0, keepdims=True)
        return attend_sum, feed_sum

    zero = jnp.zeros((1, D), F32)
    attend_sum, feed_sum = lax.fori_loop(0, 4, rows, (zero, zero))
    odd = place[1] == 1

    def store(o, tile, even, other):
        keep[o // 2, tile] = jnp.where(odd, other, even)
        mail = jnp.where(odd, even, other)
        send[o // 2, tile] = (split_row(mail) if tile == G_TILES - 1 else mail).astype(BF)

    def post(slots, sem):
        copies = [
            pltpu.make_async_copy(keep.at[slots], keep_out.at[slots], sems.at[sem]),
            pltpu.make_async_copy(send.at[slots], send_out.at[slots], sems.at[sem + 1]),
        ]
        for copy in copies:
            copy.start()
        return copies

    def up_grad(j):
        return nn(low_t[...], gh_all[:, 512 * j : 512 * j + 512])

    def up_store(j, val):
        sums[0:1, 4 * D + 512 * j : 4 * D + 512 * j + 512] = val[D : D + 1]
        for o in range(0, 16, 2):
            for jj in range(4):
                for i in range(2):
                    top, col = 32 * o + 16 * i, slice(128 * jj, 128 * jj + 128)
                    store(o, 2 * (4 * j + jj) + i, val[top : top + 16, col], val[top + 32 : top + 48, col])

    def down_grad(j):
        return nn(active_t[512 * j : 512 * j + (528 if j == 3 else 512)], gs_all[...])

    def down_store(j, val):
        if j == 3:
            sums[0:1, 3 * D : 4 * D] = val[D : D + 1]
        for o in (0, 2):
            for jj in range(4):
                for i in range(8):
                    top, col = 128 * o + 16 * i, slice(128 * jj, 128 * jj + 128)
                    store(16 + 4 * j + o, 8 * jj + i, val[top : top + 16, col], val[top + 128 : top + 144, col])

    def out_grad(_):
        return nn(ctx_t[...], gbr[...])

    def out_store(_, val):
        sums[0:1, 2 * D : 3 * D] = val[D : D + 1]
        for o in range(0, 8, 2):
            for j in range(4):
                for i in range(4):
                    top, col = 64 * o + 16 * i, slice(128 * j, 128 * j + 128)
                    even, other = val[top : top + 16, col], val[top + 64 : top + 80, col]
                    wo_keep[o // 2, 4 * j + i] = jnp.where(odd, other, even)
                    wo_send[o // 2, 4 * j + i] = jnp.where(odd, even, other)

    for r in range(4):
        at = slice(256 * r, 256 * r + 256)
        gctx[at, :] = nt(gbr[at, :], square(wo, 0)).astype(BF)
    lane = lax.broadcasted_iota(jnp.int32, (1, 128), 1)
    gate = jnp.where(lane == 2 * place[2], jnp.sum(attend_sum), 0.0)
    gate = jnp.where(lane == 2 * place[2] + 1, jnp.sum(feed_sum), gate)
    high = gate.astype(BF).astype(F32)
    rest = gate - high
    mid = rest.astype(BF).astype(F32)
    last = (rest - mid).astype(BF).astype(F32)
    row = lax.broadcasted_iota(jnp.int32, (16, 128), 0)
    base = jnp.where(row == 1, high, jnp.where(row == 2, mid, jnp.where(row == 3, last, 0.0)))
    sums[0:1, 0 : 2 * D] = jnp.zeros((1, 2 * D), F32)

    def tail(o):
        even = jnp.where(row == 0, sums[0:1, 128 * o : 128 * o + 128], base)
        other = jnp.where(row == 0, sums[0:1, 128 * o + 128 : 128 * o + 256], base)
        store(o, G_TILES - 1, even, other)

    copies, before = [], None
    blocks = [(up_grad, up_store, j) for j in range(4)] + [(out_grad, out_store, 0)]
    blocks += [(down_grad, down_store, j) for j in (3, 2, 1, 0)]
    for index, (product, put, j) in enumerate(blocks):
        val = product(j)
        if before:
            before[0](before[1], before[2])
        before = (put, j, val)
        if index == 6:
            for o in range(0, PARTS, 2):
                tail(o)
            copies += post(pl.ds(0, 8), 5)
        if index == 8:
            copies += post(pl.ds(12, 4), 7)
    down_store(0, val)
    copies += post(pl.ds(8, 4), 9)
    pltpu.make_async_copy(layer, layer_out, sems.at[0]).wait()
    for copy in copies:
        copy.wait()


def pair_back(p, parities, q_all, k_all, v_all, g_all, lse, dq_t, dk_acc, dv_acc, firsts, buffers):
    k_t, s0, s1, g0, g1, p0, p1, d0, d1 = buffers
    scores, grads, probs, diffs = (s0, s1), (g0, g1), (p0, p1), (d0, d1)
    steps = [(parity, r) for parity in parities for r in range(4)]
    lanes = pl.ds(pl.multiple_of(p * 128, 128), 128)
    q_in, k_in = q_all.at[pl.ds(2 * p, 2)], k_all.at[pl.ds(2 * p, 2)]
    for parity in parities:
        k_t[parity] = k_in[parity].T

    def mine(block, i):
        return jnp.where(half_of(steps[i][0], (256, 128)), block, jnp.zeros_like(block))

    def score(i):
        parity, r = steps[i]
        qa = q_in[parity, r * 256 : r * 256 + 256]
        ga = mine(g_all[r * 256 : r * 256 + 256, lanes], i)

        def part(c):
            scores[i % 2][c : c + BIG] = nt(k_in[parity, c : c + BIG], qa)

        def grad(c):
            grads[i % 2][c : c + BIG] = nt(v_all[c : c + BIG, lanes], ga)

        return [task for c in range(0, ROWS, BIG) for task in (partial(part, c), partial(grad, c))]

    def soften(i):
        parity, r = steps[i]
        s, g, out, diff = scores[i % 2], grads[i % 2], probs[i % 2], diffs[i % 2]
        logs = lse[pl.ds(2 * p + parity, 1), r * 256 : r * 256 + 256]
        state = {}

        def power(c):
            e = jnp.exp(s[c : c + CHUNK] - logs)
            s[c : c + CHUNK] = e
            out[c : c + CHUNK] = e.astype(BF)
            part = jnp.sum((e * g[c : c + CHUNK]).reshape(-1, 8, 256), axis=0)
            state["inner"] = state["inner"] + part if c else part
            if c == ROWS - CHUNK:
                state["inner"] = jnp.sum(state["inner"], axis=0, keepdims=True)

        def minus(c):
            diff[c : c + CHUNK] = (s[c : c + CHUNK] * (g[c : c + CHUNK] - state["inner"])).astype(BF)

        at = range(0, ROWS, CHUNK)
        return [(5.5, partial(power, c)) for c in at] + [(2.5, partial(minus, c)) for c in at]

    def collect(i):
        parity, r = steps[i]
        rows = slice(64 * parity, 64 * parity + 64)
        at = slice(r * 256, r * 256 + 256)
        qz, gz = mine(q_in[parity, at], i), mine(g_all[at, lanes], i)
        total = []

        def part(c):
            total.append(nn(k_t[parity, rows, c : c + 256], diffs[i % 2][c : c + 256]))
            if c == ROWS - 256:
                dq_t[rows, r * 256 : r * 256 + 256] = ((total[0] + total[1]) + (total[2] + total[3])) * 0.125

        def add(acc, first, ref, z, c):
            val = nn(ref[c : c + BIG], z)
            base = acc if i else first
            acc[c : c + BIG] = val if base is None else base[c : c + BIG] + val

        tasks = []
        for c in range(0, ROWS, 256):
            if c % BIG == 0:
                tasks += [partial(add, dv_acc, firsts[1], probs[i % 2], gz, c), partial(add, dk_acc, firsts[0], diffs[i % 2], qz, c)]
            tasks += [partial(part, c)]
        return tasks

    for task in score(0):
        task()
    last = len(steps) - 1
    for i in range(last + 2):
        later = (score(i + 1) if i < last else []) + (collect(i - 1) if i else [])
        mix(soften(i) if i <= last else [], later)


def back_first_body(q_all, k_all, v_all, g_all, lse, dq_t, dk_acc, dv_acc, *buffers):
    pair_back(0, (0,), q_all, k_all, v_all, g_all, lse, dq_t, dk_acc, dv_acc, (None, None), buffers)


def back_body(place, q_all, k_all, v_all, g_all, lse, x_t, dq_first, dk_first, dv_first, *refs):
    (dq_out, dk_out, dv_out, keep, send), refs = refs[:5], refs[5:]
    dq_t, dk_acc, dv_acc, sums, *buffers = refs
    odd = place[1] == 1

    def finish(p):
        out = pl.ds(pl.multiple_of(p * 128, 128), 128)
        dq = dq_t[...].astype(BF).T
        dk = dk_acc[...].astype(BF)
        dv = dv_acc[...].astype(BF)
        dq_out[:, out] = dq
        dk_out[:, out] = dk
        dv_out[:, out] = dv
        val = nn(x_t[...], jnp.concatenate([dq, dk, dv, dv], axis=1))
        sums[pl.ds(p, 1), :] = val[D : D + 1, 0:128]
        sums[pl.ds(4 + p, 1), :] = val[D : D + 1, 256:384]
        for index in range(3):
            for o in range(0, 8, 2):
                for i in range(4):
                    col, top = slice(128 * index, 128 * index + 128), 64 * o + 16 * i
                    even, other = val[top : top + 16, col], val[top + 64 : top + 80, col]
                    at = pl.ds(pl.multiple_of(SHARE * p + 64 * (4 * index + o // 2) + 16 * i, 16), 16)
                    keep[at] = jnp.where(odd, other, even)
                    send[at] = jnp.where(odd, even, other)

    def pair(p, _):
        pair_back(p, (0, 1), q_all, k_all, v_all, g_all, lse, dq_t, dk_acc, dv_acc, (None, None), buffers)
        finish(p)
        return 0

    dq_t[:64] = dq_first[...]
    pair_back(0, (1,), q_all, k_all, v_all, g_all, lse, dq_t, dk_acc, dv_acc, (dk_first, dv_first), buffers)
    finish(0)
    lax.fori_loop(1, 4, pair, 0)
    row = lax.broadcasted_iota(jnp.int32, (8, 128), 0)
    even, other = jnp.zeros((8, 128), F32), jnp.zeros((8, 128), F32)
    for o in range(0, 8, 2):
        even = jnp.where(row == o // 2, sums[o : o + 1, :], even)
        other = jnp.where(row == o // 2, sums[o + 1 : o + 2, :], other)
    keep[4 * SHARE :] = jnp.where(odd, other, even)
    send[4 * SHARE :] = jnp.where(odd, even, other)


def split_row(tile):
    row = lax.broadcasted_iota(jnp.int32, tile.shape, 0)
    rest = tile[0:1] - tile[0:1].astype(BF).astype(F32)
    return jnp.where(row == 4, rest, tile)


def join_row(tile):
    row = lax.broadcasted_iota(jnp.int32, tile.shape, 0)
    whole = tile[0:1] + tile[4:5]
    return jnp.where(row == 0, whole, jnp.where(row == 4, 0.0, tile))


def feed_xy_body(place, keep, got, wo_keep, wo_got, *outs):
    size = keep.shape[1]
    for t in range(4):
        here = place[3] ^ t
        out = outs[t]
        for z in range(4):
            at = 4 * z + here
            out[size * z : size * z + size - 1] = (keep[at, : size - 1] + got[at, : size - 1].astype(F32)).astype(out.dtype)
            total = keep[at, size - 1] + join_row(got[at, size - 1].astype(F32))
            out[size * z + size - 1] = (split_row(total) if t else total).astype(out.dtype)
        out[4 * size :] = (wo_keep[here] + wo_got[here]).astype(out.dtype)


def feed_z_body(place, keep, g1, g2, g3, out0, out1, out2, out3, wo_out):
    size = out0.shape[0]
    for t, out in enumerate((out0, out1, out2, out3)):
        at = pl.ds((place[4] ^ t) * size, size - 1)
        total = keep[at] + g1[at].astype(F32) + g2[at].astype(F32) + g3[at].astype(F32)
        out[: size - 1] = total.astype(out.dtype)
        at = (place[4] ^ t) * size + size - 1
        total = keep[at]
        for g in (g1, g2, g3):
            total = total + join_row(g[at].astype(F32))
        out[size - 1] = (split_row(total) if t else total).astype(out.dtype)
    at = slice(4 * size, 4 * size + 16)
    wo_out[...] = keep[at] + g1[at].astype(F32) + g2[at].astype(F32) + g3[at].astype(F32)


def square_xy_body(place, keep, got, *outs):
    for t in range(4):
        here = place[3] ^ t
        out = outs[t]
        for z in range(3):
            for p in range(4):
                rows = pl.ds(pl.multiple_of(SHARE * p + 64 * (4 * z + here), 64), 64)
                total = keep[rows] + got[rows]
                out[16 * z + 4 * p : 16 * z + 4 * p + 4] = total.reshape(4, 16, 128).astype(out.dtype)
        row = lax.broadcasted_iota(jnp.int32, (16, 128), 0)
        total = keep[pl.ds(4 * SHARE + here, 1)] + got[pl.ds(4 * SHARE + here, 1)]
        total = jnp.where(row == 0, total, 0.0)
        out[48] = (split_row(total) if t else total).astype(out.dtype)


def square_z_body(place, keep, g1, g2, g3, wo, out0, out1, out2, out3, whole):
    for z in range(3):
        at = slice(16 * z, 16 * z + 16)
        whole[z, :16] = keep[at] + g1[at].astype(F32) + g2[at].astype(F32) + g3[at].astype(F32)
        whole[z + 1, 16] = jnp.zeros((16, 128), F32)
    whole[3, :16] = wo[...]
    total = keep[48]
    for g in (g1, g2, g3):
        total = total + join_row(g[48].astype(F32))
    whole[0, 16] = total
    for t, out in enumerate((out0, out1, out2, out3)):
        at = place[4] ^ t
        out[:16] = whole[at, :16].astype(out.dtype)
        out[16] = (split_row(whole[at, 16]) if t else whole[at, 16]).astype(out.dtype)


def input_body(gm, dq, dk, dv, w, out):
    for r in range(4):
        at = slice(256 * r, 256 * r + 256)
        total = gm[at, :]
        for index in range(3):
            total = total + nt((dq, dk, dv)[index][at, :], square(w, index))
        out[at, :] = total


def to_columns(flat, rows):
    return flat.reshape(rows // 16, 16, -1, 128).transpose(2, 0, 1, 3).reshape(-1, 16, 128)


def from_columns(tiles, rows):
    return tiles.reshape(-1, rows // 16, 16, 128).transpose(1, 2, 0, 3).reshape(-1)


def swap(x, n, bit):
    return lax.ppermute(x, AXES, [(i, i ^ bit) for i in range(n)])


def small(body, outs, args, scratch=()):
    ins = [SMEM if arg.dtype == jnp.int32 else VMEM for arg in args]
    size = sum(arg.size for arg in args)
    return call(body, outs, ins, scratch, 2 * size, 6 * size, 16)(*args)


def blocks_of(*shape):
    return [(shape + (16, 128), F32)] + [(shape + (16, 128), BF)] * 3


def hop(parts, n, step):
    return [parts[0]] + [swap(part, n, step * t) for t, part in enumerate(parts) if t]


def tie(values, after):
    return lax.optimization_barrier((values, after))[0]


def along_z(own, n):
    return jnp.stack([own] + [swap(own, n, 8 * z) for z in (1, 2, 3)])


def along_xy(stack, n):
    return [stack] + [swap(stack, n, 2 * xy) for xy in (1, 2, 3)]


def across(chips, n):
    return chips + [swap(part, n, 1) for part in chips]


def pack_square_body(flat, biases, out, wide):
    wide[...] = flat[...].astype(F32)
    for j in range(4):
        for i in range(4):
            out[4 * j + i] = wide[pl.ds(64 * i + j, 16, stride=4), :].astype(BF)
    row = lax.broadcasted_iota(jnp.int32, (16, 128), 0)
    out[16] = jnp.where(row == 0, biases[...].astype(F32), 0.0).astype(BF)


def pack_feed_body(place, flat, out, wide):
    wide[...] = flat[...].astype(F32)

    @pl.when(place[0] < PARTS // 2)
    def _():
        for j in range(16):
            for i in range(2):
                out[2 * j + i] = wide[pl.ds(256 * i + j, 16, stride=16), :].astype(BF)

    @pl.when(place[0] >= PARTS // 2)
    def _():
        for j in range(4):
            for i in range(8):
                out[8 * j + i] = wide[pl.ds(64 * i + j, 16, stride=4), :].astype(BF)


def copy_body(ref, out):
    for i in range(5):
        out[i] = ref[i]


def added(keep, gots, at):
    total = keep[at]
    for g in gots:
        total = total + g[at].astype(F32)
    return total


def added_tail(keep, gots, at):
    total = keep[at]
    for g in gots:
        total = total + join_row(g[at].astype(F32))
    return total


def finish_feed_body(place, keep, f1, f2, f3, ff, tail):
    gots = (f1, f2, f3)

    @pl.when(place[0] < PARTS // 2)
    def _():
        for j in range(16):
            for i in range(2):
                ff[pl.ds(256 * i + j, 16, stride=16), :] = added(keep, gots, 2 * j + i)

    @pl.when(place[0] >= PARTS // 2)
    def _():
        for j in range(4):
            for i in range(8):
                ff[pl.ds(64 * i + j, 16, stride=4), :] = added(keep, gots, 8 * j + i)

    tail[...] = added_tail(keep, gots, F_TILES)


def finish_square_body(place, keep, a1, a2, a3, tail, att, bias, gate):
    gots = (a1, a2, a3)
    for j in range(4):
        for i in range(4):
            att[pl.ds(64 * i + j, 16, stride=4), :] = added(keep, gots, 4 * j + i)
    bias[...] = jnp.where(place[0] < 8, added_tail(keep, gots, 16)[0:1], tail[0:1])
    gates = tail[1:2] + tail[2:3] + tail[3:4]
    lane = lax.broadcasted_iota(jnp.int32, (1, 128), 1)
    for g in range(2):
        gate[g] = jnp.sum(jnp.where((lane < 2 * PARTS) & (lane % 2 == g), gates, 0.0))


def own_pieces(attention, feedforward, biases, upper, parts):
    tail = jnp.pad(biases.reshape(1, 1, 128), ((0, 0), (0, 15), (0, 0)))
    own_a = jnp.concatenate([to_columns(attention, 4 * D // parts), tail], axis=0)
    up = to_columns(feedforward, 2 * D // parts)
    down = to_columns(feedforward, 2 * FF // parts)
    return own_a, jnp.where(upper, up, down)


def pieces_any(attention, feedforward, biases):
    full = [lax.all_gather(x, AXES, axis=0, tiled=True).reshape(PARTS, -1) for x in (attention, feedforward, biases)]
    upper = jnp.arange(PARTS) < PARTS // 2
    a, f = jax.vmap(lambda *x: own_pieces(*x, PARTS))(*full, upper)
    a, f = a.reshape((4, 4, 2) + a.shape[1:]), f.reshape((4, 4, 2) + f.shape[1:])

    return [[x[:, xy, c] for c in range(2) for xy in range(4)] for x in (a, f)]


def local(direct, tokens, cotangent, attention, feedforward, biases, gates, counts, lengths):
    me = lax.axis_index(AXES)
    n = PARTS
    row = (ROWS, D)

    def prepare(counts):
        *masks, x_t = call(
            prepare_body,
            [((2, ROWS, 128), BF), ((2, ROWS, 128), BF), ((D + 16, ROWS), BF)],
            [SMEM, SMEM, VMEM], [], 1000, 1000, 16,
        )(counts, lengths, tokens)
        return masks, x_t

    if direct:
        place = jnp.stack([me, me % 2, me, (me // 2) % 4, me // 8]).astype(jnp.int32)
        (own_a,) = small(
            pack_square_body, [((A_TILES, 16, 128), BF)], (attention.reshape(-1, 128), biases.reshape(1, 128)), [((256, 128), F32)]
        )
        (own_f,) = small(
            pack_feed_body, [((F_TILES, 16, 128), BF)], (place, feedforward.reshape(-1, 128)), [((512, 128), F32)]
        )
        stack_a = along_z(own_a, n)
        far = [swap(own_f, n, 16), swap(own_f, n, 24)]
        chips_a = along_xy(stack_a, n)
        near = swap(own_f, n, 8)
        far, near, place, counts = lax.optimization_barrier((far, near, place, counts))
        masks, x_t = prepare(counts)
        (place,) = call(copy_body, [((5,), jnp.int32, SMEM)], [SMEM], [], 8 << 30, 1000, 16)(place)
        stack_f = jnp.stack([own_f, near] + far)
        chips_a, stack_f, place, masks = lax.optimization_barrier((chips_a, stack_f, place, masks))
        ga_all = across(chips_a, n)
        chips_f = along_xy(stack_f, n)
    else:
        masks, x_t = prepare(counts)
        ga_all, gf_all = pieces_any(attention, feedforward, biases)
        place = jnp.zeros((5,), jnp.int32)
    row = (ROWS, D)
    q, k, v, w, bias = call(
        project_body,
        [((H, ROWS, 128), BF)] * 2 + [(row, BF), ((PARTS, A_TILES, 16, 128), BF), ((1, 8 * D), F32)],
        [SMEM] + [VMEM] * 11, [], 1000, 1000, 20,
    )(place, tokens, *masks, *ga_all)
    ctx, ctx_t, lse = call(
        attend_body,
        [(row, BF), ((D + 16, ROWS), BF), ((8, ROWS), F32)],
        [VMEM] * 3,
        [((128, ROWS), BF), ((128, ROWS), F32)] + [((ROWS, 256), F32)] * 2 + [((ROWS, 256), BF)] * 2,
        1000, 1000, 20,
    )(q, k, v)
    branch, low, low_t, gs = call(
        branch_body,
        [(row, F32), (row, BF), ((D + 16, ROWS), BF), (row, BF)],
        [SMEM] + [VMEM] * 5, [], 1000, 1000, 20,
    )(gates, tokens, cotangent, ctx, w, bias)
    if direct:
        own, y, x, xy = chips_f
        xy, branch = lax.optimization_barrier((xy, branch))
        own_other, xy_other = swap(tie(own, ctx), n, 1), swap(xy, n, 1)
        y, x, own_other, xy_other = lax.optimization_barrier((y, x, own_other, xy_other))
        gf_all = [own, y, x, xy, own_other, swap(y, n, 1), swap(x, n, 1), xy_other]
    layer, gm, gctx, ff_keep, ff_send, wo_keep, wo_send = call(
        feed_body,
        [(row, BF, ANY), (row, F32), (row, BF)]
        + [((n // 2, G_TILES, 16, 128), F32, ANY), ((n // 2, G_TILES, 16, 128), BF, ANY)]
        + [((4, 16, 16, 128), F32)] * 2,
        [SMEM, SMEM] + [VMEM] * 17,
        [((PARTS, F_TILES, 16, 128), BF), (row, BF),
         ((FF + 16, ROWS), BF), ((ROWS, FF), BF)]
        + [((256, D), F32)] * 4 + [((256, FF), BF)] + [((256, D), F32)] * 2 + [((1, 8 * D), F32)]
        + [(row, BF), ((n // 2, G_TILES, 16, 128), F32), ((n // 2, G_TILES, 16, 128), BF), DMA((16,))],
        16 << 30, 30 << 20, 32,
    )(place, gates, tokens, cotangent, branch, low, low_t, gs, ctx_t, w, bias, *gf_all)

    half, whole = (ROWS // 16, ROWS), (128, ROWS)
    buffers = [((2, 128, ROWS), BF)] + [((ROWS, 256), F32)] * 4 + [((ROWS, 256), BF)] * 4
    sums = [((ROWS, 128), F32)] * 2
    barrier = lax.optimization_barrier
    if direct:
        got, wo_got = swap(ff_send, n, 1), swap(wo_send, n, 1)
    begun = call(
        back_first_body, [(half, F32)] + sums, [VMEM] * 5, buffers, 1000, 1000, 28
    )(q, k, v, gctx, lse)
    if direct:
        got, wo_got, begun = barrier((got, wo_got, begun))
        parts = small(feed_xy_body, blocks_of(4 * G_TILES + 16), (place, ff_keep, got, wo_keep, wo_got))
        q, parts = barrier((q, parts))
        ff_got = hop(parts, n, 2)
    *grads, keep, send = call(
        back_body,
        [(row, BF)] * 3 + [((4 * SHARE + 8, 128), F32)] * 2,
        [SMEM] + [VMEM] * 9,
        [(whole, F32)] + sums + [((8, 128), F32)] + buffers,
        1000, 1000, 28,
    )(place, q, k, v, gctx, lse, x_t, *begun)
    if direct:
        got = swap(send, n, 1)
    (input_grad,) = call(
        input_body, [(row, F32)], [VMEM] * 5, [], 32 << 30, 1000, 24
    )(gm, *grads, w)
    if direct:
        got, input_grad, ff_got = barrier((got, input_grad, ff_got))
        parts = small(square_xy_body, blocks_of(49), (place, keep, got))
        ff_got, parts = barrier((ff_got, parts))
        got = hop(parts, n, 2)
        *ff_parts, wo = small(feed_z_body, blocks_of(G_TILES) + [((16, 16, 128), F32)], (place, *ff_got))
        ff_got = hop(ff_parts, n, 8)
        got, ff_parts = barrier((got, ff_parts))
    if direct:
        parts = small(square_z_body, blocks_of(17), (place, *got, wo), [((4, 17, 16, 128), F32)])
        got = hop(parts, n, 8)
        ff_grad, tail = call(
            finish_feed_body, [((512, 128), F32), ((16, 128), F32)], [SMEM] + [VMEM] * 4, [], 1000, 1000, 16,
        )(place, *ff_got)
        got, tail = barrier((got, tail))
        att_grad, bias_grad, gate_grad = call(
            finish_square_body,
            [((256, 128), F32), ((1, 128), F32), ((2,), F32, SMEM)],
            [SMEM] + [VMEM] * 5, [], 1000, 1000, 16,
        )(place, *got, tail)
        att_grad, ff_grad, bias_grad = att_grad.reshape(-1), ff_grad.reshape(-1), bias_grad.reshape(-1)
        return layer, input_grad, att_grad, ff_grad, bias_grad, gate_grad

    def owners(keep, send):
        return jnp.stack([keep, send], axis=1).reshape((-1,) + keep.shape[1:])

    def reduce(flat):
        return lax.psum_scatter(flat.reshape(-1), AXES, scatter_dimension=0, tiled=True)

    mail = ff_send.astype(F32)
    mail = mail.at[:, F_TILES, 0].add(mail[:, F_TILES, 4])
    both = owners(ff_keep, mail)
    up = jax.vmap(lambda t: from_columns(t, 2 * D // n))(both[: n // 2, :F_TILES]).reshape(-1)
    down = jax.vmap(lambda t: from_columns(t, 2 * FF // n))(both[n // 2 :, :F_TILES]).reshape(-1)
    ff_grad = reduce(jnp.concatenate([up, down]))
    tail = both[0, F_TILES]
    gate_grad = lax.psum((tail[1] + tail[2] + tail[3])[:2], AXES)
    bias_grad = owners(keep[4 * SHARE : 4 * SHARE + 4], send[4 * SHARE : 4 * SHARE + 4])
    bias_grad = jnp.concatenate([bias_grad, both[8:, F_TILES, 0]])
    both = jnp.stack([x[: 4 * SHARE].reshape(4, 12, 4, 16, 128) for x in (keep, send)], axis=2)
    both = both.reshape(4, 24, 4, 16, 128).transpose(1, 0, 2, 3, 4)
    both = jnp.concatenate([both.reshape(24, 16, 16, 128), owners(wo_keep, wo_send)])
    att_grad = jax.vmap(lambda t: from_columns(t, 4 * D // n))(both)
    return layer, input_grad, reduce(att_grad), ff_grad, reduce(bias_grad), gate_grad


def solution(mesh):
    direct = dict(mesh.shape) == {"dp": 8, "fsdp": 4}
    both = P(AXES)
    rows = P(AXES, None)
    return jax.shard_map(
        partial(local, direct),
        mesh=mesh,
        in_specs=(rows, rows, both, both, both, P(), rows, rows),
        out_specs=(rows, rows, both, both, both, P()),
        check_vma=False,
    )
```
